32 devices in a mesh: dp: 8 (over y, x, core), fsdp: 4 (over z).
Axes of the slice: x: 2, y: 2, z: 4, core: 2. Of those that a mesh axis runs over, the one named last changes fastest.
Arguments:
- tokens: bfloat16 [135168, 384], P(('dp', 'fsdp')), may hold values from -6 to 6
- centers: float32 [3, 135168], P(None, ('dp', 'fsdp')), may hold values from -1 to 1
- mask_count: int32 [2048], P(('dp', 'fsdp')), may hold values from 16 to 28, as said below
- mask_index: int32 [2048, 28], P(('dp', 'fsdp')), may hold values from 0 to 63, as said below
- mask_embed: float32 [384], replicated, may hold values from -6 to 6
- place_weight: float32 [3, 128], replicated, may hold values from -3.5 to 3.5
- place_bias: float32 [128], replicated, may hold values from -3 to 3
- place_proj: bfloat16 [128, 384], P('fsdp'), may hold values from -0.5 to 0.5
- place_shift: float32 [384], replicated, may hold values from -2 to 2
- norm_gain: float32 [384], replicated, may hold values from 0.5 to 1.5
- norm_shift: float32 [384], replicated, may hold values from -2 to 2
- joint_weight: bfloat16 [384, 1152], P('fsdp'), may hold values from -0.3125 to 0.3125
- out_weight: bfloat16 [384, 384], P('fsdp'), may hold values from -0.875 to 0.875
- out_bias: float32 [384], replicated, may hold values from -2 to 2
- mlp_gain: float32 [384], replicated, may hold values from 0.5 to 1.5
- mlp_shift: float32 [384], replicated, may hold values from -2 to 2
- up_weight: bfloat16 [384, 1536], P('fsdp'), may hold values from -0.3125 to 0.3125
- up_bias: float32 [1536], replicated, may hold values from -3 to 3
- down_weight: bfloat16 [1536, 384], P('fsdp'), may hold values from -0.15625 to 0.15625
- down_bias: float32 [384], replicated, may hold values from -2 to 2
- cotangent: bfloat16 [135168, 384], P(('dp', 'fsdp')), may hold values from -6 to 6
Outputs:
- output: bfloat16 [135168, 384], P(('dp', 'fsdp'))
- tokens_grad: bfloat16 [135168, 384], P(('dp', 'fsdp'))
- embed_grad: float32 [384], replicated
- place_weight_grad: float32 [3, 128], replicated
- place_bias_grad: float32 [128], replicated
- place_proj_grad: float32 [128, 384], replicated
- place_shift_grad: float32 [384], replicated
- norm_gain_grad: float32 [384], replicated
- norm_shift_grad: float32 [384], replicated
- joint_weight_grad: float32 [384, 1152], replicated
- out_weight_grad: float32 [384, 384], replicated
- out_bias_grad: float32 [384], replicated
- mlp_gain_grad: float32 [384], replicated
- mlp_shift_grad: float32 [384], replicated
- up_weight_grad: float32 [384, 1536], replicated
- up_bias_grad: float32 [1536], replicated
- down_weight_grad: float32 [1536, 384], replicated
- down_bias_grad: float32 [384], replicated
The draws below stay inside these ranges and needn't reach their ends.
Inputs may be any that keep to these rules, and one draw needn't show every extreme that they name: `mask_count`: number of masked patches of each cloud; some cloud has exactly 28 and some exactly 16. `mask_index`: each row holds 28 different patch numbers.
All inputs are finite; a program needn't handle non-finite values.
Results may differ from the reference program's by a relative error of at most 0.017.
Values may be sent and summed in bfloat16 or wider, within the bound.
No kernel may reach another device: no remote copies, remote signals or barrier semaphores. Data moves between devices by JAX's collectives and lax.ppermute only.
A program may use at most 256 MiB of HBM per device.

```python
import jax
import jax.numpy as jnp
from jax import lax

D = 384
HEADS = 6
FF = 1536
POSH = 128
PATCHES = 64
SEQ = 66
TILE = 8
MASK_LEAST = 16
MASK_MOST = 28
CLOUDS = 2048
ROWS = 135168


def draw_mask_count(key, part):
    key = jax.random.fold_in(key, 11)
    first_key, second_key, third_key = jax.random.split(key, 3)
    counts = jax.random.randint(first_key, (CLOUDS,), MASK_LEAST, MASK_MOST + 1, dtype=jnp.int32)
    most_at = jax.random.randint(second_key, (), 0, CLOUDS, dtype=jnp.int32)
    least_at = (most_at + 1 + jax.random.randint(third_key, (), 0, CLOUDS - 1, dtype=jnp.int32)) % CLOUDS
    counts = counts.at[most_at].set(MASK_MOST)
    return counts.at[least_at].set(MASK_LEAST)


def draw_mask_index(key, part):
    key = jax.random.fold_in(key, 12)
    cloud_keys = jax.random.split(key, CLOUDS)
    orders = jax.vmap(lambda cloud_key: jax.random.permutation(cloud_key, PATCHES))(cloud_keys)
    return orders[:, :MASK_MOST].astype(jnp.int32)


def steps_of(stream_key, shape, shards, least, high):
    factor_of, own = 1.0, jax.random.fold_in(stream_key, 6)
    for dim, shards_of in shards:
        steps = jnp.exp(jax.random.uniform(jax.random.fold_in(own, dim), (shards_of,), jnp.float32, least / len(shards), high / len(shards)))
        factor_of = factor_of * jnp.repeat(steps, shape[dim] // shards_of).reshape([-1 if axis == dim else 1 for axis in range(len(shape))])
    return factor_of


def noise(own_key, dims, scale, most, shards=(), kind=jnp.bfloat16):
    array = jax.random.normal(own_key, dims, jnp.float32) * scale
    if len(shards) > 0:
        array = steps_of(own_key, dims, shards, -0.22, 0.18) * array
    return jnp.clip(array, min=-most, max=most).astype(kind)


def setup_inputs(seed: int = 0) -> dict:
    arg_keys = jax.random.split(jax.random.key(seed), 22)
    tokens = noise(arg_keys[0], (ROWS, D), 1.0, 6.0, ((0, 32),))
    centers = jnp.clip(jax.random.uniform(arg_keys[1], (3, ROWS), jnp.float32, -1.0, 1.0) * steps_of(arg_keys[1], (3, ROWS), ((1, 32),), -0.4, 0.0), -1.0, 1.0)
    mask_count = draw_mask_count(jax.random.fold_in(arg_keys[21], 71), 0)
    mask_index = draw_mask_index(jax.random.fold_in(arg_keys[21], 71), 0)
    mask_embed = noise(arg_keys[4], (D,), 1.0, 6.0, (), jnp.float32)
    place_weight = noise(arg_keys[5], (3, POSH), 3 ** -0.5, 3.5, (), jnp.float32)
    place_bias = noise(arg_keys[6], (POSH,), 0.5, 3.0, (), jnp.float32)
    place_proj = noise(arg_keys[7], (POSH, D), POSH ** -0.5, 0.5, ((0, 4),))
    place_shift = noise(arg_keys[8], (D,), 0.3, 2.0, (), jnp.float32)
    norm_gain = jnp.clip(1.0 + 0.1 * jax.random.normal(arg_keys[9], (D,), jnp.float32), 0.5, 1.5)
    norm_shift = noise(arg_keys[10], (D,), 0.3, 2.0, (), jnp.float32)
    joint_weight = noise(arg_keys[11], (D, 3 * D), D ** -0.5, 0.3125, ((0, 4),))
    out_weight = noise(arg_keys[12], (D, D), (D // 8) ** -0.5, 0.875, ((0, 4),))
    out_bias = noise(arg_keys[13], (D,), 0.3, 2.0, (), jnp.float32)
    mlp_gain = jnp.clip(1.0 + 0.1 * jax.random.normal(arg_keys[14], (D,), jnp.float32), 0.5, 1.5)
    mlp_shift = noise(arg_keys[15], (D,), 0.3, 2.0, (), jnp.float32)
    up_weight = noise(arg_keys[16], (D, FF), D ** -0.5, 0.3125, ((0, 4),))
    up_bias = noise(arg_keys[17], (FF,), 0.5, 3.0, (), jnp.float32)
    down_weight = noise(arg_keys[18], (FF, D), FF ** -0.5, 0.15625, ((0, 4),))
    down_bias = noise(arg_keys[19], (D,), 0.3, 2.0, (), jnp.float32)
    cotangent = noise(arg_keys[20], (ROWS, D), 1.0, 6.0, ((0, 32),))
    return {"tokens": tokens, "centers": centers, "mask_count": mask_count, "mask_index": mask_index, "mask_embed": mask_embed, "place_weight": place_weight, "place_bias": place_bias, "place_proj": place_proj, "place_shift": place_shift, "norm_gain": norm_gain, "norm_shift": norm_shift, "joint_weight": joint_weight, "out_weight": out_weight, "out_bias": out_bias, "mlp_gain": mlp_gain, "mlp_shift": mlp_shift, "up_weight": up_weight, "up_bias": up_bias, "down_weight": down_weight, "down_bias": down_bias, "cotangent": cotangent}


@jax.custom_vjp
def low(v):
    return lax.optimization_barrier(v.astype(jnp.bfloat16)).astype(jnp.float32)

@jax.custom_vjp
def low_back(v):
    return v

def low_keep(v):
    return (low(v), None)

def low_pass(kept, grad):
    return (grad,)

def back_keep(v):
    return (v, None)

def back_low(kept, grad):
    return (low(grad),)
low.defvjp(low_keep, low_pass)
low_back.defvjp(back_keep, back_low)

def highest(left, right):
    return jnp.dot(left, right, precision=lax.Precision.HIGHEST)

def layer_norm(values, gain_row, shift_row):
    centred = values - lax.optimization_barrier(jnp.mean(values, axis=-1, keepdims=True))
    spread = lax.optimization_barrier(jnp.mean(centred * centred, axis=-1, keepdims=True))
    return centred * lax.rsqrt(spread + 1e-05) * gain_row + shift_row

def masked_rows(mask_count, mask_index):
    patch_ids = jnp.arange(PATCHES, dtype=jnp.int32)
    slot_ids = jnp.arange(MASK_MOST, dtype=jnp.int32)
    chosen = (mask_index[:, :, None] == patch_ids[None, None, :]) & (slot_ids[None, :, None] < mask_count[:, None, None])
    hit_patch = jnp.any(chosen, axis=1)
    border = jnp.zeros((hit_patch.shape[0], 1), dtype=bool)
    return jnp.concatenate([border, hit_patch, border], axis=1).reshape(-1)

def block_mask(tile_rows):
    row_ids = jnp.arange(tile_rows, dtype=jnp.int32)
    same_cloud = row_ids[:, None] // SEQ == row_ids[None, :] // SEQ
    live_key = row_ids % SEQ != SEQ - 1
    return same_cloud & live_key[None, :]

def group_forward(params, token_rows, center_rows, hidden_rows):
    mask_embed, place_weight, place_bias, place_proj, place_shift, norm_gain, norm_shift, joint_weight, out_weight, out_bias, mlp_gain, mlp_shift, up_weight, up_bias, down_weight, down_bias = params
    tile_rows = token_rows.shape[0]
    head_size = D // HEADS
    place_hidden = jax.nn.gelu(highest(center_rows, place_weight) + place_bias, approximate=False)
    placed = low_back(highest(low(place_hidden), place_proj)) + place_shift
    entry_rows = jnp.where(hidden_rows[:, None], mask_embed[None, :], token_rows) + placed
    normed = low(layer_norm(entry_rows, norm_gain, norm_shift))
    joint_rows = low(low_back(highest(normed, joint_weight))).reshape(tile_rows, 3, HEADS, head_size)
    scores = low_back(jnp.einsum('qhd,khd->hqk', joint_rows[:, 0], joint_rows[:, 1], precision=lax.Precision.HIGHEST) * head_size ** (-0.5))
    scores = jnp.where(block_mask(tile_rows)[None], scores, -1e+30)
    row_top = lax.optimization_barrier(jnp.max(scores, axis=-1, keepdims=True))
    weights = jnp.exp(scores - row_top)
    attention = weights / lax.optimization_barrier(jnp.sum(weights, axis=-1, keepdims=True))
    mixture = low(low_back(jnp.einsum('hqk,khd->qhd', low(attention), joint_rows[:, 2], precision=lax.Precision.HIGHEST))).reshape(tile_rows, D)
    middle = entry_rows + (low_back(highest(mixture, out_weight)) + out_bias)
    normed_two = low(layer_norm(middle, mlp_gain, mlp_shift))
    raised = low_back(highest(normed_two, up_weight)) + up_bias
    gated_rows = low(jax.nn.gelu(raised, approximate=False))
    return middle + (low_back(highest(gated_rows, down_weight)) + down_bias)

def reference(tokens, centers, mask_count, mask_index, mask_embed, place_weight, place_bias, place_proj, place_shift, norm_gain, norm_shift, joint_weight, out_weight, out_bias, mlp_gain, mlp_shift, up_weight, up_bias, down_weight, down_bias, cotangent):
    hidden_rows = masked_rows(mask_count, mask_index)
    group_rows = TILE * SEQ
    groups = tokens.shape[0] // group_rows
    token_groups = tokens.astype(jnp.float32).reshape(groups, group_rows, D)
    center_groups = centers.T.reshape(groups, group_rows, 3)
    hidden_groups = hidden_rows.reshape(groups, group_rows)
    params = (mask_embed, place_weight, place_bias, place_proj.astype(jnp.float32), place_shift, norm_gain, norm_shift, joint_weight.astype(jnp.float32), out_weight.astype(jnp.float32), out_bias, mlp_gain, mlp_shift, up_weight.astype(jnp.float32), up_bias, down_weight.astype(jnp.float32), down_bias)

    def whole(params, token_groups):

        def scan_step(carried, inputs):
            return (carried, jax.checkpoint(group_forward)(params, inputs[0], inputs[1], inputs[2]))
        return lax.scan(scan_step, jnp.zeros((), jnp.float32), (token_groups, center_groups, hidden_groups))[1]
    result, pullback = jax.vjp(whole, params, token_groups)
    gradients, token_grad = pullback(cotangent.astype(jnp.float32).reshape(groups, group_rows, D))
    output = result.reshape(-1, D).astype(jnp.bfloat16)
    tokens_grad = token_grad.reshape(-1, D).astype(jnp.bfloat16)
    return (output, tokens_grad, gradients[0], gradients[1], gradients[2], gradients[3], gradients[4], gradients[5], gradients[6], gradients[7], gradients[8], gradients[9], gradients[10], gradients[11], gradients[12], gradients[13], gradients[14], gradients[15])
```

```python
import functools

import jax
import jax.numpy as jnp
from jax import lax
from jax.experimental import pallas as pl
from jax.experimental.pallas import tpu as pltpu
from jax.sharding import PartitionSpec as P

D = 384
HEADS = 6
FF = 1536
POSH = 128
SEQ = 66
TILE = 8
ROWS = TILE * SEQ
STEP = 64
WIN = 80
KEYS = 128
PAIRS = HEADS // 2
GROUP = 12
VMEM = 60 * 2**20
LOG2E = 1.4426950408889634
ROOT_HALF = 0.7071067811865476
PDF = 0.3989422804014327
bf16 = jnp.bfloat16
f32 = jnp.float32

NN = (((1,), (0,)), ((), ()))
NT = (((1,), (1,)), ((), ()))
TN = (((0,), (0,)), ((), ()))


def dot(left, right, dims=NN):
    return lax.dot_general(left, right, dims, preferred_element_type=f32)


def cdf(u):
    return 0.5 + 0.5 * lax.erf(u * ROOT_HALF)


def smooth_slope(u, mass):
    return mass + u * (PDF * jnp.exp2(u * u * (-0.5 * LOG2E)))


def row_mean(values):
    return jnp.sum(values, axis=-1, keepdims=True) * (1.0 / values.shape[-1])


def normalised(values):
    centred = values - row_mean(values)
    scale = lax.rsqrt(row_mean(centred * centred) + 1e-05)
    return centred * scale, scale


def hidden_column(targets, rows):
    row_ids = lax.broadcasted_iota(jnp.int32, (rows, targets.shape[1]), 0)
    hits = jnp.where(row_ids == targets, 1.0, 0.0)
    return jnp.max(hits, axis=1, keepdims=True)


def lane_mask(rows, odd, kind=bf16):
    lanes = lax.broadcasted_iota(jnp.int32, (rows, 128), 1)
    return (lanes >= 64) if odd else (lanes < 64)


def stacked_heads(tile):
    zero = jnp.zeros_like(tile)
    even = lane_mask(tile.shape[0], False)
    return jnp.concatenate([jnp.where(even, tile, zero), jnp.where(even, zero, tile)], axis=0)


def merged_heads(pair):
    half = pair.shape[0] // 2
    even = lane_mask(half, False)
    return jnp.where(even, pair[:half], pair[half:])


def row_range(rows, low, high, width=128):
    ids = lax.broadcasted_iota(jnp.int32, (rows, width), 0)
    return (ids >= low) & (ids < high)


def spread_heads(flipped):
    none = jnp.zeros((64, flipped.shape[1]), flipped.dtype)
    left = jnp.concatenate([flipped[:64], none], axis=0)
    right = jnp.concatenate([none, flipped[64:]], axis=0)
    return jnp.concatenate([left, right], axis=1)


def head_ones(value):
    rows = lax.broadcasted_iota(jnp.int32, (2 * KEYS, 128), 0) < KEYS
    lanes = lax.broadcasted_iota(jnp.int32, (2 * KEYS, 128), 1) < 64
    return jnp.where(rows == lanes, value, 0.0).astype(bf16)


def lane_ones(value):
    rows = lax.broadcasted_iota(jnp.int32, (128, 2 * KEYS), 0) < 64
    lanes = lax.broadcasted_iota(jnp.int32, (128, 2 * KEYS), 1) < KEYS
    return jnp.where(rows == lanes, value, 0.0).astype(bf16)


def pack_kernel(spot, proj, joint, out, up, down, half_early, half_late, early, late):
    rows = joint.shape[0]
    for part in range(3):
        early[part * rows : part * rows + rows, :] = joint[:, part * D : part * D + D]
    early[3 * rows :, :] = proj[...]
    late[:rows, :] = out[...]
    for part in range(4):
        late[(part + 1) * rows : (part + 2) * rows, :] = up[:, part * D : part * D + D]
    late[5 * rows : 5 * rows + down.shape[0], :] = down[...]
    for source, target in ((early, half_early), (late, half_late)):
        half = target.shape[0]
        target[...] = source[pl.ds(pl.multiple_of(spot[0] * half, 16), half), :]


def pack(core, proj, joint, out, up, down):
    rows, low, deep = joint.shape[0], proj.shape[0], down.shape[0]
    sizes = (3 * rows + low, 5 * rows + deep)
    vmem = pl.BlockSpec(memory_space=pltpu.VMEM)
    return pl.pallas_call(
        pack_kernel,
        in_specs=[pl.BlockSpec(memory_space=pltpu.SMEM)] + [vmem] * 5,
        out_specs=[vmem, vmem],
        out_shape=[shape_of((size // 2, D), bf16) for size in sizes],
        scratch_shapes=[pltpu.VMEM((size, D), bf16) for size in sizes],
        compiler_params=settings(),
        name="pack",
    )(core, proj, joint, out, up, down)


def unpack_early(core, mine, other, joint_w, proj):
    groups, half, _ = mine.shape
    rows, low = D // groups, POSH // groups

    def place(side, source):
        for group in range(groups):
            at = 0
            while at < half:
                row = side * half + at
                if row < 3 * rows:
                    part, inner = divmod(row, rows)
                    size = min(half - at, rows - inner)
                    first = group * rows + inner
                    joint_w[first : first + size, part * D : part * D + D] = source[group, at : at + size]
                else:
                    size = half - at
                    first = group * low + row - 3 * rows
                    proj[first : first + size, :] = source[group, at : at + size]
                at += size

    @pl.when(core == 0)
    def _():
        place(0, mine)
        place(1, other)

    @pl.when(core == 1)
    def _():
        place(0, other)
        place(1, mine)


def unpack_late(core, mine, other, out_w, up_w, down_w):
    groups, half, _ = mine.shape
    rows, deep = D // groups, FF // groups

    def place(side, source):
        for group in range(groups):
            at = 0
            while at < half:
                row = side * half + at
                if row < rows:
                    size = min(half - at, rows - row)
                    first = group * rows + row
                    out_w[first : first + size, :] = source[group, at : at + size]
                elif row < 5 * rows:
                    block, inner = divmod(row - rows, rows)
                    size = min(half - at, rows - inner)
                    first = group * rows + inner
                    up_w[first : first + size, block * D : block * D + D] = source[group, at : at + size]
                else:
                    size = half - at
                    first = group * deep + row - 5 * rows
                    down_w[first : first + size, :] = source[group, at : at + size]
                at += size

    @pl.when(core == 0)
    def _():
        place(0, mine)
        place(1, other)

    @pl.when(core == 1)
    def _():
        place(0, other)
        place(1, mine)


def picked(rows, first, source):
    ids = lax.broadcasted_iota(jnp.int32, (16, rows), 0) - lax.broadcasted_iota(jnp.int32, (16, rows), 1)
    return dot(jnp.where(ids == first, 1.0, 0.0).astype(bf16), source)


def split16(values):
    high = values.astype(bf16)
    return high, (values - high.astype(f32)).astype(bf16)


def place_inputs(centers, place_weight, place_bias, cen, place_w):
    for tile in range(cen.shape[0]):
        high, rest = split16(centers[:, tile * ROWS : tile * ROWS + ROWS])
        ids = lax.broadcasted_iota(jnp.int32, (16, ROWS), 0)
        ones = jnp.where((ids == 9) | (ids == 10), 1.0, 0.0)
        cen[tile] = (picked(3, 0, high) + picked(3, 3, rest) + picked(3, 6, high) + ones).astype(bf16)
    high, rest = split16(place_weight[...])
    bias_high, bias_rest = split16(place_bias[...])
    value = picked(3, 0, high) + picked(3, 3, high) + picked(3, 6, rest) + picked(1, 9, bias_high) + picked(1, 10, bias_rest)
    place_w[...] = value.astype(bf16)


def front_kernel(core, tokens, centers, targets, vec, place_weight, place_bias, mine, other,
                 entry, joint, mixture, shares, weights, joint_w, proj, cen, place_w, qkv):
    step = pl.program_id(0)

    @pl.when(step == 0)
    def _():
        qkv[ROWS:, :] = jnp.zeros((qkv.shape[0] - ROWS, 3 * D), bf16)
        unpack_early(core[0], mine, other, joint_w, proj)
        place_inputs(centers, place_weight, place_bias, cen, place_w)

    pre = dot(cen[step], place_w[...], TN)
    low = (pre * cdf(pre)).astype(bf16)
    placed = dot(low, proj[...]) + vec[1:2, :]
    hidden = hidden_column(targets[0], ROWS)
    rows = jnp.where(hidden > 0.5, vec[0:1, :], tokens[...].astype(f32)) + placed
    entry[...] = rows
    unit, _ = normalised(rows)
    normed = (unit * vec[2:3, :] + vec[3:4, :]).astype(bf16)
    for part in range(9):
        cols = slice(part * 128, part * 128 + 128)
        value = dot(normed, joint_w[:, cols])
        if part < 3:
            value = value * (0.125 * LOG2E)
        value = value.astype(bf16)
        qkv[:ROWS, cols] = value
        joint[:, cols] = value
    jobs = [(pair, cloud) for pair in range(PAIRS) for cloud in range(TILE)]
    tails = {}
    lanes = lax.broadcasted_iota(jnp.int32, (1, 2 * KEYS), 1) % KEYS
    sums_of = head_ones(1.0)
    for at in range(0, len(jobs), GROUP):
        group = jobs[at : at + GROUP]
        scores = []
        for pair, cloud in group:
            base = cloud * STEP
            query = qkv[base : base + WIN, pair * 128 : pair * 128 + 128]
            key = qkv[base : base + KEYS, D + pair * 128 : D + pair * 128 + 128]
            scores.append(dot(query, spread_heads(key.T)))
        exps = []
        for (pair, cloud), score in zip(group, scores):
            live = (lanes >= 2 * cloud) & (lanes < 2 * cloud + SEQ - 1)
            score = jnp.where(live, score, -1e30)
            parts = []
            for half in (score[:, :KEYS], score[:, KEYS:]):
                parts.append(jnp.exp2(half - jnp.max(half, axis=-1, keepdims=True)).astype(bf16))
            exps.append(jnp.concatenate(parts, axis=1))
        boths = []
        for (pair, cloud), e in zip(group, exps):
            base = cloud * STEP
            value = qkv[base : base + KEYS, 2 * D + pair * 128 : 2 * D + pair * 128 + 128]
            boths.append(dot(e, jnp.concatenate([stacked_heads(value), sums_of], axis=1)))
        for (pair, cloud), e, both in zip(group, exps, boths):
            base = cloud * STEP
            cols = slice(pair * 128, pair * 128 + 128)
            share = 1.0 / both[:, 128:]
            mix = both[:, :128] * share
            spot = slice(pair * 256, pair * 256 + 256)
            none = jnp.zeros((16, 2 * KEYS), bf16)
            weights[cloud, :16, spot] = jnp.where(row_range(16, 2 * cloud, 16, 256), e[:16], none)
            weights[cloud, 16:64, spot] = e[16:64]
            weights[cloud, 64:80, spot] = jnp.where(row_range(16, 0, 2 * cloud + 2, 256), e[64:80], none)
            head_mix, head_share = mix[:16], share[:16]
            if cloud:
                head = row_range(16, 0, 2 * cloud)
                tail_mix, tail_share = tails[pair]
                head_mix = jnp.where(head, tail_mix, head_mix)
                head_share = jnp.where(head, tail_share, head_share)
            mixture[base : base + 16, cols] = head_mix.astype(bf16)
            shares[base : base + 16, cols] = head_share.astype(bf16)
            mixture[base + 16 : base + 64, cols] = mix[16:64].astype(bf16)
            shares[base + 16 : base + 64, cols] = share[16:64].astype(bf16)
            tails[pair] = (mix[64:], share[64:])
            if cloud == TILE - 1:
                mixture[ROWS - 16 :, cols] = mix[64:].astype(bf16)
                shares[ROWS - 16 :, cols] = share[64:].astype(bf16)


def whole(shape):
    return pl.BlockSpec(shape, lambda i: (0,) * len(shape))


def rows_of(width, rows=ROWS):
    return pl.BlockSpec((rows, width), lambda i: (i, 0))


def slab(shape):
    return pl.BlockSpec((1, *shape), lambda i: (i,) + (0,) * len(shape))


def shape_of(dims, kind):
    return jax.ShapeDtypeStruct(dims, kind)


def cost(microseconds):
    return pl.CostEstimate(flops=int(microseconds * 9e8), bytes_accessed=int(microseconds * 2e6), transcendentals=0)


def settings():
    return pltpu.CompilerParams(vmem_limit_bytes=VMEM)


def front(core, tokens, centers, targets, vec, place_weight, place_bias, mine, other):
    count = tokens.shape[0]
    steps = count // ROWS
    return pl.pallas_call(
        front_kernel,
        grid=(steps,),
        in_specs=[
            pl.BlockSpec(memory_space=pltpu.SMEM), rows_of(D), whole(centers.shape), slab((1, 256)), whole((8, D)),
            whole((3, POSH)), whole((1, POSH)), whole(mine.shape), whole(other.shape),
        ],
        out_specs=[
            rows_of(D), rows_of(3 * D), rows_of(D), rows_of(D),
            pl.BlockSpec((TILE, WIN, HEADS * KEYS), lambda i: (i, 0, 0)), whole((D, 3 * D)), whole((POSH, D)),
            whole((steps, 16, ROWS)), whole((16, POSH)),
        ],
        out_shape=[
            shape_of((count, D), f32), shape_of((count, 3 * D), bf16),
            shape_of((count, D), bf16), shape_of((count, D), bf16),
            shape_of((steps * TILE, WIN, HEADS * KEYS), bf16), shape_of((D, 3 * D), bf16), shape_of((POSH, D), bf16),
            shape_of((steps, 16, ROWS), bf16), shape_of((16, POSH), bf16),
        ],
        scratch_shapes=[pltpu.VMEM((ROWS + 48, 3 * D), bf16)],
        compiler_params=settings(),
        cost_estimate=cost(28),
        name="front",
    )(core, tokens, centers, targets, vec, place_weight, place_bias, mine, other)


def write_sums(sums, order, first, values):
    size = sums.shape[0] // len(order)
    at = 0
    while at < values.shape[0]:
        row = first + at
        segment, inner = divmod(row, size)
        step = min(size - inner, values.shape[0] - at)
        spot = order[segment] * size + inner
        sums[spot : spot + step, :] = values[at : at + step].astype(bf16)
        at += step


def share_halves(core, sums, kept, sent):
    half = sent.shape[0]
    kept[...] = sums[pl.ds(pl.multiple_of(core * half, 16), half), :]
    sent[...] = sums[pl.ds(pl.multiple_of((1 - core) * half, 16), half), :]


def padded(rows, size):
    return -(-rows // (16 * size)) * 16 * size


def middle_kernel(chunk, order, core, entry, mixture, shares, cot, vec, up_b, mine, other,
                  middle, gated, mid_grad, mix_grad, kept, sent, up_bg, vec_g, down_w,
                  down_acc, up_acc, out_acc, out_w, up_w, sums):
    step = pl.program_id(0)

    @pl.when(step == 0)
    def _():
        unpack_late(core[0], mine, other, out_w, up_w, down_w)
        for ref in (down_acc, up_acc, out_acc, up_bg, vec_g):
            ref[...] = jnp.zeros(ref.shape, ref.dtype)

    parts = FF // chunk
    spans = [slice(part * chunk, part * chunk + chunk) for part in range(parts)]
    mix = mixture[...]
    cotangent = cot[...]
    mid = entry[...] + (dot(mix, out_w[...]) + vec[4:5, :])
    gates = [dot(cotangent, down_w[spans[0], :], NT)]
    middle[...] = mid
    unit, scale = normalised(mid)
    normed = (unit * vec[5:6, :] + vec[6:7, :]).astype(bf16)
    lows = []

    def down_part(part):
        down_acc[:, spans[part]] += dot(cotangent, gated[:, spans[part]], TN)

    def up_part(part):
        up_acc[:, spans[part]] += dot(normed, lows[part], TN)

    for part in range(parts):
        cols = spans[part]
        raised = dot(normed, up_w[:, cols]) + up_b[:, cols]
        if part + 1 < parts:
            gates.append(dot(cotangent, down_w[spans[part + 1], :], NT))
        mass = cdf(raised)
        gated[:, cols] = (raised * mass).astype(bf16)
        grad = gates[part] * smooth_slope(raised, mass)
        up_bg[:, cols] += jnp.sum(grad, axis=0, keepdims=True)
        lows.append(grad.astype(bf16))
        if part:
            down_part(part - 1)
            if part > 1:
                up_part(part - 2)
    back = dot(jnp.concatenate(lows, axis=1), up_w[...], NT)
    up_part(parts - 2)
    down_part(parts - 1)
    up_part(parts - 1)
    upstream = cotangent.astype(f32)
    tilted = back * vec[5:6, :]
    grad = upstream + scale * (tilted - row_mean(tilted) - unit * row_mean(tilted * unit))
    mid_grad[...] = grad
    low = grad.astype(bf16)
    mix_grad[...] = (dot(low, out_w[...], NT) * shares[...].astype(f32)).astype(bf16)
    out_acc[...] += dot(mix, low, TN)
    vec_g[0:1, :] += jnp.sum(back * unit, axis=0, keepdims=True)
    vec_g[1:2, :] += jnp.sum(back, axis=0, keepdims=True)
    vec_g[2:3, :] += jnp.sum(grad, axis=0, keepdims=True)
    vec_g[3:4, :] += jnp.sum(upstream, axis=0, keepdims=True)

    @pl.when(step == pl.num_programs(0) - 1)
    def _():
        for part in range(4):
            write_sums(sums, order, part * D, up_acc[:, part * D : part * D + D])
        write_sums(sums, order, 4 * D, down_acc[...].T)
        write_sums(sums, order, 8 * D, out_acc[...])
        if sums.shape[0] > 9 * D:
            write_sums(sums, order, 9 * D, jnp.zeros((sums.shape[0] - 9 * D, D), f32))
        share_halves(core[0], sums, kept, sent)


def middle_part(core, entry, mixture, shares, cot, vec, up_b, mine, other, order, rows=1056, chunk=512):
    count = entry.shape[0]
    size = padded(9 * D, len(order))
    return pl.pallas_call(
        functools.partial(middle_kernel, chunk, order),
        grid=(count // rows,),
        in_specs=[
            pl.BlockSpec(memory_space=pltpu.SMEM), rows_of(D, rows), rows_of(D, rows), rows_of(D, rows), rows_of(D, rows),
            whole((8, D)), whole((1, FF)), whole(mine.shape), whole(other.shape),
        ],
        out_specs=[
            rows_of(D, rows), rows_of(FF, rows), rows_of(D, rows), rows_of(D, rows),
            whole((size // 2, D)), whole((size // 2, D)), whole((1, FF)), whole((8, D)), whole((FF, D)),
        ],
        out_shape=[
            shape_of((count, D), f32), shape_of((count, FF), bf16), shape_of((count, D), f32), shape_of((count, D), bf16),
            shape_of((size // 2, D), bf16), shape_of((size // 2, D), bf16),
            shape_of((1, FF), f32), shape_of((8, D), f32), shape_of((FF, D), bf16),
        ],
        scratch_shapes=[
            pltpu.VMEM((D, FF), f32), pltpu.VMEM((D, FF), f32), pltpu.VMEM((D, D), f32),
            pltpu.VMEM((D, D), bf16), pltpu.VMEM((D, FF), bf16), pltpu.VMEM((size, D), bf16),
        ],
        compiler_params=settings(),
        cost_estimate=cost(55),
        name="middle",
    )(core, entry, mixture, shares, cot, vec, up_b, mine, other)


def back_kernel(is_first, is_last, order, *refs):
    entry, joint, mixture, weights, mix_grad, mid_grad, cen, targets, vec, place_w, proj, joint_w = refs[:12]
    refs = refs[12:]
    if not is_first:
        before, refs = refs[1:5], refs[5:]
    if is_last:
        core, up_bg, mid_vec_g, tokens_g, kept, sent, joint_g, proj_g, place_g, vec_g, qkv, dqkv, sums = refs
    else:
        tokens_g, joint_g, proj_g, place_g, vec_g, qkv, dqkv = refs
    step = pl.program_id(0)

    @pl.when(step == 0)
    def _():
        for at, ref in enumerate((joint_g, proj_g, place_g, vec_g)):
            ref[...] = jnp.zeros(ref.shape, ref.dtype) if is_first else before[at][...]
        qkv[ROWS:, :] = jnp.zeros((qkv.shape[0] - ROWS, 3 * D), bf16)

    qkv[:ROWS, :] = joint[...]
    pre = dot(cen[0], place_w[...], TN)
    unit, scale = normalised(entry[...])
    normed = (unit * vec[2:3, :] + vec[3:4, :]).astype(bf16)
    minus = lane_ones(-1.0)
    jobs = [(pair, cloud) for pair in range(PAIRS) for cloud in range(TILE)]
    tails = {}
    for at in range(0, len(jobs), GROUP):
        group = jobs[at : at + GROUP]
        gaps = []
        for pair, cloud in group:
            base = cloud * STEP
            window = slice(base, base + WIN)
            cols = slice(pair * 128, pair * 128 + 128)
            value = qkv[base : base + KEYS, 2 * D + pair * 128 : 2 * D + pair * 128 + 128]
            dmw = mix_grad[window, cols]
            left = jnp.concatenate([dmw, dmw * mixture[window, cols]], axis=1)
            gaps.append(dot(left, jnp.concatenate([spread_heads(value.T), minus], axis=0)))
        es, dss = [], []
        for (pair, cloud), gap in zip(group, gaps):
            e = weights[cloud, :, pair * 256 : pair * 256 + 256]
            es.append(e)
            dss.append((e.astype(f32) * gap).astype(bf16))
        results = []
        for (pair, cloud), e, ds in zip(group, es, dss):
            base = cloud * STEP
            query = stacked_heads(qkv[base : base + WIN, pair * 128 : pair * 128 + 128])
            key = stacked_heads(qkv[base : base + KEYS, D + pair * 128 : D + pair * 128 + 128])
            sdm = stacked_heads(mix_grad[base : base + WIN, pair * 128 : pair * 128 + 128])
            e = jnp.concatenate([e[:, :KEYS], e[:, KEYS:]], axis=0)
            tall = jnp.concatenate([ds[:, :KEYS], ds[:, KEYS:]], axis=0)
            results.append((dot(ds, key), dot(tall, query, TN), dot(e, sdm, TN)))
        for (pair, cloud), (dq, dk, dv) in zip(group, results):
            base = cloud * STEP
            parts = (dq * 0.125, dk[:WIN] * (1.0 / LOG2E), dv[:WIN])
            for which, part in enumerate(parts):
                cols = slice(which * D + pair * 128, which * D + pair * 128 + 128)
                head = part[:16]
                if cloud:
                    head = jnp.where(row_range(16, 0, 2 * cloud), tails[pair, which], head)
                dqkv[base : base + 16, cols] = head.astype(bf16)
                dqkv[base + 16 : base + 64, cols] = part[16:64].astype(bf16)
                tails[pair, which] = part[64:80]
                if cloud == TILE - 1:
                    dqkv[ROWS - 16 :, cols] = part[64:80].astype(bf16)


    back = dot(dqkv[...], joint_w[...], NT)
    for part in range(3):
        cols = slice(part * D, part * D + D)
        joint_g[:, cols] += dot(normed, dqkv[:, cols], TN)
    tilted = back * vec[2:3, :]
    grad = mid_grad[...] + scale * (tilted - row_mean(tilted) - unit * row_mean(tilted * unit))
    low = grad.astype(bf16)
    mass = cdf(pre)
    place_low = (pre * mass).astype(bf16)
    pre_grad = dot(low, proj[...], NT) * smooth_slope(pre, mass)
    proj_g[...] += dot(place_low, low, TN)
    hidden = hidden_column(targets[0], ROWS)
    marked = jnp.where(hidden > 0.5, grad, 0.0)
    tokens_g[...] = (grad - marked).astype(bf16)
    high_part = pre_grad.astype(bf16)
    low_part = (pre_grad - high_part.astype(f32)).astype(bf16)
    place_g[...] += dot(cen[0], jnp.concatenate([high_part, low_part], axis=1))
    vec_g[0:1, :] += jnp.sum(marked, axis=0, keepdims=True)
    vec_g[1:2, :] += jnp.sum(grad, axis=0, keepdims=True)
    vec_g[2:3, :] += jnp.sum(back * unit, axis=0, keepdims=True)
    vec_g[3:4, :] += jnp.sum(back, axis=0, keepdims=True)
    if not is_last:
        return

    @pl.when(step == pl.num_programs(0) - 1)
    def _():
        for part in range(3):
            write_sums(sums, order, part * D, joint_g[:, part * D : part * D + D])
        write_sums(sums, order, 3 * D, proj_g[...])
        place = place_g[:, :POSH] + place_g[:, POSH:]
        place_weight = place[0:3] + place_g[3:6, :POSH]
        small = jnp.concatenate(
            [
                vec_g[0:4, :],
                mid_vec_g[0:4, :],
                jnp.concatenate([place_weight[0:1], place_weight[1:2], place_weight[2:3]], axis=1),
                jnp.concatenate([place[9:10], jnp.zeros((1, D - POSH), f32)], axis=1),
                jnp.concatenate([up_bg[:, part * D : part * D + D] for part in range(4)], axis=0),
                jnp.zeros((sums.shape[0] - 3 * D - POSH - 14, D), f32),
            ],
            axis=0,
        )
        write_sums(sums, order, 3 * D + POSH, small)
        share_halves(core[0], sums, kept, sent)


def back_part(given, first, steps, order, before=None, extra=None):
    count = given[0].shape[0]

    def shifted(width):
        return pl.BlockSpec((ROWS, width), lambda i: (i + first, 0))

    def shifted_slab(shape):
        return pl.BlockSpec((1, *shape), lambda i: (i + first, 0, 0))

    accs = [(D, 3 * D), (POSH, D), (16, 256), (8, D)]
    in_specs = [
        shifted(D), shifted(3 * D), shifted(D),
        pl.BlockSpec((TILE, WIN, HEADS * KEYS), lambda i: (i + first, 0, 0)),
        shifted(D), shifted(D), shifted_slab((16, ROWS)), shifted_slab((1, 256)),
        whole((8, D)), whole((16, POSH)), whole((POSH, D)), whole((D, 3 * D)),
    ]
    given = list(given)
    if before is not None:
        given += before
        in_specs += [pl.BlockSpec(memory_space=pl.ANY)] + [whole(acc) for acc in accs]
    out_specs, out_shape = [shifted(D)], [shape_of((count, D), bf16)]
    scratch = [pltpu.VMEM((ROWS + 48, 3 * D), bf16), pltpu.VMEM((ROWS, 3 * D), bf16)]
    if extra is not None:
        given += extra
        in_specs += [pl.BlockSpec(memory_space=pltpu.SMEM), whole((1, FF)), whole((8, D))]
        size = padded(3 * D + POSH + 16, len(order))
        out_specs += [whole((size // 2, D))] * 2
        out_shape += [shape_of((size // 2, D), bf16)] * 2
        scratch = [pltpu.VMEM(acc, f32) for acc in accs] + scratch + [pltpu.VMEM((size, D), bf16)]
    else:
        out_specs += [whole(acc) for acc in accs]
        out_shape += [shape_of(acc, f32) for acc in accs]
    return pl.pallas_call(
        functools.partial(back_kernel, before is None, extra is not None, order),
        grid=(steps,),
        in_specs=in_specs,
        out_specs=out_specs,
        out_shape=out_shape,
        scratch_shapes=scratch,
        input_output_aliases={} if before is None else {12: 0},
        compiler_params=settings(),
        cost_estimate=cost(5 * steps),
        name="back",
    )(*given)


def finish_kernel(middle, gated, vec, down_w, output):
    output[...] = (middle[...] + (dot(gated[...], down_w[...]) + vec[7:8, :])).astype(bf16)


def finish(middle, gated, vec, down_w, rows=528):
    count = middle.shape[0]
    return pl.pallas_call(
        finish_kernel,
        grid=(count // rows,),
        in_specs=[rows_of(D, rows), rows_of(FF, rows), whole((8, D)), whole((FF, D))],
        out_specs=rows_of(D, rows),
        out_shape=shape_of((count, D), bf16),
        compiler_params=settings(),
        cost_estimate=cost(12),
        name="finish",
    )(middle, gated, vec, down_w)


def marked_targets(mask_count, mask_index):
    clouds, most = mask_index.shape
    slot = jnp.arange(most, dtype=jnp.int32)[None, :]
    cloud = (jnp.arange(clouds, dtype=jnp.int32) % TILE)[:, None]
    targets = jnp.where(slot < mask_count[:, None], mask_index + (1 + SEQ * cloud), -1)
    return jnp.pad(targets, ((0, 0), (0, 32 - most)), constant_values=-1).reshape(clouds // TILE, 1, 256)


def joined_offsets(size):
    held, groups = [0], [[0]]
    bit = size // 2
    while bit:
        groups.append([offset ^ bit for offset in held])
        held = held + groups[-1]
        bit //= 2
    return groups


def close_kernel(groups, spot, *refs):
    pieces, (joint_g, proj_g, small, sums) = refs[:-4], refs[-4:]
    segment = pieces[0].shape[0]
    for piece, offsets in zip(pieces, groups):
        for at, offset in enumerate(offsets):
            row = pl.multiple_of((spot[0] ^ offset) * segment, 16)
            sums[pl.ds(row, segment), :] = piece[at * segment : at * segment + segment, :]
    for part in range(3):
        joint_g[:, part * D : part * D + D] = sums[part * D : part * D + D, :].astype(f32)
    proj_g[...] = sums[3 * D : 3 * D + POSH, :].astype(f32)
    small[...] = sums[3 * D + POSH : 3 * D + POSH + 16, :].astype(f32)


def close(spot, pieces, size):
    vmem = pl.BlockSpec(memory_space=pltpu.VMEM)
    return pl.pallas_call(
        functools.partial(close_kernel, joined_offsets(size)),
        in_specs=[pl.BlockSpec(memory_space=pltpu.SMEM)] + [vmem] * len(pieces),
        out_specs=[vmem] * 3,
        out_shape=[shape_of((D, 3 * D), f32), shape_of((POSH, D), f32), shape_of((16, D), f32)],
        scratch_shapes=[pltpu.VMEM((pieces[0].shape[0] * size, D), bf16)],
        compiler_params=settings(),
        name="close",
    )(spot, *pieces)


CALLS = 4


def bits_of(size):
    return [1 << bit for bit in range(size.bit_length() - 1)]


def spot_of(index, size):
    spot, span = 0, size
    for bit in bits_of(size):
        span //= 2
        spot += span * ((index // bit) % 2)
    return spot


def segments(size):
    return [spot_of(index, size) for index in range(size)]


def swapped(values, bit, size):
    return lax.ppermute(values, "dp", [(i, i ^ bit) for i in range(size)])


def total(terms):
    return sum(term.astype(f32) for term in terms).astype(bf16)


def halves(terms, bit):
    side = (lax.axis_index("dp") // bit) % 2
    pairs = [term.reshape(2, term.shape[0] // 2, D) for term in terms]
    sent = [lax.dynamic_index_in_dim(pair, 1 - side, 0, keepdims=False) for pair in pairs]
    kept = [lax.dynamic_index_in_dim(pair, side, 0, keepdims=False) for pair in pairs]
    return sent, kept


def halved(terms, bit, size, ready=None):
    sent, kept = halves(terms, bit)
    return kept + [swapped(total(sent) if ready is None else ready, bit, size)]


def across(terms, bit, size):
    value = total(terms)
    return [value, lax.ppermute(value, "fsdp", [(i, i ^ bit) for i in range(size)])]


def tied(first, second):
    return lax.optimization_barrier((first, second))


def wide(blocks):
    return jnp.concatenate(blocks, axis=1).astype(f32)


def per_device(
    sizes,
    tokens,
    centers,
    mask_count,
    mask_index,
    mask_embed,
    place_weight,
    place_bias,
    place_proj,
    place_shift,
    norm_gain,
    norm_shift,
    joint_weight,
    out_weight,
    out_bias,
    mlp_gain,
    mlp_shift,
    up_weight,
    up_bias,
    down_weight,
    down_bias,
    cotangent,
):
    dp, fsdp = sizes["dp"], sizes["fsdp"]
    spot = lax.axis_index("dp").astype(jnp.int32)[None]
    core = spot % 2
    early, late = pack(core, place_proj, joint_weight, out_weight, up_weight, down_weight)
    early = lax.all_gather(early, "fsdp", axis=0)
    early_other = swapped(early, 1, dp)
    late, early = tied(late, early)
    late = lax.all_gather(late, "fsdp", axis=0)
    targets = marked_targets(mask_count, mask_index)
    vec = jnp.stack([mask_embed, place_shift, norm_gain, norm_shift, out_bias, mlp_gain, mlp_shift, down_bias])
    up_b = up_bias[None, :]
    entry, joint, mixture, shares, weights, joint_w, proj, cen, place_w = front(
        core, tokens, centers, targets, vec, place_weight, place_bias[None, :], early, early_other
    )
    late_other = swapped(late, 1, dp)
    late, mixture = tied(late, mixture)
    late_other = swapped(late, 1, dp)
    order = segments(dp)
    middle, gated, mid_grad, mix_grad, kept, sent, up_bg, vec_g, down_w = middle_part(
        core, entry, mixture, shares, cotangent, vec, up_b, late, late_other, order
    )
    stages = [functools.partial(halved, bit=bit, size=dp) for bit in bits_of(dp)]
    stages += [functools.partial(across, bit=bit, size=fsdp) for bit in bits_of(fsdp)]
    steps = tokens.shape[0] // ROWS
    parts = [steps * (part + 1) // CALLS - steps * part // CALLS for part in range(CALLS)]
    before, first = None, 0
    sums = [kept, swapped(sent, 1, dp)]
    for part, count in enumerate(parts):
        if part:
            mix_grad, sums[-1] = tied(mix_grad, sums[-1])
            sums = stages[part](sums)
        given = (entry, joint, mixture, weights, mix_grad, mid_grad, cen, targets, vec, place_w, proj, joint_w)
        extra = [core, up_bg, vec_g] if part == CALLS - 1 else None
        before = back_part(given, first, count, order, before, extra)
        first += count
    tokens_grad, kept, sent = before
    sent, sums[-1] = tied(sent, sums[-1])
    for stage in stages[CALLS:]:
        sums = stage(sums)
    last = stages[1]([kept, swapped(sent, 1, dp)])
    output = finish(middle, gated, vec, down_w)
    sums[-1], output = tied(sums[-1], output)
    sums = total(sums)
    last[-1], sums = tied(last[-1], sums)
    sums = lax.all_gather(sums, "dp", axis=0, tiled=True)
    for stage in stages[2:]:
        last = stage(last)
    pieces = [total(last)]
    for bit in reversed(bits_of(dp)):
        held = pieces[0] if len(pieces) == 1 else jnp.concatenate(pieces, axis=0)
        pieces.append(swapped(held, bit, dp))
    joint_grad, proj_grad, small = close(spot, pieces, dp)
    up_grad = wide([sums[part * D : part * D + D] for part in range(4)])
    down_grad = sums[4 * D : 8 * D].astype(f32)
    out_grad = sums[8 * D : 9 * D].astype(f32)
    return (
        output,
        tokens_grad,
        small[0],
        small[8].reshape(3, POSH),
        small[9, :POSH],
        proj_grad,
        small[1],
        small[2],
        small[3],
        joint_grad,
        out_grad,
        small[6],
        small[4],
        small[5],
        up_grad,
        small[10:14].reshape(FF),
        down_grad,
        small[7],
    )


def solution(mesh):
    rows = P(("dp", "fsdp"), None)
    in_specs = (
        rows,
        P(None, ("dp", "fsdp")),
        P(("dp", "fsdp")),
        rows,
        P(),
        P(),
        P(),
        P("fsdp", None),
        P(),
        P(),
        P(),
        P("fsdp", None),
        P("fsdp", None),
        P(),
        P(),
        P(),
        P("fsdp", None),
        P(),
        P("fsdp", None),
        P(),
        rows,
    )
    out_specs = (rows, rows) + (P(),) * 16
    return jax.shard_map(
        functools.partial(per_device, dict(mesh.shape)), mesh=mesh, in_specs=in_specs, out_specs=out_specs, check_vma=False
    )
```

```python
import functools

import jax
import jax.numpy as jnp
from jax import lax
from jax.experimental import pallas as pl
from jax.experimental.pallas import tpu as pltpu
from jax.sharding import PartitionSpec as P

D = 384
HEADS = 6
FF = 1536
POSH = 128
SEQ = 66
TILE = 8
ROWS = TILE * SEQ
STEP = 64
WIN = 80
KEYS = 128
PAIRS = HEADS // 2
GROUP = 8
SUBS = 2
VMEM = 60 * 2**20
LOG2E = 1.4426950408889634
ROOT_HALF = 0.7071067811865476
PDF = 0.3989422804014327
bf16 = jnp.bfloat16
f32 = jnp.float32

NN = (((1,), (0,)), ((), ()))
NT = (((1,), (1,)), ((), ()))
TN = (((0,), (0,)), ((), ()))


def dot(left, right, dims=NN):
    return lax.dot_general(left, right, dims, preferred_element_type=f32)


def cdf(u):
    return 0.5 + 0.5 * lax.erf(u * ROOT_HALF)


def smooth_slope(u, mass):
    return mass + u * (PDF * jnp.exp2(u * u * (-0.5 * LOG2E)))


def row_mean(values):
    return jnp.sum(values, axis=-1, keepdims=True) * (1.0 / values.shape[-1])


def normalised(values):
    centred = values - row_mean(values)
    scale = lax.rsqrt(row_mean(centred * centred) + 1e-05)
    return centred * scale, scale


def hidden_column(targets, rows):
    row_ids = lax.broadcasted_iota(jnp.int32, (rows, targets.shape[1]), 0)
    hits = jnp.where(row_ids == targets, 1.0, 0.0)
    return jnp.max(hits, axis=1, keepdims=True)


def lane_mask(rows, odd, kind=bf16):
    lanes = lax.broadcasted_iota(jnp.int32, (rows, 128), 1)
    return (lanes >= 64) if odd else (lanes < 64)


def stacked_heads(tile):
    zero = jnp.zeros_like(tile)
    even = lane_mask(tile.shape[0], False)
    return jnp.concatenate([jnp.where(even, tile, zero), jnp.where(even, zero, tile)], axis=0)


def merged_heads(pair):
    half = pair.shape[0] // 2
    even = lane_mask(half, False)
    return jnp.where(even, pair[:half], pair[half:])


def row_range(rows, low, high, width=128):
    ids = lax.broadcasted_iota(jnp.int32, (rows, width), 0)
    return (ids >= low) & (ids < high)


def spread_heads(flipped):
    none = jnp.zeros((64, flipped.shape[1]), flipped.dtype)
    left = jnp.concatenate([flipped[:64], none], axis=0)
    right = jnp.concatenate([none, flipped[64:]], axis=0)
    return jnp.concatenate([left, right], axis=1)


def head_ones(value):
    rows = lax.broadcasted_iota(jnp.int32, (2 * KEYS, 128), 0) < KEYS
    lanes = lax.broadcasted_iota(jnp.int32, (2 * KEYS, 128), 1) < 64
    return jnp.where(rows == lanes, value, 0.0).astype(bf16)


def lane_ones(value):
    rows = lax.broadcasted_iota(jnp.int32, (128, 2 * KEYS), 0) < 64
    lanes = lax.broadcasted_iota(jnp.int32, (128, 2 * KEYS), 1) < KEYS
    return jnp.where(rows == lanes, value, 0.0).astype(bf16)


def pack_kernel(spot, proj, joint, out, up, down, *refs):
    vectors, (packed, vec, early, late) = refs[:8], refs[8:]
    for at, vector in enumerate(vectors):
        vec[at : at + 1, :] = vector[...].reshape(1, D)
    rows = joint.shape[0]
    for part in range(3):
        early[part * rows : part * rows + rows, :] = joint[:, part * D : part * D + D]
    early[3 * rows :, :] = proj[...]
    late[:rows, :] = out[...]
    for part in range(4):
        late[(part + 1) * rows : (part + 2) * rows, :] = up[:, part * D : part * D + D]
    late[5 * rows : 5 * rows + down.shape[0], :] = down[...]
    half = early.shape[0] // 2
    piece = packed.shape[0] - half
    packed[:half, :] = early[pl.ds(pl.multiple_of((spot[0] % 2) * half, 16), half), :]
    chips = late.shape[0] // piece // 2
    own = (spot[0] % 2) * chips + spot[0] // 2
    packed[half:, :] = late[pl.ds(pl.multiple_of(own * piece, 16), piece), :]


def pack(spot, proj, joint, out, up, down, vectors, parts):
    rows, low, deep = joint.shape[0], proj.shape[0], down.shape[0]
    size = 3 * rows + low
    late = padded(5 * rows + deep, parts)
    vmem = pl.BlockSpec(memory_space=pltpu.VMEM)
    return pl.pallas_call(
        pack_kernel,
        in_specs=[pl.BlockSpec(memory_space=pltpu.SMEM)] + [vmem] * 13,
        out_specs=[vmem, vmem],
        out_shape=[shape_of((size // 2 + late // parts, D), bf16), shape_of((8, D), f32)],
        scratch_shapes=[pltpu.VMEM((size, D), bf16), pltpu.VMEM((late, D), bf16)],
        compiler_params=settings(),
        name="pack",
    )(spot, proj, joint, out, up, down, *vectors)


def unpack_early(core, mine, other, joint_w, proj):
    groups = mine.shape[0]
    rows, low = D // groups, POSH // groups
    half = (3 * rows + low) // 2

    def place(side, source):
        for group in range(groups):
            at = 0
            while at < half:
                row = side * half + at
                if row < 3 * rows:
                    part, inner = divmod(row, rows)
                    size = min(half - at, rows - inner)
                    first = group * rows + inner
                    joint_w[first : first + size, part * D : part * D + D] = source[group, at : at + size]
                else:
                    size = half - at
                    first = group * low + row - 3 * rows
                    proj[first : first + size, :] = source[group, at : at + size]
                at += size

    @pl.when(core == 0)
    def _():
        place(0, mine)
        place(1, other)

    @pl.when(core == 1)
    def _():
        place(0, other)
        place(1, mine)


def unpack_late(spot, mine, other, near, near_other, lates, out_w, up_w, down_w):
    _, chips, groups, piece, _ = lates.shape
    rows, deep = D // groups, FF // groups
    half = mine.shape[1] - piece
    core, chip = spot % 2, spot // 2
    for side, own, rest in ((core, mine, near), (1 - core, other, near_other)):
        lates[side, chip] = own[:, half:, :]
        for offset, source in enumerate(rest):
            lates[side, chip ^ (offset + 1)] = source[...]
    for at_chip in range(2 * chips):
        for group in range(groups):
            at = 0
            while at < piece:
                row = at_chip * piece + at
                source = lates.at[at_chip // chips, at_chip % chips, group]
                if row < rows:
                    size = min(piece - at, rows - row)
                    first = group * rows + row
                    out_w[first : first + size, :] = source[at : at + size, :]
                elif row < 5 * rows:
                    block, inner = divmod(row - rows, rows)
                    size = min(piece - at, rows - inner)
                    first = group * rows + inner
                    up_w[first : first + size, block * D : block * D + D] = source[at : at + size, :]
                elif row < 5 * rows + deep:
                    inner = row - 5 * rows
                    size = min(piece - at, deep - inner)
                    first = group * deep + inner
                    down_w[first : first + size, :] = source[at : at + size, :]
                else:
                    size = piece - at
                at += size


def picked(rows, first, source):
    ids = lax.broadcasted_iota(jnp.int32, (16, rows), 0) - lax.broadcasted_iota(jnp.int32, (16, rows), 1)
    return dot(jnp.where(ids == first, 1.0, 0.0).astype(bf16), source)


def split16(values):
    high = values.astype(bf16)
    return high, (values - high.astype(f32)).astype(bf16)


def place_inputs(centers, place_weight, place_bias, cen, place_w):
    for tile in range(cen.shape[0]):
        high, rest = split16(centers[:, tile * ROWS : tile * ROWS + ROWS])
        ids = lax.broadcasted_iota(jnp.int32, (16, ROWS), 0)
        ones = jnp.where((ids == 9) | (ids == 10), 1.0, 0.0)
        cen[tile] = (picked(3, 0, high) + picked(3, 3, rest) + picked(3, 6, high) + ones).astype(bf16)
    high, rest = split16(place_weight[...])
    bias_high, bias_rest = split16(place_bias[...])
    value = picked(3, 0, high) + picked(3, 3, high) + picked(3, 6, rest) + picked(1, 9, bias_high) + picked(1, 10, bias_rest)
    place_w[...] = value.astype(bf16)


def front_kernel(core, tokens, centers, targets, vec, place_weight, place_bias, mine, other,
                 entry, joint, mixture, shares, weights, joint_w, proj, cen, place_w, qkv):
    step = pl.program_id(0)

    @pl.when(step == 0)
    def _():
        for sub in range(SUBS):
            qkv[sub, ROWS:, :] = jnp.zeros((qkv.shape[1] - ROWS, 3 * D), bf16)
        unpack_early(core[0], mine, other, joint_w, proj)
        place_inputs(centers, place_weight, place_bias, cen, place_w)

    lanes = lax.broadcasted_iota(jnp.int32, (1, 2 * KEYS), 1) % KEYS
    sums_of = head_ones(1.0)
    none = jnp.zeros((16, 2 * KEYS), bf16)
    scale_row = jnp.where(lax.broadcasted_iota(jnp.int32, (1, 3 * D), 1) < D, 0.125 * LOG2E, 1.0)

    def normal_rows(sub):
        span = slice(sub * ROWS, sub * ROWS + ROWS)
        pre = dot(cen[step * SUBS + sub], place_w[...], TN)
        low = (pre * cdf(pre)).astype(bf16)
        placed = dot(low, proj[...]) + vec[1:2, :]
        hidden = hidden_column(targets[sub], ROWS)
        rows = jnp.where(hidden > 0.5, vec[0:1, :], tokens[span, :].astype(f32)) + placed
        entry[span, :] = rows
        unit, _ = normalised(rows)
        return (unit * vec[2:3, :] + vec[3:4, :]).astype(bf16)

    def project(sub, normed, first):
        cols = slice(first, min(first + 256, 3 * D))
        value = (dot(normed, joint_w[:, cols]) * scale_row[:, cols]).astype(bf16)
        qkv[sub, :ROWS, cols] = value
        joint[sub * ROWS : sub * ROWS + ROWS, cols] = value

    def score(sub, pair, cloud):
        base = cloud * STEP
        query = qkv[sub, base : base + WIN, pair * 128 : pair * 128 + 128]
        key = qkv[sub, base : base + KEYS, D + pair * 128 : D + pair * 128 + 128]
        return dot(query, spread_heads(key.T))

    def exponentials(cloud, scores):
        live = (lanes >= 2 * cloud) & (lanes < 2 * cloud + SEQ - 1)
        scores = jnp.where(live, scores, -1e30)
        parts = []
        for half in (scores[:, :KEYS], scores[:, KEYS:]):
            parts.append(jnp.exp2(half - jnp.max(half, axis=-1, keepdims=True)).astype(bf16))
        return jnp.concatenate(parts, axis=1)

    def mixed(sub, pair, cloud, e):
        base = cloud * STEP
        value = qkv[sub, base : base + KEYS, 2 * D + pair * 128 : 2 * D + pair * 128 + 128]
        return dot(e, jnp.concatenate([stacked_heads(value), sums_of], axis=1))

    tails = {}

    def store(sub, pair, cloud, e, both):
        base = sub * ROWS + cloud * STEP
        cols = slice(pair * 128, pair * 128 + 128)
        share = 1.0 / both[:, 128:]
        mix = both[:, :128] * share
        spot = slice(pair * 256, pair * 256 + 256)
        at = sub * TILE + cloud
        weights[at, :16, spot] = jnp.where(row_range(16, 2 * cloud, 16, 256), e[:16], none)
        weights[at, 16:64, spot] = e[16:64]
        weights[at, 64:80, spot] = jnp.where(row_range(16, 0, 2 * cloud + 2, 256), e[64:80], none)
        head_mix, head_share = mix[:16], share[:16]
        if cloud:
            head = row_range(16, 0, 2 * cloud)
            tail_mix, tail_share = tails[sub, pair]
            head_mix = jnp.where(head, tail_mix, head_mix)
            head_share = jnp.where(head, tail_share, head_share)
        mixture[base : base + 16, cols] = head_mix.astype(bf16)
        shares[base : base + 16, cols] = head_share.astype(bf16)
        mixture[base + 16 : base + 64, cols] = mix[16:64].astype(bf16)
        shares[base + 16 : base + 64, cols] = share[16:64].astype(bf16)
        tails[sub, pair] = (mix[64:], share[64:])
        if cloud == TILE - 1:
            mixture[base + 64 : base + 80, cols] = mix[64:].astype(bf16)
            shares[base + 64 : base + 80, cols] = share[64:].astype(bf16)

    jobs = [(pair, cloud) for pair in range(PAIRS) for cloud in range(TILE)]
    groups = [jobs[at : at + GROUP] for at in range(0, len(jobs), GROUP)]
    normed = [normal_rows(sub) for sub in range(SUBS)]
    chunks = range(0, 3 * D, 256)
    for first in chunks:
        project(0, normed[0], first)
    waiting = None
    for sub in range(SUBS):
        fill = [functools.partial(project, sub + 1, normed[sub + 1], first) for first in chunks] if sub + 1 < SUBS else []
        share_of = -(-len(fill) // len(groups))
        for group in groups:
            exps = [exponentials(cloud, score(sub, pair, cloud)) for pair, cloud in group]
            for task in fill[:share_of]:
                task()
            fill = fill[share_of:]
            if waiting:
                close_group(mixed, store, *waiting)
            waiting = (sub, group, exps)
    close_group(mixed, store, *waiting)


def close_group(mixed, store, sub, group, exps):
    boths = [mixed(sub, pair, cloud, e) for (pair, cloud), e in zip(group, exps)]
    for (pair, cloud), e, both in zip(group, exps, boths):
        store(sub, pair, cloud, e, both)


def whole(shape):
    return pl.BlockSpec(shape, lambda i: (0,) * len(shape))


def rows_of(width, rows=ROWS):
    return pl.BlockSpec((rows, width), lambda i: (i, 0))


def slab(shape):
    return pl.BlockSpec((1, *shape), lambda i: (i,) + (0,) * len(shape))


def shape_of(dims, kind):
    return jax.ShapeDtypeStruct(dims, kind)


def cost(microseconds):
    return pl.CostEstimate(flops=int(microseconds * 9e8), bytes_accessed=int(microseconds * 2e6), transcendentals=0)


def settings():
    return pltpu.CompilerParams(vmem_limit_bytes=VMEM)


def front(core, tokens, centers, targets, vec, place_weight, place_bias, mine, other):
    count = tokens.shape[0]
    steps = count // ROWS
    rows = SUBS * ROWS
    return pl.pallas_call(
        front_kernel,
        grid=(steps // SUBS,),
        in_specs=[
            pl.BlockSpec(memory_space=pltpu.SMEM), rows_of(D, rows), whole(centers.shape),
            pl.BlockSpec((SUBS, 1, 256), lambda i: (i, 0, 0)), whole((8, D)),
            whole((3, POSH)), whole((1, POSH)), whole(mine.shape), whole(other.shape),
        ],
        out_specs=[
            rows_of(D, rows), rows_of(3 * D, rows), rows_of(D, rows), rows_of(D, rows),
            pl.BlockSpec((SUBS * TILE, WIN, HEADS * KEYS), lambda i: (i, 0, 0)), whole((D, 3 * D)), whole((POSH, D)),
            whole((steps, 16, ROWS)), whole((16, POSH)),
        ],
        out_shape=[
            shape_of((count, D), f32), shape_of((count, 3 * D), bf16),
            shape_of((count, D), bf16), shape_of((count, D), bf16),
            shape_of((steps * TILE, WIN, HEADS * KEYS), bf16), shape_of((D, 3 * D), bf16), shape_of((POSH, D), bf16),
            shape_of((steps, 16, ROWS), bf16), shape_of((16, POSH), bf16),
        ],
        scratch_shapes=[pltpu.VMEM((SUBS, ROWS + 48, 3 * D), bf16)],
        compiler_params=settings(),
        cost_estimate=cost(28),
        name="front",
    )(core, tokens, centers, targets, vec, place_weight, place_bias, mine, other)


def write_sums(sums, order, first, values):
    size = sums.shape[0] // len(order)
    at = 0
    while at < values.shape[0]:
        row = first + at
        segment, inner = divmod(row, size)
        step = min(size - inner, values.shape[0] - at)
        spot = order[segment] * size + inner
        sums[spot : spot + step, :] = values[at : at + step].astype(bf16)
        at += step


def share_halves(core, sums, kept, sent):
    half = sent.shape[0]
    kept[...] = sums[pl.ds(pl.multiple_of(core * half, 16), half), :]
    sent[...] = sums[pl.ds(pl.multiple_of((1 - core) * half, 16), half), :]


def padded(rows, size):
    return -(-rows // (16 * size)) * 16 * size


def middle_kernel(chunk, order, spot, entry, mixture, shares, cot, vec, up_b, mine, other, *refs):
    chips = len(order) // 2
    near, near_other, refs = refs[: chips - 1], refs[chips - 1 : 2 * chips - 2], refs[2 * chips - 2 :]
    (output, mid_grad, mix_grad, kept, sent, up_bg, vec_g,
     down_acc, up_acc, out_acc, out_w, up_w, down_w, gated, sums, lates) = refs
    step = pl.program_id(0)

    @pl.when(step == 0)
    def _():
        unpack_late(spot[0], mine, other, near, near_other, lates, out_w, up_w, down_w)
        for ref in (down_acc, up_acc, out_acc, up_bg, vec_g):
            ref[...] = jnp.zeros(ref.shape, ref.dtype)

    parts = FF // chunk
    spans = [slice(part * chunk, part * chunk + chunk) for part in range(parts)]
    mix = mixture[...]
    cotangent = cot[...]
    mid = entry[...] + (dot(mix, out_w[...]) + vec[4:5, :])
    gates = [dot(cotangent, down_w[spans[0], :], NT)]
    unit, scale = normalised(mid)
    normed = (unit * vec[5:6, :] + vec[6:7, :]).astype(bf16)
    lows = []

    def down_part(part):
        down_acc[:, spans[part]] += dot(cotangent, gated[:, spans[part]], TN)

    def up_part(part):
        up_acc[:, spans[part]] += dot(normed, lows[part], TN)

    for part in range(parts):
        cols = spans[part]
        raised = dot(normed, up_w[:, cols]) + up_b[:, cols]
        if part + 1 < parts:
            gates.append(dot(cotangent, down_w[spans[part + 1], :], NT))
        mass = cdf(raised)
        gated[:, cols] = (raised * mass).astype(bf16)
        grad = gates[part] * smooth_slope(raised, mass)
        up_bg[:, cols] += jnp.sum(grad, axis=0, keepdims=True)
        lows.append(grad.astype(bf16))
        if part:
            down_part(part - 1)
            if part > 1:
                up_part(part - 2)
    back = dot(jnp.concatenate(lows, axis=1), up_w[...], NT)
    up_part(parts - 2)
    down_part(parts - 1)
    up_part(parts - 1)
    output[...] = (mid + (dot(gated[...], down_w[...]) + vec[7:8, :])).astype(bf16)
    upstream = cotangent.astype(f32)
    tilted = back * vec[5:6, :]
    grad = upstream + scale * (tilted - row_mean(tilted) - unit * row_mean(tilted * unit))
    mid_grad[...] = grad
    low = grad.astype(bf16)
    mix_grad[...] = (dot(low, out_w[...], NT) * shares[...].astype(f32)).astype(bf16)
    out_acc[...] += dot(mix, low, TN)
    vec_g[0:1, :] += jnp.sum(back * unit, axis=0, keepdims=True)
    vec_g[1:2, :] += jnp.sum(back, axis=0, keepdims=True)
    vec_g[2:3, :] += jnp.sum(grad, axis=0, keepdims=True)
    vec_g[3:4, :] += jnp.sum(upstream, axis=0, keepdims=True)

    @pl.when(step == pl.num_programs(0) - 1)
    def _():
        for part in range(4):
            write_sums(sums, order, part * D, up_acc[:, part * D : part * D + D])
        write_sums(sums, order, 4 * D, down_acc[...].T)
        write_sums(sums, order, 8 * D, out_acc[...])
        if sums.shape[0] > 9 * D:
            write_sums(sums, order, 9 * D, jnp.zeros((sums.shape[0] - 9 * D, D), f32))
        share_halves(spot[0] % 2, sums, kept, sent)


def middle_part(spot, entry, mixture, shares, cot, vec, up_b, mine, other, near, near_other, order, rows=1056, chunk=512):
    count = entry.shape[0]
    size = padded(9 * D, len(order))
    return pl.pallas_call(
        functools.partial(middle_kernel, chunk, order),
        grid=(count // rows,),
        in_specs=[
            pl.BlockSpec(memory_space=pltpu.SMEM), rows_of(D, rows), rows_of(D, rows), rows_of(D, rows), rows_of(D, rows),
            whole((8, D)), whole((1, FF)), whole(mine.shape), whole(other.shape),
        ]
        + [whole(piece.shape) for piece in [*near, *near_other]],
        out_specs=[
            rows_of(D, rows), rows_of(D, rows), rows_of(D, rows),
            whole((size // 2, D)), whole((size // 2, D)), whole((1, FF)), whole((8, D)),
        ],
        out_shape=[
            shape_of((count, D), bf16), shape_of((count, D), f32), shape_of((count, D), bf16),
            shape_of((size // 2, D), bf16), shape_of((size // 2, D), bf16), shape_of((1, FF), f32), shape_of((8, D), f32),
        ],
        scratch_shapes=[
            pltpu.VMEM((D, FF), f32), pltpu.VMEM((D, FF), f32), pltpu.VMEM((D, D), f32),
            pltpu.VMEM((D, D), bf16), pltpu.VMEM((D, FF), bf16), pltpu.VMEM((FF, D), bf16),
            pltpu.VMEM((rows, FF), bf16), pltpu.VMEM((size, D), bf16),
            pltpu.VMEM((2, len(order) // 2, *near[0].shape), bf16),
        ],
        compiler_params=settings(),
        cost_estimate=cost(55),
        name="middle",
    )(spot, entry, mixture, shares, cot, vec, up_b, mine, other, *near, *near_other)


def back_kernel(is_first, is_last, order, *refs):
    entry, joint, mixture, weights, mix_grad, mid_grad, cen, targets, vec, place_w, proj, joint_w = refs[:12]
    refs = refs[12:]
    if not is_first:
        before, refs = refs[1:5], refs[5:]
    if is_last:
        core, up_bg, mid_vec_g, tokens_g, kept, sent, joint_g, proj_g, place_g, vec_g, qkv, dqkv, sums = refs
    else:
        tokens_g, joint_g, proj_g, place_g, vec_g, qkv, dqkv = refs
    step = pl.program_id(0)

    @pl.when(step == 0)
    def _():
        for at, ref in enumerate((joint_g, proj_g, place_g, vec_g)):
            ref[...] = jnp.zeros(ref.shape, ref.dtype) if is_first else before[at][...]
        qkv[ROWS:, :] = jnp.zeros((qkv.shape[0] - ROWS, 3 * D), bf16)

    qkv[:ROWS, :] = joint[...]
    pre = dot(cen[0], place_w[...], TN)
    unit, scale = normalised(entry[...])
    normed = (unit * vec[2:3, :] + vec[3:4, :]).astype(bf16)
    minus = lane_ones(-1.0)
    jobs = [(pair, cloud) for pair in range(PAIRS) for cloud in range(TILE)]
    tails = {}
    for at in range(0, len(jobs), GROUP):
        group = jobs[at : at + GROUP]
        gaps = []
        for pair, cloud in group:
            base = cloud * STEP
            window = slice(base, base + WIN)
            cols = slice(pair * 128, pair * 128 + 128)
            value = qkv[base : base + KEYS, 2 * D + pair * 128 : 2 * D + pair * 128 + 128]
            dmw = mix_grad[window, cols]
            left = jnp.concatenate([dmw, dmw * mixture[window, cols]], axis=1)
            gaps.append(dot(left, jnp.concatenate([spread_heads(value.T), minus], axis=0)))
        es, dss = [], []
        for (pair, cloud), gap in zip(group, gaps):
            e = weights[cloud, :, pair * 256 : pair * 256 + 256]
            es.append(e)
            dss.append((e.astype(f32) * gap).astype(bf16))
        results = []
        for (pair, cloud), e, ds in zip(group, es, dss):
            base = cloud * STEP
            query = stacked_heads(qkv[base : base + WIN, pair * 128 : pair * 128 + 128])
            key = stacked_heads(qkv[base : base + KEYS, D + pair * 128 : D + pair * 128 + 128])
            sdm = stacked_heads(mix_grad[base : base + WIN, pair * 128 : pair * 128 + 128])
            e = jnp.concatenate([e[:, :KEYS], e[:, KEYS:]], axis=0)
            tall = jnp.concatenate([ds[:, :KEYS], ds[:, KEYS:]], axis=0)
            results.append((dot(ds, key), dot(tall, query, TN), dot(e, sdm, TN)))
        for (pair, cloud), (dq, dk, dv) in zip(group, results):
            base = cloud * STEP
            parts = (dq * 0.125, dk[:WIN] * (1.0 / LOG2E), dv[:WIN])
            for which, part in enumerate(parts):
                cols = slice(which * D + pair * 128, which * D + pair * 128 + 128)
                head = part[:16]
                if cloud:
                    head = jnp.where(row_range(16, 0, 2 * cloud), tails[pair, which], head)
                dqkv[base : base + 16, cols] = head.astype(bf16)
                dqkv[base + 16 : base + 64, cols] = part[16:64].astype(bf16)
                tails[pair, which] = part[64:80]
                if cloud == TILE - 1:
                    dqkv[ROWS - 16 :, cols] = part[64:80].astype(bf16)


    back = dot(dqkv[...], joint_w[...], NT)
    joint_g[...] += dot(normed, dqkv[...], TN)
    tilted = back * vec[2:3, :]
    grad = mid_grad[...] + scale * (tilted - row_mean(tilted) - unit * row_mean(tilted * unit))
    low = grad.astype(bf16)
    mass = cdf(pre)
    place_low = (pre * mass).astype(bf16)
    pre_grad = dot(low, proj[...], NT) * smooth_slope(pre, mass)
    proj_g[...] += dot(place_low, low, TN)
    hidden = hidden_column(targets[0], ROWS)
    marked = jnp.where(hidden > 0.5, grad, 0.0)
    tokens_g[...] = (grad - marked).astype(bf16)
    high_part = pre_grad.astype(bf16)
    low_part = (pre_grad - high_part.astype(f32)).astype(bf16)
    place_g[...] += dot(cen[0], jnp.concatenate([high_part, low_part], axis=1))
    vec_g[0:1, :] += jnp.sum(marked, axis=0, keepdims=True)
    vec_g[1:2, :] += jnp.sum(grad, axis=0, keepdims=True)
    vec_g[2:3, :] += jnp.sum(back * unit, axis=0, keepdims=True)
    vec_g[3:4, :] += jnp.sum(back, axis=0, keepdims=True)
    if not is_last:
        return

    @pl.when(step == pl.num_programs(0) - 1)
    def _():
        for part in range(3):
            write_sums(sums, order, part * D, joint_g[:, part * D : part * D + D])
        write_sums(sums, order, 3 * D, proj_g[...])
        place = place_g[:, :POSH] + place_g[:, POSH:]
        place_weight = place[0:3] + place_g[3:6, :POSH]
        small = jnp.concatenate(
            [
                vec_g[0:4, :],
                mid_vec_g[0:4, :],
                jnp.concatenate([place_weight[0:1], place_weight[1:2], place_weight[2:3]], axis=1),
                jnp.concatenate([place[9:10], jnp.zeros((1, D - POSH), f32)], axis=1),
                jnp.concatenate([up_bg[:, part * D : part * D + D] for part in range(4)], axis=0),
                jnp.zeros((sums.shape[0] - 3 * D - POSH - 14, D), f32),
            ],
            axis=0,
        )
        write_sums(sums, order, 3 * D + POSH, small)
        share_halves(core[0], sums, kept, sent)


def back_part(given, first, steps, order, before=None, extra=None):
    count = given[0].shape[0]

    def shifted(width):
        return pl.BlockSpec((ROWS, width), lambda i: (i + first, 0))

    def shifted_slab(shape):
        return pl.BlockSpec((1, *shape), lambda i: (i + first, 0, 0))

    accs = [(D, 3 * D), (POSH, D), (16, 256), (8, D)]
    in_specs = [
        shifted(D), shifted(3 * D), shifted(D),
        pl.BlockSpec((TILE, WIN, HEADS * KEYS), lambda i: (i + first, 0, 0)),
        shifted(D), shifted(D), shifted_slab((16, ROWS)), shifted_slab((1, 256)),
        whole((8, D)), whole((16, POSH)), whole((POSH, D)), whole((D, 3 * D)),
    ]
    given = list(given)
    if before is not None:
        given += before
        in_specs += [pl.BlockSpec(memory_space=pl.ANY)] + [whole(acc) for acc in accs]
    out_specs, out_shape = [shifted(D)], [shape_of((count, D), bf16)]
    scratch = [pltpu.VMEM((ROWS + 48, 3 * D), bf16), pltpu.VMEM((ROWS, 3 * D), bf16)]
    if extra is not None:
        given += extra
        in_specs += [pl.BlockSpec(memory_space=pltpu.SMEM), whole((1, FF)), whole((8, D))]
        size = padded(3 * D + POSH + 16, len(order))
        out_specs += [whole((size // 2, D))] * 2
        out_shape += [shape_of((size // 2, D), bf16)] * 2
        scratch = [pltpu.VMEM(acc, f32) for acc in accs] + scratch + [pltpu.VMEM((size, D), bf16)]
    else:
        out_specs += [whole(acc) for acc in accs]
        out_shape += [shape_of(acc, f32) for acc in accs]
    return pl.pallas_call(
        functools.partial(back_kernel, before is None, extra is not None, order),
        grid=(steps,),
        in_specs=in_specs,
        out_specs=out_specs,
        out_shape=out_shape,
        scratch_shapes=scratch,
        input_output_aliases={} if before is None else {12: 0},
        compiler_params=settings(),
        cost_estimate=cost(5 * steps),
        name="back",
    )(*given)


def marked_targets(mask_count, mask_index):
    clouds, most = mask_index.shape
    slot = jnp.arange(most, dtype=jnp.int32)[None, :]
    cloud = (jnp.arange(clouds, dtype=jnp.int32) % TILE)[:, None]
    targets = jnp.where(slot < mask_count[:, None], mask_index + (1 + SEQ * cloud), -1)
    return jnp.pad(targets, ((0, 0), (0, 32 - most)), constant_values=-1).reshape(clouds // TILE, 1, 256)


def gather_pieces(spot, offsets, pieces, sums):
    segment = pieces[0].shape[0]
    chips = len(pieces) // 2
    for offset, piece in zip(offsets, pieces):
        holder = spot ^ offset
        row = pl.multiple_of(((holder % 2) * chips + holder // 2) * segment, 16)
        sums[pl.ds(row, segment), :] = piece[...]


def close_kernel(offsets, spot, *refs):
    pieces, refs = refs[: len(offsets)], refs[len(offsets) :]
    joint_g, proj_g, place_g, small, sums = refs[0], refs[1], refs[2], refs[3:-1], refs[-1]
    gather_pieces(spot[0], offsets, pieces, sums)
    for part in range(3):
        joint_g[:, part * D : part * D + D] = sums[part * D : part * D + D, :].astype(f32)
    proj_g[...] = sums[3 * D : 3 * D + POSH, :].astype(f32)
    rows = sums[3 * D + POSH : 3 * D + POSH + 16, :].astype(f32)
    for part in range(3):
        place_g[part : part + 1, :] = rows[8:9, part * POSH : part * POSH + POSH]
    small[0][...] = rows[9:10, :POSH].reshape(POSH)
    small[1][...] = jnp.concatenate([rows[10 + part : 11 + part] for part in range(4)], axis=1).reshape(FF)
    for at in range(8):
        small[2 + at][...] = rows[at : at + 1].reshape(D)


def widen_kernel(offsets, spot, *refs):
    pieces, refs = refs[: len(offsets)], refs[len(offsets) :]
    up_g, down_g, out_g, sums = refs
    gather_pieces(spot[0], offsets, pieces, sums)
    for part in range(4):
        up_g[:, part * D : part * D + D] = sums[part * D : part * D + D, :].astype(f32)
    down_g[...] = sums[4 * D : 8 * D, :].astype(f32)
    out_g[...] = sums[8 * D : 9 * D, :].astype(f32)


def unpacked(kernel, name, shapes, spot, offsets, pieces):
    vmem = pl.BlockSpec(memory_space=pltpu.VMEM)
    return pl.pallas_call(
        functools.partial(kernel, offsets),
        in_specs=[pl.BlockSpec(memory_space=pltpu.SMEM)] + [vmem] * len(pieces),
        out_specs=[vmem] * len(shapes),
        out_shape=[shape_of(shape, f32) for shape in shapes],
        scratch_shapes=[pltpu.VMEM((pieces[0].shape[0] * len(pieces), D), bf16)],
        compiler_params=settings(),
        cost_estimate=cost(4),
        name=name,
    )(spot, *pieces)


CALLS = 1


def bits_of(size):
    return [1 << bit for bit in range(size.bit_length() - 1)]


def chip_bits(size):
    bits = bits_of(size)[:0:-1]
    return [bits[at : at + 2] for at in range(0, len(bits), 2)]


def offsets_of(bits):
    found = [0]
    for bit in reversed(bits):
        found += [offset + bit for offset in found]
    return found


def swapped(values, offset, size):
    return lax.ppermute(values, "dp", [(i, i ^ offset) for i in range(size)])


def total(terms):
    return sum(term.astype(f32) for term in terms).astype(bf16)


def scattered(terms, bits, size):
    offsets = offsets_of(bits)
    mine = (lax.axis_index("dp") // bits[-1]) % len(offsets)
    parts = [term.reshape(len(offsets), -1, D) for term in terms]

    def part(offset):
        return [lax.dynamic_index_in_dim(term, mine ^ (offset // bits[-1]), 0, keepdims=False) for term in parts]

    return part(0) + [swapped(total(part(offset)), offset, size) for offset in offsets[1:]]


def joined(pieces, bits, size):
    found = dict(pieces)
    for offset in offsets_of(bits)[1:]:
        for held, piece in pieces.items():
            found[held ^ offset] = swapped(piece, offset, size)
    return found


def across(terms, bit, size):
    value = total(terms)
    return [value, lax.ppermute(value, "fsdp", [(i, i ^ bit) for i in range(size)])]


def tied(first, second):
    return lax.optimization_barrier((first, second))


def per_device(
    sizes,
    tokens,
    centers,
    mask_count,
    mask_index,
    mask_embed,
    place_weight,
    place_bias,
    place_proj,
    place_shift,
    norm_gain,
    norm_shift,
    joint_weight,
    out_weight,
    out_bias,
    mlp_gain,
    mlp_shift,
    up_weight,
    up_bias,
    down_weight,
    down_bias,
    cotangent,
):
    dp, fsdp = sizes["dp"], sizes["fsdp"]
    spot = lax.axis_index("dp").astype(jnp.int32)[None]
    core = spot % 2
    vectors = (mask_embed, place_shift, norm_gain, norm_shift, out_bias, mlp_gain, mlp_shift, down_bias)
    packed, vec = pack(spot, place_proj, joint_weight, out_weight, up_weight, down_weight, vectors, dp)
    packed = lax.all_gather(packed, "fsdp", axis=0)
    packed_other = swapped(packed, 1, dp)
    half = (3 * joint_weight.shape[0] + place_proj.shape[0]) // 2
    late = packed[:, half:]
    near = [swapped(late, 2 * offset, dp) for offset in range(1, dp // 2)]
    targets = marked_targets(mask_count, mask_index)
    up_b = up_bias[None, :]
    entry, joint, mixture, shares, weights, joint_w, proj, cen, place_w = front(
        core, tokens, centers, targets, vec, place_weight, place_bias[None, :], packed, packed_other
    )
    near, mixture = tied(near, mixture)
    near_other = [swapped(piece, 1, dp) for piece in near]
    order = list(range(dp))
    output, mid_grad, mix_grad, kept, sent, up_bg, vec_g = middle_part(
        spot, entry, mixture, shares, cotangent, vec, up_b, packed, packed_other, near, near_other, order
    )
    chips = chip_bits(dp)
    stages = [functools.partial(scattered, bits=bits, size=dp) for bits in chips]
    stages += [functools.partial(across, bit=bit, size=fsdp) for bit in bits_of(fsdp)]
    steps = tokens.shape[0] // ROWS
    parts = [steps * (part + 1) // CALLS - steps * part // CALLS for part in range(CALLS)]
    before, first = None, 0
    sums = [kept, swapped(sent, 1, dp)]
    for part, count in enumerate(parts):
        mix_grad, sums[-1] = tied(mix_grad, sums[-1])
        sums = stages[part](sums)
        given = (entry, joint, mixture, weights, mix_grad, mid_grad, cen, targets, vec, place_w, proj, joint_w)
        extra = [core, up_bg, vec_g] if part == CALLS - 1 else None
        before = back_part(given, first, count, order, before, extra)
        first += count
    tokens_grad, kept, sent = before
    rest = stages[CALLS:]
    sent, sums[-1] = tied(sent, sums[-1])
    sums = rest[0](sums)
    last = [kept, swapped(sent, 1, dp)]
    sums[-1], last[-1] = tied(sums[-1], last[-1])
    for at, stage in enumerate(rest[1:]):
        sums = stage(sums)
        last = stages[at](last)
        sums[-1], last[-1] = tied(sums[-1], last[-1])
    sums = {0: total(sums)}
    for bits in reversed(chips):
        sums = joined(sums, bits, dp)
    for stage in stages[len(rest) - 1 :]:
        last = stage(last)
    last = {0: total(last)}
    for bits in reversed(chips):
        last = joined(last, bits, dp)
    sums, last = joined(sums, [1], dp), joined(last, [1], dp)
    up_grad, down_grad, out_grad = unpacked(
        widen_kernel, "widen", [(D, FF), (FF, D), (D, D)], spot, list(sums), list(sums.values())
    )
    joint_grad, proj_grad, place_weight_grad, place_bias_grad, up_bias_grad, *small = unpacked(
        close_kernel,
        "close",
        [(D, 3 * D), (POSH, D), (3, POSH), (POSH,), (FF,)] + [(D,)] * 8,
        spot,
        list(last),
        list(last.values()),
    )
    return (
        output,
        tokens_grad,
        small[0],
        place_weight_grad,
        place_bias_grad,
        proj_grad,
        small[1],
        small[2],
        small[3],
        joint_grad,
        out_grad,
        small[6],
        small[4],
        small[5],
        up_grad,
        up_bias_grad,
        down_grad,
        small[7],
    )


def solution(mesh):
    rows = P(("dp", "fsdp"), None)
    in_specs = (
        rows,
        P(None, ("dp", "fsdp")),
        P(("dp", "fsdp")),
        rows,
        P(),
        P(),
        P(),
        P("fsdp", None),
        P(),
        P(),
        P(),
        P("fsdp", None),
        P("fsdp", None),
        P(),
        P(),
        P(),
        P("fsdp", None),
        P(),
        P("fsdp", None),
        P(),
        rows,
    )
    out_specs = (rows, rows) + (P(),) * 16
    return jax.shard_map(
        functools.partial(per_device, dict(mesh.shape)), mesh=mesh, in_specs=in_specs, out_specs=out_specs, check_vma=False
    )
```

```python
import functools

import jax
import jax.numpy as jnp
from jax import lax
from jax.experimental import pallas as pl
from jax.experimental.pallas import tpu as pltpu
from jax.sharding import PartitionSpec as P

D = 384
HEADS = 6
FF = 1536
POSH = 128
SEQ = 66
TILE = 8
ROWS = TILE * SEQ
STEP = 64
WIN = 80
KEYS = 128
PAIRS = HEADS // 2
GROUP = 8
BACK_GROUP = 24
SUBS = 2
VMEM = 60 * 2**20
LOG2E = 1.4426950408889634
ROOT_HALF = 0.7071067811865476
PDF = 0.3989422804014327
bf16 = jnp.bfloat16
f32 = jnp.float32

NN = (((1,), (0,)), ((), ()))
NT = (((1,), (1,)), ((), ()))
TN = (((0,), (0,)), ((), ()))


def dot(left, right, dims=NN):
    return lax.dot_general(left, right, dims, preferred_element_type=f32)


def cdf(u):
    return 0.5 + 0.5 * lax.erf(u * ROOT_HALF)


def smooth_slope(u, mass):
    return mass + u * (PDF * jnp.exp2(u * u * (-0.5 * LOG2E)))


def row_mean(values):
    return jnp.sum(values, axis=-1, keepdims=True) * (1.0 / values.shape[-1])


def normalised(values):
    centred = values - row_mean(values)
    scale = lax.rsqrt(row_mean(centred * centred) + 1e-05)
    return centred * scale, scale


def hidden_column(targets, rows):
    row_ids = lax.broadcasted_iota(jnp.int32, (rows, targets.shape[1]), 0)
    hits = jnp.where(row_ids == targets, 1.0, 0.0)
    return jnp.max(hits, axis=1, keepdims=True)


def lane_mask(rows, odd, kind=bf16):
    lanes = lax.broadcasted_iota(jnp.int32, (rows, 128), 1)
    return (lanes >= 64) if odd else (lanes < 64)


def stacked_heads(tile):
    zero = jnp.zeros_like(tile)
    even = lane_mask(tile.shape[0], False)
    return jnp.concatenate([jnp.where(even, tile, zero), jnp.where(even, zero, tile)], axis=0)


def merged_heads(pair):
    half = pair.shape[0] // 2
    even = lane_mask(half, False)
    return jnp.where(even, pair[:half], pair[half:])


def row_range(rows, low, high, width=128):
    ids = lax.broadcasted_iota(jnp.int32, (rows, width), 0)
    return (ids >= low) & (ids < high)


def spread_heads(flipped):
    none = jnp.zeros((64, flipped.shape[1]), flipped.dtype)
    left = jnp.concatenate([flipped[:64], none], axis=0)
    right = jnp.concatenate([none, flipped[64:]], axis=0)
    return jnp.concatenate([left, right], axis=1)


def head_ones(value):
    rows = lax.broadcasted_iota(jnp.int32, (2 * KEYS, 128), 0) < KEYS
    lanes = lax.broadcasted_iota(jnp.int32, (2 * KEYS, 128), 1) < 64
    return jnp.where(rows == lanes, value, 0.0).astype(bf16)


def lane_ones(value):
    rows = lax.broadcasted_iota(jnp.int32, (128, 2 * KEYS), 0) < 64
    lanes = lax.broadcasted_iota(jnp.int32, (128, 2 * KEYS), 1) < KEYS
    return jnp.where(rows == lanes, value, 0.0).astype(bf16)


def pack_kernel(spot, proj, joint, out, up, down, *refs):
    vectors, (packed, vec, early, late) = refs[:8], refs[8:]
    for at, vector in enumerate(vectors):
        vec[at : at + 1, :] = vector[...].reshape(1, D)
    rows = joint.shape[0]
    for part in range(3):
        early[part * rows : part * rows + rows, :] = joint[:, part * D : part * D + D]
    early[3 * rows :, :] = proj[...]
    late[:rows, :] = out[...]
    for part in range(4):
        late[(part + 1) * rows : (part + 2) * rows, :] = up[:, part * D : part * D + D]
    late[5 * rows : 5 * rows + down.shape[0], :] = down[...]
    half = early.shape[0] // 2
    piece = packed.shape[0] - half
    packed[:half, :] = early[pl.ds(pl.multiple_of((spot[0] % 2) * half, 16), half), :]
    chips = late.shape[0] // piece // 2
    own = (spot[0] % 2) * chips + spot[0] // 2
    packed[half:, :] = late[pl.ds(pl.multiple_of(own * piece, 16), piece), :]


def pack(spot, proj, joint, out, up, down, vectors, parts):
    rows, low, deep = joint.shape[0], proj.shape[0], down.shape[0]
    size = 3 * rows + low
    late = padded(5 * rows + deep, parts)
    vmem = pl.BlockSpec(memory_space=pltpu.VMEM)
    return pl.pallas_call(
        pack_kernel,
        in_specs=[pl.BlockSpec(memory_space=pltpu.SMEM)] + [vmem] * 13,
        out_specs=[vmem, vmem],
        out_shape=[shape_of((size // 2 + late // parts, D), bf16), shape_of((8, D), f32)],
        scratch_shapes=[pltpu.VMEM((size, D), bf16), pltpu.VMEM((late, D), bf16)],
        compiler_params=settings(),
        name="pack",
    )(spot, proj, joint, out, up, down, *vectors)


def unpack_early(core, mine, other, joint_w, proj):
    groups = mine.shape[0]
    rows, low = D // groups, POSH // groups
    half = (3 * rows + low) // 2

    def place(side, source):
        for group in range(groups):
            at = 0
            while at < half:
                row = side * half + at
                if row < 3 * rows:
                    part, inner = divmod(row, rows)
                    size = min(half - at, rows - inner)
                    first = group * rows + inner
                    joint_w[first : first + size, part * D : part * D + D] = source[group, at : at + size]
                else:
                    size = half - at
                    first = group * low + row - 3 * rows
                    proj[first : first + size, :] = source[group, at : at + size]
                at += size

    @pl.when(core == 0)
    def _():
        place(0, mine)
        place(1, other)

    @pl.when(core == 1)
    def _():
        place(0, other)
        place(1, mine)


def unpack_late(spot, mine, other, near, near_other, lates, out_w, up_w, down_w):
    _, chips, groups, piece, _ = lates.shape
    rows, deep = D // groups, FF // groups
    half = mine.shape[1] - piece
    core, chip = spot % 2, spot // 2
    for side, own, rest in ((core, mine, near), (1 - core, other, near_other)):
        lates[side, chip] = own[:, half:, :]
        for offset, source in enumerate(rest):
            lates[side, chip ^ (offset + 1)] = source[...]
    for at_chip in range(2 * chips):
        for group in range(groups):
            at = 0
            while at < piece:
                row = at_chip * piece + at
                source = lates.at[at_chip // chips, at_chip % chips, group]
                if row < rows:
                    size = min(piece - at, rows - row)
                    first = group * rows + row
                    out_w[first : first + size, :] = source[at : at + size, :]
                elif row < 5 * rows:
                    block, inner = divmod(row - rows, rows)
                    size = min(piece - at, rows - inner)
                    first = group * rows + inner
                    up_w[first : first + size, block * D : block * D + D] = source[at : at + size, :]
                elif row < 5 * rows + deep:
                    inner = row - 5 * rows
                    size = min(piece - at, deep - inner)
                    first = group * deep + inner
                    down_w[first : first + size, :] = source[at : at + size, :]
                else:
                    size = piece - at
                at += size


def picked(rows, first, source):
    ids = lax.broadcasted_iota(jnp.int32, (16, rows), 0) - lax.broadcasted_iota(jnp.int32, (16, rows), 1)
    return dot(jnp.where(ids == first, 1.0, 0.0).astype(bf16), source)


def split16(values):
    high = values.astype(bf16)
    return high, (values - high.astype(f32)).astype(bf16)


def place_inputs(centers, place_weight, place_bias, cen, place_w):
    for tile in range(cen.shape[0]):
        high, rest = split16(centers[:, tile * ROWS : tile * ROWS + ROWS])
        ids = lax.broadcasted_iota(jnp.int32, (16, ROWS), 0)
        ones = jnp.where((ids == 9) | (ids == 10), 1.0, 0.0)
        cen[tile] = (picked(3, 0, high) + picked(3, 3, rest) + picked(3, 6, high) + ones).astype(bf16)
    high, rest = split16(place_weight[...])
    bias_high, bias_rest = split16(place_bias[...])
    value = picked(3, 0, high) + picked(3, 3, high) + picked(3, 6, rest) + picked(1, 9, bias_high) + picked(1, 10, bias_rest)
    place_w[...] = value.astype(bf16)


def front_kernel(core, tokens, centers, targets, vec, place_weight, place_bias, mine, other,
                 entry, joint, mixture, shares, weights, joint_w, proj, cen, place_w, qkv):
    step = pl.program_id(0)

    @pl.when(step == 0)
    def _():
        for sub in range(SUBS):
            qkv[sub, ROWS:, :] = jnp.zeros((qkv.shape[1] - ROWS, 3 * D), bf16)
        unpack_early(core[0], mine, other, joint_w, proj)
        place_inputs(centers, place_weight, place_bias, cen, place_w)

    lanes = lax.broadcasted_iota(jnp.int32, (1, 2 * KEYS), 1) % KEYS
    sums_of = head_ones(1.0)
    none = jnp.zeros((16, 2 * KEYS), bf16)
    scale_row = jnp.where(lax.broadcasted_iota(jnp.int32, (1, 3 * D), 1) < D, 0.125 * LOG2E, 1.0)

    def normal_rows(sub):
        span = slice(sub * ROWS, sub * ROWS + ROWS)
        pre = dot(cen[step * SUBS + sub], place_w[...], TN)
        low = (pre * cdf(pre)).astype(bf16)
        placed = dot(low, proj[...]) + vec[1:2, :]
        hidden = hidden_column(targets[sub], ROWS)
        rows = jnp.where(hidden > 0.5, vec[0:1, :], tokens[span, :].astype(f32)) + placed
        entry[span, :] = rows
        unit, _ = normalised(rows)
        return (unit * vec[2:3, :] + vec[3:4, :]).astype(bf16)

    def project(sub, normed, first):
        cols = slice(first, min(first + 256, 3 * D))
        value = (dot(normed, joint_w[:, cols]) * scale_row[:, cols]).astype(bf16)
        qkv[sub, :ROWS, cols] = value
        joint[sub * ROWS : sub * ROWS + ROWS, cols] = value

    def score(sub, pair, cloud):
        base = cloud * STEP
        query = qkv[sub, base : base + WIN, pair * 128 : pair * 128 + 128]
        key = qkv[sub, base : base + KEYS, D + pair * 128 : D + pair * 128 + 128]
        return dot(query, spread_heads(key.T))

    def exponentials(cloud, scores):
        live = (lanes >= 2 * cloud) & (lanes < 2 * cloud + SEQ - 1)
        scores = jnp.where(live, scores, -1e30)
        parts = []
        for half in (scores[:, :KEYS], scores[:, KEYS:]):
            parts.append(jnp.exp2(half - jnp.max(half, axis=-1, keepdims=True)).astype(bf16))
        return jnp.concatenate(parts, axis=1)

    def mixed(sub, pair, cloud, e):
        base = cloud * STEP
        value = qkv[sub, base : base + KEYS, 2 * D + pair * 128 : 2 * D + pair * 128 + 128]
        return dot(e, jnp.concatenate([stacked_heads(value), sums_of], axis=1))

    tails = {}

    def store(sub, pair, cloud, e, both):
        base = sub * ROWS + cloud * STEP
        cols = slice(pair * 128, pair * 128 + 128)
        share = 1.0 / both[:, 128:]
        mix = both[:, :128] * share
        spot = slice(pair * 256, pair * 256 + 256)
        at = sub * TILE + cloud
        weights[at, :16, spot] = jnp.where(row_range(16, 2 * cloud, 16, 256), e[:16], none)
        weights[at, 16:64, spot] = e[16:64]
        weights[at, 64:80, spot] = jnp.where(row_range(16, 0, 2 * cloud + 2, 256), e[64:80], none)
        head_mix, head_share = mix[:16], share[:16]
        if cloud:
            head = row_range(16, 0, 2 * cloud)
            tail_mix, tail_share = tails[sub, pair]
            head_mix = jnp.where(head, tail_mix, head_mix)
            head_share = jnp.where(head, tail_share, head_share)
        mixture[base : base + 16, cols] = head_mix.astype(bf16)
        shares[base : base + 16, cols] = head_share.astype(bf16)
        mixture[base + 16 : base + 64, cols] = mix[16:64].astype(bf16)
        shares[base + 16 : base + 64, cols] = share[16:64].astype(bf16)
        tails[sub, pair] = (mix[64:], share[64:])
        if cloud == TILE - 1:
            mixture[base + 64 : base + 80, cols] = mix[64:].astype(bf16)
            shares[base + 64 : base + 80, cols] = share[64:].astype(bf16)

    jobs = [(pair, cloud) for pair in range(PAIRS) for cloud in range(TILE)]
    groups = [jobs[at : at + GROUP] for at in range(0, len(jobs), GROUP)]
    normed = [normal_rows(sub) for sub in range(SUBS)]
    chunks = range(0, 3 * D, 256)
    for first in chunks:
        project(0, normed[0], first)
    waiting = None
    for sub in range(SUBS):
        fill = [functools.partial(project, sub + 1, normed[sub + 1], first) for first in chunks] if sub + 1 < SUBS else []
        share_of = -(-len(fill) // len(groups))
        for group in groups:
            exps = [exponentials(cloud, score(sub, pair, cloud)) for pair, cloud in group]
            for task in fill[:share_of]:
                task()
            fill = fill[share_of:]
            if waiting:
                close_group(mixed, store, *waiting)
            waiting = (sub, group, exps)
    close_group(mixed, store, *waiting)


def close_group(mixed, store, sub, group, exps):
    boths = [mixed(sub, pair, cloud, e) for (pair, cloud), e in zip(group, exps)]
    for (pair, cloud), e, both in zip(group, exps, boths):
        store(sub, pair, cloud, e, both)


def whole(shape):
    return pl.BlockSpec(shape, lambda i: (0,) * len(shape))


def rows_of(width, rows=ROWS):
    return pl.BlockSpec((rows, width), lambda i: (i, 0))


def slab(shape):
    return pl.BlockSpec((1, *shape), lambda i: (i,) + (0,) * len(shape))


def shape_of(dims, kind):
    return jax.ShapeDtypeStruct(dims, kind)


def cost(microseconds):
    return pl.CostEstimate(flops=int(microseconds * 9e8), bytes_accessed=int(microseconds * 2e6), transcendentals=0)


def settings():
    return pltpu.CompilerParams(vmem_limit_bytes=VMEM)


def front(core, tokens, centers, targets, vec, place_weight, place_bias, mine, other):
    count = tokens.shape[0]
    steps = count // ROWS
    rows = SUBS * ROWS
    return pl.pallas_call(
        front_kernel,
        grid=(steps // SUBS,),
        in_specs=[
            pl.BlockSpec(memory_space=pltpu.SMEM), rows_of(D, rows), whole(centers.shape),
            pl.BlockSpec((SUBS, 1, 256), lambda i: (i, 0, 0)), whole((8, D)),
            whole((3, POSH)), whole((1, POSH)), whole(mine.shape), whole(other.shape),
        ],
        out_specs=[
            rows_of(D, rows), rows_of(3 * D, rows), rows_of(D, rows), rows_of(D, rows),
            pl.BlockSpec((SUBS * TILE, WIN, HEADS * KEYS), lambda i: (i, 0, 0)), whole((D, 3 * D)), whole((POSH, D)),
            whole((steps, 16, ROWS)), whole((16, POSH)),
        ],
        out_shape=[
            shape_of((count, D), f32), shape_of((count, 3 * D), bf16),
            shape_of((count, D), bf16), shape_of((count, D), bf16),
            shape_of((steps * TILE, WIN, HEADS * KEYS), bf16), shape_of((D, 3 * D), bf16), shape_of((POSH, D), bf16),
            shape_of((steps, 16, ROWS), bf16), shape_of((16, POSH), bf16),
        ],
        scratch_shapes=[pltpu.VMEM((SUBS, ROWS + 48, 3 * D), bf16)],
        compiler_params=settings(),
        cost_estimate=cost(28),
        name="front",
    )(core, tokens, centers, targets, vec, place_weight, place_bias, mine, other)


def write_sums(sums, order, first, values):
    size = sums.shape[0] // len(order)
    at = 0
    while at < values.shape[0]:
        row = first + at
        segment, inner = divmod(row, size)
        step = min(size - inner, values.shape[0] - at)
        spot = order[segment] * size + inner
        sums[spot : spot + step, :] = values[at : at + step].astype(bf16)
        at += step


def share_halves(core, sums, kept, sent):
    half = sent.shape[0]
    kept[...] = sums[pl.ds(pl.multiple_of(core * half, 16), half), :]
    sent[...] = sums[pl.ds(pl.multiple_of((1 - core) * half, 16), half), :]


def padded(rows, size):
    return -(-rows // (16 * size)) * 16 * size


def middle_kernel(chunk, order, spot, entry, mixture, shares, cot, vec, up_b, mine, other, *refs):
    chips = len(order) // 2
    near, near_other, refs = refs[: chips - 1], refs[chips - 1 : 2 * chips - 2], refs[2 * chips - 2 :]
    (output, mid_grad, mix_grad, kept, sent, up_bg, vec_g,
     down_acc, up_acc, out_acc, out_w, up_w, down_w, gated, sums, lates) = refs
    step = pl.program_id(0)

    @pl.when(step == 0)
    def _():
        unpack_late(spot[0], mine, other, near, near_other, lates, out_w, up_w, down_w)
        for ref in (down_acc, up_acc, out_acc, up_bg, vec_g):
            ref[...] = jnp.zeros(ref.shape, ref.dtype)

    parts = FF // chunk
    spans = [slice(part * chunk, part * chunk + chunk) for part in range(parts)]
    mix = mixture[...]
    cotangent = cot[...]
    mid = entry[...] + (dot(mix, out_w[...]) + vec[4:5, :])
    gates = [dot(cotangent, down_w[spans[0], :], NT)]
    unit, scale = normalised(mid)
    normed = (unit * vec[5:6, :] + vec[6:7, :]).astype(bf16)
    lows = []

    def down_part(part):
        down_acc[:, spans[part]] += dot(cotangent, gated[:, spans[part]], TN)

    def up_part(part):
        up_acc[:, spans[part]] += dot(normed, lows[part], TN)

    for part in range(parts):
        cols = spans[part]
        raised = dot(normed, up_w[:, cols]) + up_b[:, cols]
        if part + 1 < parts:
            gates.append(dot(cotangent, down_w[spans[part + 1], :], NT))
        mass = cdf(raised)
        gated[:, cols] = (raised * mass).astype(bf16)
        grad = gates[part] * smooth_slope(raised, mass)
        up_bg[:, cols] += jnp.sum(grad, axis=0, keepdims=True)
        lows.append(grad.astype(bf16))
        if part:
            down_part(part - 1)
            if part > 1:
                up_part(part - 2)
    back = dot(jnp.concatenate(lows, axis=1), up_w[...], NT)
    up_part(parts - 2)
    down_part(parts - 1)
    up_part(parts - 1)
    output[...] = (mid + (dot(gated[...], down_w[...]) + vec[7:8, :])).astype(bf16)
    upstream = cotangent.astype(f32)
    tilted = back * vec[5:6, :]
    grad = upstream + scale * (tilted - row_mean(tilted) - unit * row_mean(tilted * unit))
    mid_grad[...] = grad
    low = grad.astype(bf16)
    mix_grad[...] = (dot(low, out_w[...], NT) * shares[...].astype(f32)).astype(bf16)
    out_acc[...] += dot(mix, low, TN)
    vec_g[0:1, :] += jnp.sum(back * unit, axis=0, keepdims=True)
    vec_g[1:2, :] += jnp.sum(back, axis=0, keepdims=True)
    vec_g[2:3, :] += jnp.sum(grad, axis=0, keepdims=True)
    vec_g[3:4, :] += jnp.sum(upstream, axis=0, keepdims=True)

    @pl.when(step == pl.num_programs(0) - 1)
    def _():
        for part in range(4):
            write_sums(sums, order, part * D, up_acc[:, part * D : part * D + D])
        write_sums(sums, order, 4 * D, down_acc[...].T)
        write_sums(sums, order, 8 * D, out_acc[...])
        if sums.shape[0] > 9 * D:
            write_sums(sums, order, 9 * D, jnp.zeros((sums.shape[0] - 9 * D, D), f32))
        share_halves(spot[0] % 2, sums, kept, sent)


def middle_part(spot, entry, mixture, shares, cot, vec, up_b, mine, other, near, near_other, order, rows=1056, chunk=512):
    count = entry.shape[0]
    size = padded(9 * D, len(order))
    return pl.pallas_call(
        functools.partial(middle_kernel, chunk, order),
        grid=(count // rows,),
        in_specs=[
            pl.BlockSpec(memory_space=pltpu.SMEM), rows_of(D, rows), rows_of(D, rows), rows_of(D, rows), rows_of(D, rows),
            whole((8, D)), whole((1, FF)), whole(mine.shape), whole(other.shape),
        ]
        + [whole(piece.shape) for piece in [*near, *near_other]],
        out_specs=[
            rows_of(D, rows), rows_of(D, rows), rows_of(D, rows),
            whole((size // 2, D)), whole((size // 2, D)), whole((1, FF)), whole((8, D)),
        ],
        out_shape=[
            shape_of((count, D), bf16), shape_of((count, D), f32), shape_of((count, D), bf16),
            shape_of((size // 2, D), bf16), shape_of((size // 2, D), bf16), shape_of((1, FF), f32), shape_of((8, D), f32),
        ],
        scratch_shapes=[
            pltpu.VMEM((D, FF), f32), pltpu.VMEM((D, FF), f32), pltpu.VMEM((D, D), f32),
            pltpu.VMEM((D, D), bf16), pltpu.VMEM((D, FF), bf16), pltpu.VMEM((FF, D), bf16),
            pltpu.VMEM((rows, FF), bf16), pltpu.VMEM((size, D), bf16),
            pltpu.VMEM((2, len(order) // 2, *near[0].shape), bf16),
        ],
        compiler_params=settings(),
        cost_estimate=cost(55),
        name="middle",
    )(spot, entry, mixture, shares, cot, vec, up_b, mine, other, *near, *near_other)


def back_kernel(is_first, is_last, order, *refs):
    entry, joint, mixture, weights, mix_grad, mid_grad, cen, targets, vec, place_w, proj, joint_w = refs[:12]
    refs = refs[12:]
    if not is_first:
        before, refs = refs[1:5], refs[5:]
    if is_last:
        core, up_bg, mid_vec_g, tokens_g, kept, sent, joint_g, proj_g, place_g, vec_g, qkv, dqkv, sums = refs
    else:
        tokens_g, joint_g, proj_g, place_g, vec_g, qkv, dqkv = refs
    step = pl.program_id(0)

    @pl.when(step == 0)
    def _():
        for at, ref in enumerate((joint_g, proj_g, place_g, vec_g)):
            ref[...] = jnp.zeros(ref.shape, ref.dtype) if is_first else before[at][...]
        qkv[ROWS:, :] = jnp.zeros((qkv.shape[0] - ROWS, 3 * D), bf16)

    qkv[:ROWS, :] = joint[...]
    pre = dot(cen[0], place_w[...], TN)
    unit, scale = normalised(entry[...])
    normed = (unit * vec[2:3, :] + vec[3:4, :]).astype(bf16)
    minus = lane_ones(-1.0)
    jobs = [(pair, cloud) for pair in range(PAIRS) for cloud in range(TILE)]
    tails = {}
    for at in range(0, len(jobs), BACK_GROUP):
        group = jobs[at : at + BACK_GROUP]
        gaps = []
        for pair, cloud in group:
            base = cloud * STEP
            window = slice(base, base + WIN)
            cols = slice(pair * 128, pair * 128 + 128)
            value = qkv[base : base + KEYS, 2 * D + pair * 128 : 2 * D + pair * 128 + 128]
            dmw = mix_grad[window, cols]
            left = jnp.concatenate([dmw, dmw * mixture[window, cols]], axis=1)
            gaps.append(dot(left, jnp.concatenate([spread_heads(value.T), minus], axis=0)))
        es, dss = [], []
        for (pair, cloud), gap in zip(group, gaps):
            e = weights[cloud, :, pair * 256 : pair * 256 + 256]
            es.append(e)
            dss.append((e.astype(f32) * gap).astype(bf16))
        results = []
        for (pair, cloud), e, ds in zip(group, es, dss):
            base = cloud * STEP
            query = stacked_heads(qkv[base : base + WIN, pair * 128 : pair * 128 + 128])
            key = stacked_heads(qkv[base : base + KEYS, D + pair * 128 : D + pair * 128 + 128])
            sdm = stacked_heads(mix_grad[base : base + WIN, pair * 128 : pair * 128 + 128])
            e = jnp.concatenate([e[:, :KEYS], e[:, KEYS:]], axis=0)
            tall = jnp.concatenate([ds[:, :KEYS], ds[:, KEYS:]], axis=0)
            results.append((dot(ds, key), dot(tall[:, :WIN], query, TN), dot(e[:, :WIN], sdm, TN)))
        for (pair, cloud), (dq, dk, dv) in zip(group, results):
            base = cloud * STEP
            parts = (dq * 0.125, dk * (1.0 / LOG2E), dv)
            for which, part in enumerate(parts):
                cols = slice(which * D + pair * 128, which * D + pair * 128 + 128)
                head = part[:16]
                if cloud:
                    head = jnp.where(row_range(16, 0, 2 * cloud), tails[pair, which], head)
                dqkv[base : base + 16, cols] = head.astype(bf16)
                dqkv[base + 16 : base + 64, cols] = part[16:64].astype(bf16)
                tails[pair, which] = part[64:80]
                if cloud == TILE - 1:
                    dqkv[ROWS - 16 :, cols] = part[64:80].astype(bf16)


    back = dot(dqkv[...], joint_w[...], NT)
    joint_g[...] += dot(normed, dqkv[...], TN)
    tilted = back * vec[2:3, :]
    grad = mid_grad[...] + scale * (tilted - row_mean(tilted) - unit * row_mean(tilted * unit))
    low = grad.astype(bf16)
    mass = cdf(pre)
    place_low = (pre * mass).astype(bf16)
    pre_grad = dot(low, proj[...], NT) * smooth_slope(pre, mass)
    proj_g[...] += dot(place_low, low, TN)
    hidden = hidden_column(targets[0], ROWS)
    marked = jnp.where(hidden > 0.5, grad, 0.0)
    tokens_g[...] = (grad - marked).astype(bf16)
    high_part = pre_grad.astype(bf16)
    low_part = (pre_grad - high_part.astype(f32)).astype(bf16)
    place_g[...] += dot(cen[0], jnp.concatenate([high_part, low_part], axis=1))
    vec_g[0:1, :] += jnp.sum(marked, axis=0, keepdims=True)
    vec_g[1:2, :] += jnp.sum(grad, axis=0, keepdims=True)
    vec_g[2:3, :] += jnp.sum(back * unit, axis=0, keepdims=True)
    vec_g[3:4, :] += jnp.sum(back, axis=0, keepdims=True)
    if not is_last:
        return

    @pl.when(step == pl.num_programs(0) - 1)
    def _():
        for part in range(3):
            write_sums(sums, order, part * D, joint_g[:, part * D : part * D + D])
        write_sums(sums, order, 3 * D, proj_g[...])
        place = place_g[:, :POSH] + place_g[:, POSH:]
        place_weight = place[0:3] + place_g[3:6, :POSH]
        small = jnp.concatenate(
            [
                vec_g[0:4, :],
                mid_vec_g[0:4, :],
                jnp.concatenate([place_weight[0:1], place_weight[1:2], place_weight[2:3]], axis=1),
                jnp.concatenate([place[9:10], jnp.zeros((1, D - POSH), f32)], axis=1),
                jnp.concatenate([up_bg[:, part * D : part * D + D] for part in range(4)], axis=0),
                jnp.zeros((sums.shape[0] - 3 * D - POSH - 14, D), f32),
            ],
            axis=0,
        )
        write_sums(sums, order, 3 * D + POSH, small)
        share_halves(core[0], sums, kept, sent)


def back_part(given, first, steps, order, before=None, extra=None):
    count = given[0].shape[0]

    def shifted(width):
        return pl.BlockSpec((ROWS, width), lambda i: (i + first, 0))

    def shifted_slab(shape):
        return pl.BlockSpec((1, *shape), lambda i: (i + first, 0, 0))

    accs = [(D, 3 * D), (POSH, D), (16, 256), (8, D)]
    in_specs = [
        shifted(D), shifted(3 * D), shifted(D),
        pl.BlockSpec((TILE, WIN, HEADS * KEYS), lambda i: (i + first, 0, 0)),
        shifted(D), shifted(D), shifted_slab((16, ROWS)), shifted_slab((1, 256)),
        whole((8, D)), whole((16, POSH)), whole((POSH, D)), whole((D, 3 * D)),
    ]
    given = list(given)
    if before is not None:
        given += before
        in_specs += [pl.BlockSpec(memory_space=pl.ANY)] + [whole(acc) for acc in accs]
    out_specs, out_shape = [shifted(D)], [shape_of((count, D), bf16)]
    scratch = [pltpu.VMEM((ROWS + 48, 3 * D), bf16), pltpu.VMEM((ROWS, 3 * D), bf16)]
    if extra is not None:
        given += extra
        in_specs += [pl.BlockSpec(memory_space=pltpu.SMEM), whole((1, FF)), whole((8, D))]
        size = padded(3 * D + POSH + 16, len(order))
        out_specs += [whole((size // 2, D))] * 2
        out_shape += [shape_of((size // 2, D), bf16)] * 2
        scratch = [pltpu.VMEM(acc, f32) for acc in accs] + scratch + [pltpu.VMEM((size, D), bf16)]
    else:
        out_specs += [whole(acc) for acc in accs]
        out_shape += [shape_of(acc, f32) for acc in accs]
    return pl.pallas_call(
        functools.partial(back_kernel, before is None, extra is not None, order),
        grid=(steps,),
        in_specs=in_specs,
        out_specs=out_specs,
        out_shape=out_shape,
        scratch_shapes=scratch,
        input_output_aliases={} if before is None else {12: 0},
        compiler_params=settings(),
        cost_estimate=cost(5 * steps),
        name="back",
    )(*given)


def marked_targets(mask_count, mask_index):
    clouds, most = mask_index.shape
    slot = jnp.arange(most, dtype=jnp.int32)[None, :]
    cloud = (jnp.arange(clouds, dtype=jnp.int32) % TILE)[:, None]
    targets = jnp.where(slot < mask_count[:, None], mask_index + (1 + SEQ * cloud), -1)
    return jnp.pad(targets, ((0, 0), (0, 32 - most)), constant_values=-1).reshape(clouds // TILE, 1, 256)


def gather_pieces(spot, offsets, pieces, sums):
    segment = pieces[0].shape[0]
    chips = len(pieces) // 2
    for offset, piece in zip(offsets, pieces):
        holder = spot ^ offset
        row = pl.multiple_of(((holder % 2) * chips + holder // 2) * segment, 16)
        sums[pl.ds(row, segment), :] = piece[...]


def close_kernel(offsets, spot, *refs):
    count = len(offsets)
    first_pieces, last_pieces, refs = refs[:count], refs[count : 2 * count], refs[2 * count :]
    up_g, down_g, out_g, joint_g, proj_g, place_g, *small = refs[:-2]
    sums, last = refs[-2:]
    step = pl.program_id(0)

    @pl.when(step == 0)
    def _():
        gather_pieces(spot[0], offsets, first_pieces, sums)
        gather_pieces(spot[0], offsets, last_pieces, last)
        out_g[...] = sums[8 * D : 9 * D, :].astype(f32)
        proj_g[...] = last[3 * D : 3 * D + POSH, :].astype(f32)
        rows = last[3 * D + POSH : 3 * D + POSH + 16, :].astype(f32)
        for part in range(3):
            place_g[part : part + 1, :] = rows[8:9, part * POSH : part * POSH + POSH]
        small[0][...] = rows[9:10, :POSH].reshape(POSH)
        small[1][...] = jnp.concatenate([rows[10 + part : 11 + part] for part in range(4)], axis=1).reshape(FF)
        for at in range(8):
            small[2 + at][...] = rows[at : at + 1].reshape(D)

    up_g[...] = sums[pl.ds(pl.multiple_of(step * D, 16), D), :].astype(f32)
    down_g[...] = sums[pl.ds(pl.multiple_of((step + 4) * D, 16), D), :].astype(f32)
    joint_g[...] = last[pl.ds(pl.multiple_of(jnp.minimum(step, 2) * D, 16), D), :].astype(f32)


def close(spot, first, last):
    pieces = [*first.values(), *last.values()]
    count = len(first)

    def one(shape):
        return pl.BlockSpec(shape, lambda i: (0,) * len(shape))

    flat = [(POSH,), (FF,)] + [(D,)] * 8
    return pl.pallas_call(
        functools.partial(close_kernel, list(first)),
        grid=(4,),
        in_specs=[pl.BlockSpec(memory_space=pltpu.SMEM)] + [one(piece.shape) for piece in pieces],
        out_specs=[
            pl.BlockSpec((D, D), lambda i: (0, i)), pl.BlockSpec((D, D), lambda i: (i, 0)), one((D, D)),
            pl.BlockSpec((D, D), lambda i: (0, jnp.minimum(i, 2))), one((POSH, D)), one((3, POSH)),
        ]
        + [one(shape) for shape in flat],
        out_shape=[
            shape_of(shape, f32) for shape in [(D, FF), (FF, D), (D, D), (D, 3 * D), (POSH, D), (3, POSH)] + flat
        ],
        scratch_shapes=[
            pltpu.VMEM((pieces[0].shape[0] * count, D), bf16), pltpu.VMEM((pieces[-1].shape[0] * count, D), bf16),
        ],
        compiler_params=settings(),
        name="close",
    )(spot, *pieces)


def bits_of(size):
    return [1 << bit for bit in range(size.bit_length() - 1)]


def chip_bits(size):
    bits = bits_of(size)[:0:-1]
    return [bits[at : at + 2] for at in range(0, len(bits), 2)]


def offsets_of(bits):
    found = [0]
    for bit in reversed(bits):
        found += [offset + bit for offset in found]
    return found


def swapped(values, offset, size):
    return lax.ppermute(values, "dp", [(i, i ^ offset) for i in range(size)])


def total(terms):
    return sum(term.astype(f32) for term in terms).astype(bf16)


def scattered(terms, bits, size):
    offsets = offsets_of(bits)
    mine = (lax.axis_index("dp") // bits[-1]) % len(offsets)
    parts = [term.reshape(len(offsets), -1, D) for term in terms]

    def part(offset):
        return [lax.dynamic_index_in_dim(term, mine ^ (offset // bits[-1]), 0, keepdims=False) for term in parts]

    return part(0) + [swapped(total(part(offset)), offset, size) for offset in offsets[1:]]


def joined(pieces, bits, size):
    found = dict(pieces)
    for offset in offsets_of(bits)[1:]:
        for held, piece in pieces.items():
            found[held ^ offset] = swapped(piece, offset, size)
    return found


def crossed(values, offset, size):
    return lax.ppermute(values, "fsdp", [(i, i ^ offset) for i in range(size)])


def tied(first, second):
    return lax.optimization_barrier((first, second))


def after(value, other):
    return lax.optimization_barrier((value, other))[0]


def per_device(
    sizes,
    tokens,
    centers,
    mask_count,
    mask_index,
    mask_embed,
    place_weight,
    place_bias,
    place_proj,
    place_shift,
    norm_gain,
    norm_shift,
    joint_weight,
    out_weight,
    out_bias,
    mlp_gain,
    mlp_shift,
    up_weight,
    up_bias,
    down_weight,
    down_bias,
    cotangent,
):
    dp, fsdp = sizes["dp"], sizes["fsdp"]
    spot = lax.axis_index("dp").astype(jnp.int32)[None]
    core = spot % 2
    vectors = (mask_embed, place_shift, norm_gain, norm_shift, out_bias, mlp_gain, mlp_shift, down_bias)
    packed, vec = pack(spot, place_proj, joint_weight, out_weight, up_weight, down_weight, vectors, dp)
    packed = lax.all_gather(packed, "fsdp", axis=0)
    packed_other = swapped(packed, 1, dp)
    half = (3 * joint_weight.shape[0] + place_proj.shape[0]) // 2
    late = packed[:, half:]
    pieces = [swapped(late, 2 * offset, dp) for offset in range(1, dp // 2)]
    targets = marked_targets(mask_count, mask_index)
    up_b = up_bias[None, :]
    entry, joint, mixture, shares, weights, joint_w, proj, cen, place_w = front(
        core, tokens, centers, targets, vec, place_weight, place_bias[None, :], packed, packed_other
    )
    pieces, mixture = tied(pieces, mixture)
    pieces_other = [swapped(piece, 1, dp) for piece in pieces]
    order = list(range(dp))
    output, mid_grad, mix_grad, kept, sent, up_bg, vec_g = middle_part(
        spot, entry, mixture, shares, cotangent, vec, up_b, packed, packed_other, pieces, pieces_other, order
    )
    chips = chip_bits(dp)
    near, far = [offset % fsdp for offset in (1, 2)]
    sums = [kept, swapped(sent, 1, dp)]
    mix_grad, sums[-1] = tied(mix_grad, sums[-1])
    sums = scattered(sums, chips[0], dp)
    given = [entry, joint, mixture, weights, mix_grad, mid_grad, cen, targets, vec, place_w, proj, joint_w]
    steps = tokens.shape[0] // ROWS
    early_steps = steps // 2
    before = list(back_part(given, 0, early_steps, order))
    for bits in chips[1:]:
        sums = scattered(sums, bits, dp)
    sums[-1], before[0] = tied(sums[-1], before[0])
    middle_row = sums[0].shape[0] // 2
    upper = total([term[:middle_row] for term in sums])
    lower = total([term[middle_row:] for term in sums])
    upper_got, lower_got = crossed(upper, near, fsdp), crossed(lower, far, fsdp)
    given[4] = after(given[4], lower)
    tokens_grad, kept, sent = back_part(given, early_steps, steps - early_steps, order, before, [core, up_bg, vec_g])
    sent, upper_got, lower_got = lax.optimization_barrier((sent, upper_got, lower_got))
    upper, lower = total([upper, upper_got]), total([lower, lower_got])
    upper_got, lower_got = crossed(upper, far, fsdp), crossed(lower, near, fsdp)
    last = [kept, swapped(sent, 1, dp)]
    last = scattered(last, chips[0], dp)
    upper_got = after(upper_got, last[-1])
    sums = {0: jnp.concatenate([total([upper, upper_got]), total([lower, lower_got])], axis=0)}
    for bits in chips[1:]:
        last = scattered(last, bits, dp)
    value = total(last)
    near_got = after(crossed(value, near, fsdp), sums[0])
    for bits in reversed(chips):
        sums = joined(sums, bits, dp)
    value = total([value, near_got])
    far_got = crossed(value, far, fsdp)
    newest = list(sums)[-1]
    far_got, sums[newest] = tied(far_got, sums[newest])
    last = {0: total([value, far_got])}
    for bits in reversed(chips):
        last = joined(last, bits, dp)
    sums, last = joined(sums, [1], dp), joined(last, [1], dp)
    up_grad, down_grad, out_grad, joint_grad, proj_grad, place_weight_grad, place_bias_grad, up_bias_grad, *small = close(
        spot, sums, last
    )
    return (
        output,
        tokens_grad,
        small[0],
        place_weight_grad,
        place_bias_grad,
        proj_grad,
        small[1],
        small[2],
        small[3],
        joint_grad,
        out_grad,
        small[6],
        small[4],
        small[5],
        up_grad,
        up_bias_grad,
        down_grad,
        small[7],
    )


def solution(mesh):
    rows = P(("dp", "fsdp"), None)
    in_specs = (
        rows,
        P(None, ("dp", "fsdp")),
        P(("dp", "fsdp")),
        rows,
        P(),
        P(),
        P(),
        P("fsdp", None),
        P(),
        P(),
        P(),
        P("fsdp", None),
        P("fsdp", None),
        P(),
        P(),
        P(),
        P("fsdp", None),
        P(),
        P("fsdp", None),
        P(),
        rows,
    )
    out_specs = (rows, rows) + (P(),) * 16
    return jax.shard_map(
        functools.partial(per_device, dict(mesh.shape)), mesh=mesh, in_specs=in_specs, out_specs=out_specs, check_vma=False
    )
```

```python
import functools

import jax
import jax.numpy as jnp
from jax import lax
from jax.experimental import pallas as pl
from jax.experimental.pallas import tpu as pltpu
from jax.sharding import PartitionSpec as P

D = 384
HEADS = 6
FF = 1536
POSH = 128
SEQ = 66
TILE = 8
ROWS = TILE * SEQ
STEP = 64
WIN = 80
KEYS = 128
PAIRS = HEADS // 2
GROUP = 8
BACK_GROUP = 24
SUBS = 2
VMEM = 60 * 2**20
LOG2E = 1.4426950408889634
ROOT_HALF = 0.7071067811865476
PDF = 0.3989422804014327
bf16 = jnp.bfloat16
f32 = jnp.float32

NN = (((1,), (0,)), ((), ()))
NT = (((1,), (1,)), ((), ()))
TN = (((0,), (0,)), ((), ()))


def dot(left, right, dims=NN):
    return lax.dot_general(left, right, dims, preferred_element_type=f32)


def cdf(u):
    return 0.5 + 0.5 * lax.erf(u * ROOT_HALF)


def smooth_slope(u, mass):
    return mass + u * (PDF * jnp.exp2(u * u * (-0.5 * LOG2E)))


def row_mean(values):
    return jnp.sum(values, axis=-1, keepdims=True) * (1.0 / values.shape[-1])


def normalised(values):
    centred = values - row_mean(values)
    scale = lax.rsqrt(row_mean(centred * centred) + 1e-05)
    return centred * scale, scale


def hidden_column(targets):
    windows = []
    for cloud in range(TILE):
        rows = lax.broadcasted_iota(jnp.int32, (WIN, targets.shape[1]), 0) + cloud * STEP
        windows.append(jnp.where(rows == targets[cloud : cloud + 1], 1.0, 0.0))
    blocks = [windows[0][:STEP]]
    for cloud in range(1, TILE):
        blocks += [windows[cloud][:16] + windows[cloud - 1][STEP:], windows[cloud][16:STEP]]
    blocks.append(windows[-1][STEP:])
    return jnp.max(jnp.concatenate(blocks, axis=0), axis=1, keepdims=True)


def lane_mask(rows, odd, kind=bf16):
    lanes = lax.broadcasted_iota(jnp.int32, (rows, 128), 1)
    return (lanes >= 64) if odd else (lanes < 64)


def stacked_heads(tile):
    zero = jnp.zeros_like(tile)
    even = lane_mask(tile.shape[0], False)
    return jnp.concatenate([jnp.where(even, tile, zero), jnp.where(even, zero, tile)], axis=0)


def merged_heads(pair):
    half = pair.shape[0] // 2
    even = lane_mask(half, False)
    return jnp.where(even, pair[:half], pair[half:])


def row_range(rows, low, high, width=128):
    ids = lax.broadcasted_iota(jnp.int32, (rows, width), 0)
    return (ids >= low) & (ids < high)


def spread_heads(flipped):
    none = jnp.zeros((64, flipped.shape[1]), flipped.dtype)
    left = jnp.concatenate([flipped[:64], none], axis=0)
    right = jnp.concatenate([none, flipped[64:]], axis=0)
    return jnp.concatenate([left, right], axis=1)


def head_ones(value):
    rows = lax.broadcasted_iota(jnp.int32, (2 * KEYS, 128), 0) < KEYS
    lanes = lax.broadcasted_iota(jnp.int32, (2 * KEYS, 128), 1) < 64
    return jnp.where(rows == lanes, value, 0.0).astype(bf16)


def lane_ones(value):
    rows = lax.broadcasted_iota(jnp.int32, (128, 2 * KEYS), 0) < 64
    lanes = lax.broadcasted_iota(jnp.int32, (128, 2 * KEYS), 1) < KEYS
    return jnp.where(rows == lanes, value, 0.0).astype(bf16)


def pack_kernel(spot, counts, index, proj, joint, out, up, down, up_bias, *refs):
    vectors, (packed, vec, up_b, targets, early, late, turned) = refs[:8], refs[8:]
    for at, vector in enumerate(vectors):
        vec[at : at + 1, :] = vector[...].reshape(1, D)
    up_b[...] = up_bias[...].reshape(1, FF)
    most, clouds = index.shape
    slots = lax.broadcasted_iota(jnp.int32, (1, 128), 1)
    turned[...] = jnp.zeros(turned.shape, f32)
    turned[:most, :clouds] = index[...].astype(f32)
    chosen = turned[...].T.astype(jnp.int32)
    for cloud in range(clouds):
        first = 1 + SEQ * (cloud % TILE)
        targets[cloud : cloud + 1, :] = jnp.where(slots < counts[cloud], chosen[cloud : cloud + 1, :] + first, -1)
    rows = joint.shape[0]
    for part in range(3):
        early[part * rows : part * rows + rows, :] = joint[:, part * D : part * D + D]
    early[3 * rows :, :] = proj[...]
    late[:rows, :] = out[...]
    for part in range(4):
        late[(part + 1) * rows : (part + 2) * rows, :] = up[:, part * D : part * D + D]
    late[5 * rows : 5 * rows + down.shape[0], :] = down[...]
    half = early.shape[0] // 2
    piece = packed.shape[0] - half
    chips = late.shape[0] // piece // 2
    packed[:half, :] = early[pl.ds(pl.multiple_of((spot[0] % 2) * half, 16), half), :]
    own = (spot[0] % 2) * chips + spot[0] // 2
    packed[half:, :] = late[pl.ds(pl.multiple_of(own * piece, 16), piece), :]


def pack(spot, counts, index, proj, joint, out, up, down, up_bias, vectors, parts):
    rows, low, deep = joint.shape[0], proj.shape[0], down.shape[0]
    size = 3 * rows + low
    late = padded(5 * rows + deep, parts)
    vmem = pl.BlockSpec(memory_space=pltpu.VMEM)
    return pl.pallas_call(
        pack_kernel,
        in_specs=[pl.BlockSpec(memory_space=pltpu.SMEM)] * 2 + [vmem] * 15,
        out_specs=[vmem] * 4,
        out_shape=[
            shape_of((size // 2 + late // parts, D), bf16), shape_of((8, D), f32), shape_of((1, FF), f32),
            shape_of((counts.shape[0], 128), jnp.int32),
        ],
        scratch_shapes=[pltpu.VMEM((size, D), bf16), pltpu.VMEM((late, D), bf16), pltpu.VMEM((128, 128), f32)],
        compiler_params=settings(),
        name="pack",
    )(spot, counts, index, proj, joint, out, up, down, up_bias, *vectors)


def unpack_early(core, mine, other, joint_w, proj):
    groups = mine.shape[0]
    rows, low = D // groups, POSH // groups
    half = (3 * rows + low) // 2

    def place(side, source):
        for group in range(groups):
            at = 0
            while at < half:
                row = side * half + at
                if row < 3 * rows:
                    part, inner = divmod(row, rows)
                    size = min(half - at, rows - inner)
                    first = group * rows + inner
                    joint_w[first : first + size, part * D : part * D + D] = source[group, at : at + size]
                else:
                    size = half - at
                    first = group * low + row - 3 * rows
                    proj[first : first + size, :] = source[group, at : at + size]
                at += size

    @pl.when(core == 0)
    def _():
        place(0, mine)
        place(1, other)

    @pl.when(core == 1)
    def _():
        place(0, other)
        place(1, mine)


def unpack_late(spot, mine, other, near, near_other, lates, out_w, up_w, down_w):
    _, chips, groups, piece, _ = lates.shape
    rows, deep = D // groups, FF // groups
    half = mine.shape[1] - piece
    core, chip = spot % 2, spot // 2
    for side, own, rest in ((core, mine, near), (1 - core, other, near_other)):
        lates[side, chip] = own[:, half:, :]
        for offset, source in enumerate(rest):
            lates[side, chip ^ (offset + 1)] = source[...]
    for at_chip in range(2 * chips):
        for group in range(groups):
            at = 0
            while at < piece:
                row = at_chip * piece + at
                source = lates.at[at_chip // chips, at_chip % chips, group]
                if row < rows:
                    size = min(piece - at, rows - row)
                    first = group * rows + row
                    out_w[first : first + size, :] = source[at : at + size, :]
                elif row < 5 * rows:
                    block, inner = divmod(row - rows, rows)
                    size = min(piece - at, rows - inner)
                    first = group * rows + inner
                    up_w[first : first + size, block * D : block * D + D] = source[at : at + size, :]
                elif row < 5 * rows + deep:
                    inner = row - 5 * rows
                    size = min(piece - at, deep - inner)
                    first = group * deep + inner
                    down_w[first : first + size, :] = source[at : at + size, :]
                else:
                    size = piece - at
                at += size


def picked(rows, first, source):
    ids = lax.broadcasted_iota(jnp.int32, (16, rows), 0) - lax.broadcasted_iota(jnp.int32, (16, rows), 1)
    return dot(jnp.where(ids == first, 1.0, 0.0).astype(bf16), source)


def split16(values):
    high = values.astype(bf16)
    return high, (values - high.astype(f32)).astype(bf16)


def place_inputs(centers, place_weight, place_bias, cen, place_w):
    for tile in range(cen.shape[0]):
        high, rest = split16(centers[:, tile * ROWS : tile * ROWS + ROWS])
        ids = lax.broadcasted_iota(jnp.int32, (16, ROWS), 0)
        ones = jnp.where((ids == 9) | (ids == 10), 1.0, 0.0)
        cen[tile] = (picked(3, 0, high) + picked(3, 3, rest) + picked(3, 6, high) + ones).astype(bf16)
    high, rest = split16(place_weight[...])
    bias_high, bias_rest = split16(place_bias[...])
    value = picked(3, 0, high) + picked(3, 3, high) + picked(3, 6, rest) + picked(1, 9, bias_high) + picked(1, 10, bias_rest)
    place_w[...] = value.astype(bf16)


def front_kernel(core, tokens, centers, targets, vec, place_weight, place_bias, mine, other,
                 entry, joint, mixture, shares, weights, joint_w, proj, cen, place_w, qkv):
    step = pl.program_id(0)

    @pl.when(step == 0)
    def _():
        for sub in range(SUBS):
            qkv[sub, ROWS:, :] = jnp.zeros((qkv.shape[1] - ROWS, 3 * D), bf16)
        unpack_early(core[0], mine, other, joint_w, proj)
        place_inputs(centers, place_weight, place_bias, cen, place_w)

    lanes = lax.broadcasted_iota(jnp.int32, (1, 2 * KEYS), 1) % KEYS
    sums_of = head_ones(1.0)
    none = jnp.zeros((16, 2 * KEYS), bf16)
    scale_row = jnp.where(lax.broadcasted_iota(jnp.int32, (1, 3 * D), 1) < D, 0.125 * LOG2E, 1.0)

    def normal_rows(sub):
        span = slice(sub * ROWS, sub * ROWS + ROWS)
        pre = dot(cen[step * SUBS + sub], place_w[...], TN)
        low = (pre * cdf(pre)).astype(bf16)
        placed = dot(low, proj[...]) + vec[1:2, :]
        hidden = hidden_column(targets[sub * TILE : sub * TILE + TILE, :])
        rows = jnp.where(hidden > 0.5, vec[0:1, :], tokens[span, :].astype(f32)) + placed
        entry[span, :] = rows.astype(bf16)
        unit, _ = normalised(rows)
        return (unit * vec[2:3, :] + vec[3:4, :]).astype(bf16)

    def project(sub, normed, first):
        cols = slice(first, min(first + 256, 3 * D))
        value = (dot(normed, joint_w[:, cols]) * scale_row[:, cols]).astype(bf16)
        qkv[sub, :ROWS, cols] = value
        joint[sub * ROWS : sub * ROWS + ROWS, cols] = value

    def score(sub, pair, cloud):
        base = cloud * STEP
        query = qkv[sub, base : base + WIN, pair * 128 : pair * 128 + 128]
        key = qkv[sub, base : base + KEYS, D + pair * 128 : D + pair * 128 + 128]
        return dot(query, spread_heads(key.T))

    def exponentials(cloud, scores):
        live = (lanes >= 2 * cloud) & (lanes < 2 * cloud + SEQ - 1)
        scores = jnp.where(live, scores, -1e30)
        parts = []
        for half in (scores[:, :KEYS], scores[:, KEYS:]):
            parts.append(jnp.exp2(half - jnp.max(half, axis=-1, keepdims=True)).astype(bf16))
        return jnp.concatenate(parts, axis=1)

    def mixed(sub, pair, cloud, e):
        base = cloud * STEP
        value = qkv[sub, base : base + KEYS, 2 * D + pair * 128 : 2 * D + pair * 128 + 128]
        return dot(e, jnp.concatenate([stacked_heads(value), sums_of], axis=1))

    tails = {}

    def store(sub, pair, cloud, e, both):
        base = sub * ROWS + cloud * STEP
        cols = slice(pair * 128, pair * 128 + 128)
        share = 1.0 / both[:, 128:]
        mix = both[:, :128] * share
        spot = slice(pair * 256, pair * 256 + 256)
        at = sub * TILE + cloud
        weights[at, :16, spot] = jnp.where(row_range(16, 2 * cloud, 16, 256), e[:16], none)
        weights[at, 16:64, spot] = e[16:64]
        weights[at, 64:80, spot] = jnp.where(row_range(16, 0, 2 * cloud + 2, 256), e[64:80], none)
        head_mix, head_share = mix[:16], share[:16]
        if cloud:
            head = row_range(16, 0, 2 * cloud)
            tail_mix, tail_share = tails[sub, pair]
            head_mix = jnp.where(head, tail_mix, head_mix)
            head_share = jnp.where(head, tail_share, head_share)
        mixture[base : base + 16, cols] = head_mix.astype(bf16)
        shares[base : base + 16, cols] = head_share.astype(bf16)
        mixture[base + 16 : base + 64, cols] = mix[16:64].astype(bf16)
        shares[base + 16 : base + 64, cols] = share[16:64].astype(bf16)
        tails[sub, pair] = (mix[64:], share[64:])
        if cloud == TILE - 1:
            mixture[base + 64 : base + 80, cols] = mix[64:].astype(bf16)
            shares[base + 64 : base + 80, cols] = share[64:].astype(bf16)

    jobs = [(pair, cloud) for pair in range(PAIRS) for cloud in range(TILE)]
    groups = [jobs[at : at + GROUP] for at in range(0, len(jobs), GROUP)]
    normed = [normal_rows(sub) for sub in range(SUBS)]
    chunks = range(0, 3 * D, 256)
    for first in chunks:
        project(0, normed[0], first)
    waiting = None
    for sub in range(SUBS):
        fill = [functools.partial(project, sub + 1, normed[sub + 1], first) for first in chunks] if sub + 1 < SUBS else []
        share_of = -(-len(fill) // len(groups))
        for group in groups:
            exps = [exponentials(cloud, score(sub, pair, cloud)) for pair, cloud in group]
            for task in fill[:share_of]:
                task()
            fill = fill[share_of:]
            if waiting:
                close_group(mixed, store, *waiting)
            waiting = (sub, group, exps)
    close_group(mixed, store, *waiting)


def close_group(mixed, store, sub, group, exps):
    boths = [mixed(sub, pair, cloud, e) for (pair, cloud), e in zip(group, exps)]
    for (pair, cloud), e, both in zip(group, exps, boths):
        store(sub, pair, cloud, e, both)


def whole(shape):
    return pl.BlockSpec(shape, lambda i: (0,) * len(shape))


def rows_of(width, rows=ROWS):
    return pl.BlockSpec((rows, width), lambda i: (i, 0))


def slab(shape):
    return pl.BlockSpec((1, *shape), lambda i: (i,) + (0,) * len(shape))


def shape_of(dims, kind):
    return jax.ShapeDtypeStruct(dims, kind)


def cost(microseconds):
    return pl.CostEstimate(flops=int(microseconds * 9e8), bytes_accessed=int(microseconds * 2e6), transcendentals=0)


def settings():
    return pltpu.CompilerParams(vmem_limit_bytes=VMEM)


def front(core, tokens, centers, targets, vec, place_weight, place_bias, mine, other):
    count = tokens.shape[0]
    steps = count // ROWS
    rows = SUBS * ROWS
    return pl.pallas_call(
        front_kernel,
        grid=(steps // SUBS,),
        in_specs=[
            pl.BlockSpec(memory_space=pltpu.SMEM), rows_of(D, rows), whole(centers.shape),
            pl.BlockSpec((SUBS * TILE, 128), lambda i: (i, 0)), whole((8, D)),
            whole((3, POSH)), whole((1, POSH)), whole(mine.shape), whole(other.shape),
        ],
        out_specs=[
            rows_of(D, rows), rows_of(3 * D, rows), rows_of(D, rows), rows_of(D, rows),
            pl.BlockSpec((SUBS * TILE, WIN, HEADS * KEYS), lambda i: (i, 0, 0)), whole((D, 3 * D)), whole((POSH, D)),
            whole((steps, 16, ROWS)), whole((16, POSH)),
        ],
        out_shape=[
            shape_of((count, D), bf16), shape_of((count, 3 * D), bf16),
            shape_of((count, D), bf16), shape_of((count, D), bf16),
            shape_of((steps * TILE, WIN, HEADS * KEYS), bf16), shape_of((D, 3 * D), bf16), shape_of((POSH, D), bf16),
            shape_of((steps, 16, ROWS), bf16), shape_of((16, POSH), bf16),
        ],
        scratch_shapes=[pltpu.VMEM((SUBS, ROWS + 48, 3 * D), bf16)],
        compiler_params=settings(),
        cost_estimate=cost(28),
        name="front",
    )(core, tokens, centers, targets, vec, place_weight, place_bias, mine, other)


def write_sums(sums, order, first, values):
    size = sums.shape[0] // len(order)
    at = 0
    while at < values.shape[0]:
        row = first + at
        segment, inner = divmod(row, size)
        step = min(size - inner, values.shape[0] - at)
        spot = order[segment] * size + inner
        sums[spot : spot + step, :] = values[at : at + step].astype(bf16)
        at += step


def share_halves(core, sums, kept, sent):
    half = sent.shape[0]
    kept[...] = sums[pl.ds(pl.multiple_of(core * half, 16), half), :]
    sent[...] = sums[pl.ds(pl.multiple_of((1 - core) * half, 16), half), :]


def padded(rows, size):
    return -(-rows // (16 * size)) * 16 * size


def middle_kernel(chunk, order, spot, entry, mixture, shares, cot, vec, up_b, mine, other, *refs):
    chips = len(order) // 2
    near, near_other, refs = refs[: chips - 1], refs[chips - 1 : 2 * chips - 2], refs[2 * chips - 2 :]
    (output, mid_grad, mix_grad, kept, sent, up_bg, vec_g,
     down_acc, up_acc, out_acc, out_w, up_w, down_w, gated, sums, lates) = refs
    step = pl.program_id(0)

    @pl.when(step == 0)
    def _():
        unpack_late(spot[0], mine, other, near, near_other, lates, out_w, up_w, down_w)
        for ref in (down_acc, up_acc, out_acc, up_bg, vec_g):
            ref[...] = jnp.zeros(ref.shape, ref.dtype)

    parts = FF // chunk
    spans = [slice(part * chunk, part * chunk + chunk) for part in range(parts)]
    mix = mixture[...]
    cotangent = cot[...]
    mid = entry[...].astype(f32) + (dot(mix, out_w[...]) + vec[4:5, :])
    gates = [dot(cotangent, down_w[spans[0], :], NT)]
    unit, scale = normalised(mid)
    normed = (unit * vec[5:6, :] + vec[6:7, :]).astype(bf16)
    lows = []

    def down_part(part):
        down_acc[:, spans[part]] += dot(cotangent, gated[:, spans[part]], TN)

    def up_part(part):
        up_acc[:, spans[part]] += dot(normed, lows[part], TN)

    for part in range(parts):
        cols = spans[part]
        raised = dot(normed, up_w[:, cols]) + up_b[:, cols]
        if part + 1 < parts:
            gates.append(dot(cotangent, down_w[spans[part + 1], :], NT))
        mass = cdf(raised)
        gated[:, cols] = (raised * mass).astype(bf16)
        grad = gates[part] * smooth_slope(raised, mass)
        up_bg[:, cols] += jnp.sum(grad, axis=0, keepdims=True)
        lows.append(grad.astype(bf16))
        if part:
            down_part(part - 1)
            if part > 1:
                up_part(part - 2)
    back = dot(jnp.concatenate(lows, axis=1), up_w[...], NT)
    up_part(parts - 2)
    down_part(parts - 1)
    up_part(parts - 1)
    output[...] = (mid + (dot(gated[...], down_w[...]) + vec[7:8, :])).astype(bf16)
    upstream = cotangent.astype(f32)
    tilted = back * vec[5:6, :]
    grad = upstream + scale * (tilted - row_mean(tilted) - unit * row_mean(tilted * unit))
    low = grad.astype(bf16)
    mid_grad[...] = low
    mix_grad[...] = (dot(low, out_w[...], NT) * shares[...].astype(f32)).astype(bf16)
    out_acc[...] += dot(mix, low, TN)
    vec_g[0:1, :] += jnp.sum(back * unit, axis=0, keepdims=True)
    vec_g[1:2, :] += jnp.sum(back, axis=0, keepdims=True)
    vec_g[2:3, :] += jnp.sum(grad, axis=0, keepdims=True)
    vec_g[3:4, :] += jnp.sum(upstream, axis=0, keepdims=True)

    @pl.when(step == pl.num_programs(0) - 1)
    def _():
        for part in range(4):
            write_sums(sums, order, part * D, up_acc[:, part * D : part * D + D])
        write_sums(sums, order, 4 * D, down_acc[...].T)
        write_sums(sums, order, 8 * D, out_acc[...])
        if sums.shape[0] > 9 * D:
            write_sums(sums, order, 9 * D, jnp.zeros((sums.shape[0] - 9 * D, D), f32))
        share_halves(spot[0] % 2, sums, kept, sent)


def middle_part(spot, entry, mixture, shares, cot, vec, up_b, mine, other, near, near_other, order, rows=704, chunk=768):
    count = entry.shape[0]
    size = padded(9 * D, len(order))
    return pl.pallas_call(
        functools.partial(middle_kernel, chunk, order),
        grid=(count // rows,),
        in_specs=[
            pl.BlockSpec(memory_space=pltpu.SMEM), rows_of(D, rows), rows_of(D, rows), rows_of(D, rows), rows_of(D, rows),
            whole((8, D)), whole((1, FF)), whole(mine.shape), whole(other.shape),
        ]
        + [whole(piece.shape) for piece in [*near, *near_other]],
        out_specs=[
            rows_of(D, rows), rows_of(D, rows), rows_of(D, rows),
            whole((size // 2, D)), whole((size // 2, D)), whole((1, FF)), whole((8, D)),
        ],
        out_shape=[
            shape_of((count, D), bf16), shape_of((count, D), bf16), shape_of((count, D), bf16),
            shape_of((size // 2, D), bf16), shape_of((size // 2, D), bf16), shape_of((1, FF), f32), shape_of((8, D), f32),
        ],
        scratch_shapes=[
            pltpu.VMEM((D, FF), f32), pltpu.VMEM((D, FF), f32), pltpu.VMEM((D, D), f32),
            pltpu.VMEM((D, D), bf16), pltpu.VMEM((D, FF), bf16), pltpu.VMEM((FF, D), bf16),
            pltpu.VMEM((rows, FF), bf16), pltpu.VMEM((size, D), bf16),
            pltpu.VMEM((2, len(order) // 2, *near[0].shape), bf16),
        ],
        compiler_params=settings(),
        cost_estimate=cost(55),
        name="middle",
    )(spot, entry, mixture, shares, cot, vec, up_b, mine, other, *near, *near_other)


def back_kernel(is_first, is_last, order, *refs):
    entry, joint, mixture, weights, mix_grad, mid_grad, cen, targets, vec, place_w, proj, joint_w = refs[:12]
    refs = refs[12:]
    if not is_first:
        before, refs = refs[1:5], refs[5:]
    if is_last:
        core, up_bg, mid_vec_g, tokens_g, kept, sent, joint_g, proj_g, place_g, vec_g, qkv, dqkv, sums = refs
    else:
        tokens_g, joint_g, proj_g, place_g, vec_g, qkv, dqkv = refs
    step = pl.program_id(0)

    @pl.when(step == 0)
    def _():
        for at, ref in enumerate((joint_g, proj_g, place_g, vec_g)):
            ref[...] = jnp.zeros(ref.shape, ref.dtype) if is_first else before[at][...]
        qkv[ROWS:, :] = jnp.zeros((qkv.shape[0] - ROWS, 3 * D), bf16)

    qkv[:ROWS, :] = joint[...]
    pre = dot(cen[0], place_w[...], TN)
    unit, scale = normalised(entry[...].astype(f32))
    normed = (unit * vec[2:3, :] + vec[3:4, :]).astype(bf16)
    minus = lane_ones(-1.0)
    jobs = [(pair, cloud) for pair in range(PAIRS) for cloud in range(TILE)]
    tails = {}
    for at in range(0, len(jobs), BACK_GROUP):
        group = jobs[at : at + BACK_GROUP]
        gaps = []
        for pair, cloud in group:
            base = cloud * STEP
            window = slice(base, base + WIN)
            cols = slice(pair * 128, pair * 128 + 128)
            value = qkv[base : base + KEYS, 2 * D + pair * 128 : 2 * D + pair * 128 + 128]
            dmw = mix_grad[window, cols]
            left = jnp.concatenate([dmw, dmw * mixture[window, cols]], axis=1)
            gaps.append(dot(left, jnp.concatenate([spread_heads(value.T), minus], axis=0)))
        es, dss = [], []
        for (pair, cloud), gap in zip(group, gaps):
            e = weights[cloud, :, pair * 256 : pair * 256 + 256]
            es.append(e)
            dss.append((e.astype(f32) * gap).astype(bf16))
        results = []
        for (pair, cloud), e, ds in zip(group, es, dss):
            base = cloud * STEP
            query = stacked_heads(qkv[base : base + WIN, pair * 128 : pair * 128 + 128])
            key = stacked_heads(qkv[base : base + KEYS, D + pair * 128 : D + pair * 128 + 128])
            sdm = stacked_heads(mix_grad[base : base + WIN, pair * 128 : pair * 128 + 128])
            e = jnp.concatenate([e[:, :KEYS], e[:, KEYS:]], axis=0)
            tall = jnp.concatenate([ds[:, :KEYS], ds[:, KEYS:]], axis=0)
            results.append((dot(ds, key), dot(tall[:, :WIN], query, TN), dot(e[:, :WIN], sdm, TN)))
        for (pair, cloud), (dq, dk, dv) in zip(group, results):
            base = cloud * STEP
            parts = (dq * 0.125, dk * (1.0 / LOG2E), dv)
            for which, part in enumerate(parts):
                cols = slice(which * D + pair * 128, which * D + pair * 128 + 128)
                head = part[:16]
                if cloud:
                    head = jnp.where(row_range(16, 0, 2 * cloud), tails[pair, which], head)
                dqkv[base : base + 16, cols] = head.astype(bf16)
                dqkv[base + 16 : base + 64, cols] = part[16:64].astype(bf16)
                tails[pair, which] = part[64:80]
                if cloud == TILE - 1:
                    dqkv[ROWS - 16 :, cols] = part[64:80].astype(bf16)


    back = dot(dqkv[...], joint_w[...], NT)
    joint_g[...] += dot(normed, dqkv[...], TN)
    tilted = back * vec[2:3, :]
    grad = mid_grad[...].astype(f32) + scale * (tilted - row_mean(tilted) - unit * row_mean(tilted * unit))
    low = grad.astype(bf16)
    mass = cdf(pre)
    place_low = (pre * mass).astype(bf16)
    pre_grad = dot(low, proj[...], NT) * smooth_slope(pre, mass)
    proj_g[...] += dot(place_low, low, TN)
    hidden = hidden_column(targets[...])
    marked = jnp.where(hidden > 0.5, grad, 0.0)
    tokens_g[...] = (grad - marked).astype(bf16)
    high_part = pre_grad.astype(bf16)
    low_part = (pre_grad - high_part.astype(f32)).astype(bf16)
    place_g[...] += dot(cen[0], jnp.concatenate([high_part, low_part], axis=1))
    vec_g[0:1, :] += jnp.sum(marked, axis=0, keepdims=True)
    vec_g[1:2, :] += jnp.sum(grad, axis=0, keepdims=True)
    vec_g[2:3, :] += jnp.sum(back * unit, axis=0, keepdims=True)
    vec_g[3:4, :] += jnp.sum(back, axis=0, keepdims=True)
    if not is_last:
        return

    @pl.when(step == pl.num_programs(0) - 1)
    def _():
        for part in range(3):
            write_sums(sums, order, part * D, joint_g[:, part * D : part * D + D])
        write_sums(sums, order, 3 * D, proj_g[...])
        place = place_g[:, :POSH] + place_g[:, POSH:]
        place_weight = place[0:3] + place_g[3:6, :POSH]
        small = jnp.concatenate(
            [
                vec_g[0:4, :],
                mid_vec_g[0:4, :],
                jnp.concatenate([place_weight[0:1], place_weight[1:2], place_weight[2:3]], axis=1),
                jnp.concatenate([place[9:10], jnp.zeros((1, D - POSH), f32)], axis=1),
                jnp.concatenate([up_bg[:, part * D : part * D + D] for part in range(4)], axis=0),
                jnp.zeros((sums.shape[0] - 3 * D - POSH - 14, D), f32),
            ],
            axis=0,
        )
        write_sums(sums, order, 3 * D + POSH, small)
        share_halves(core[0], sums, kept, sent)


def back_part(given, first, steps, order, before=None, extra=None):
    count = given[0].shape[0]

    def shifted(width):
        return pl.BlockSpec((ROWS, width), lambda i: (i + first, 0))

    def shifted_slab(shape):
        return pl.BlockSpec((1, *shape), lambda i: (i + first, 0, 0))

    accs = [(D, 3 * D), (POSH, D), (16, 256), (8, D)]
    in_specs = [
        shifted(D), shifted(3 * D), shifted(D),
        pl.BlockSpec((TILE, WIN, HEADS * KEYS), lambda i: (i + first, 0, 0)),
        shifted(D), shifted(D), shifted_slab((16, ROWS)),
        pl.BlockSpec((TILE, 128), lambda i: (i + first, 0)),
        whole((8, D)), whole((16, POSH)), whole((POSH, D)), whole((D, 3 * D)),
    ]
    given = list(given)
    if before is not None:
        given += before
        in_specs += [pl.BlockSpec(memory_space=pl.ANY)] + [whole(acc) for acc in accs]
    out_specs, out_shape = [shifted(D)], [shape_of((count, D), bf16)]
    scratch = [pltpu.VMEM((ROWS + 48, 3 * D), bf16), pltpu.VMEM((ROWS, 3 * D), bf16)]
    if extra is not None:
        given += extra
        in_specs += [pl.BlockSpec(memory_space=pltpu.SMEM), whole((1, FF)), whole((8, D))]
        size = padded(3 * D + POSH + 16, len(order))
        out_specs += [whole((size // 2, D))] * 2
        out_shape += [shape_of((size // 2, D), bf16)] * 2
        scratch = [pltpu.VMEM(acc, f32) for acc in accs] + scratch + [pltpu.VMEM((size, D), bf16)]
    else:
        out_specs += [whole(acc) for acc in accs]
        out_shape += [shape_of(acc, f32) for acc in accs]
    return pl.pallas_call(
        functools.partial(back_kernel, before is None, extra is not None, order),
        grid=(steps,),
        in_specs=in_specs,
        out_specs=out_specs,
        out_shape=out_shape,
        scratch_shapes=scratch,
        input_output_aliases={} if before is None else {12: 0},
        compiler_params=settings(),
        cost_estimate=cost(5 * steps),
        name="back",
    )(*given)


def gather_pieces(spot, offsets, pieces, sums):
    segment = pieces[0].shape[0] // len(offsets)
    chips = len(offsets)
    for core, piece in enumerate(pieces):
        for at, offset in enumerate(offsets):
            holder = spot ^ offset ^ core
            row = pl.multiple_of(((holder % 2) * chips + holder // 2) * segment, 16)
            sums[pl.ds(row, segment), :] = piece[at * segment : at * segment + segment, :]


def widen_kernel(offsets, spot, *refs):
    pieces, (up_g, down_g, out_g, sums) = refs[:2], refs[2:]
    step = pl.program_id(0)

    @pl.when(step == 0)
    def _():
        gather_pieces(spot[0], offsets, pieces, sums)
        out_g[...] = sums[8 * D : 9 * D, :].astype(f32)

    up_g[...] = sums[pl.ds(pl.multiple_of(step * D, 16), D), :].astype(f32)
    down_g[...] = sums[pl.ds(pl.multiple_of((step + 4) * D, 16), D), :].astype(f32)


def close_kernel(offsets, spot, *refs):
    pieces, (joint_g, proj_g, place_g, *small), last = refs[:2], refs[2:-1], refs[-1]
    step = pl.program_id(0)

    @pl.when(step == 0)
    def _():
        gather_pieces(spot[0], offsets, pieces, last)
        proj_g[...] = last[3 * D : 3 * D + POSH, :].astype(f32)
        rows = last[3 * D + POSH : 3 * D + POSH + 16, :].astype(f32)
        for part in range(3):
            place_g[part : part + 1, :] = rows[8:9, part * POSH : part * POSH + POSH]
        small[0][...] = rows[9:10, :POSH].reshape(POSH)
        small[1][...] = jnp.concatenate([rows[10 + part : 11 + part] for part in range(4)], axis=1).reshape(FF)
        for at in range(8):
            small[2 + at][...] = rows[at : at + 1].reshape(D)

    joint_g[...] = last[pl.ds(pl.multiple_of(step * D, 16), D), :].astype(f32)


def one(shape):
    return pl.BlockSpec(shape, lambda i: (0,) * len(shape))


def unpacked(kernel, name, steps, shapes, specs, spot, offsets, values):
    return pl.pallas_call(
        functools.partial(kernel, offsets),
        grid=(steps,),
        in_specs=[pl.BlockSpec(memory_space=pltpu.SMEM)] + [one(value.shape) for value in values],
        out_specs=specs,
        out_shape=[shape_of(shape, f32) for shape in shapes],
        scratch_shapes=[pltpu.VMEM((values[0].shape[0] * 2, D), bf16)],
        compiler_params=settings(),
        cost_estimate=cost(4),
        name=name,
    )(spot, *values)


def widen(spot, offsets, values):
    specs = [pl.BlockSpec((D, D), lambda i: (0, i)), pl.BlockSpec((D, D), lambda i: (i, 0)), one((D, D))]
    return unpacked(widen_kernel, "widen", 4, [(D, FF), (FF, D), (D, D)], specs, spot, offsets, values)


def close(spot, offsets, values):
    shapes = [(POSH, D), (3, POSH), (POSH,), (FF,)] + [(D,)] * 8
    specs = [pl.BlockSpec((D, D), lambda i: (0, i))] + [one(shape) for shape in shapes]
    return unpacked(close_kernel, "close", 3, [(D, 3 * D)] + shapes, specs, spot, offsets, values)


def bits_of(size):
    return [1 << bit for bit in range(size.bit_length() - 1)]


def chip_bits(size):
    bits = bits_of(size)[:0:-1]
    return [bits[at : at + 2] for at in range(0, len(bits), 2)]


def offsets_of(bits):
    found = [0]
    for bit in reversed(bits):
        found += [offset + bit for offset in found]
    return found


def swapped(values, offset, size):
    return lax.ppermute(values, "dp", [(i, i ^ offset) for i in range(size)])


def total(terms):
    return sum(term.astype(f32) for term in terms).astype(bf16)


def scattered(terms, bits, size):
    offsets = offsets_of(bits)
    mine = (lax.axis_index("dp") // bits[-1]) % len(offsets)
    parts = [term.reshape(len(offsets), -1, D) for term in terms]

    def part(offset):
        return [lax.dynamic_index_in_dim(term, mine ^ (offset // bits[-1]), 0, keepdims=False) for term in parts]

    return part(0) + [swapped(total(part(offset)), offset, size) for offset in offsets[1:]]


def joined(pieces, bits, size):
    found = dict(pieces)
    for offset in offsets_of(bits)[1:]:
        for held, piece in pieces.items():
            found[held ^ offset] = swapped(piece, offset, size)
    return found


def crossed(values, offset, size):
    return lax.ppermute(values, "fsdp", [(i, i ^ offset) for i in range(size)])


def tied(first, second):
    return lax.optimization_barrier((first, second))


def after(value, other):
    return lax.optimization_barrier((value, other))[0]


def per_device(
    sizes,
    tokens,
    centers,
    mask_count,
    mask_index,
    mask_embed,
    place_weight,
    place_bias,
    place_proj,
    place_shift,
    norm_gain,
    norm_shift,
    joint_weight,
    out_weight,
    out_bias,
    mlp_gain,
    mlp_shift,
    up_weight,
    up_bias,
    down_weight,
    down_bias,
    cotangent,
):
    dp, fsdp = sizes["dp"], sizes["fsdp"]
    spot = lax.axis_index("dp").astype(jnp.int32)[None]
    core = spot % 2
    vectors = (mask_embed, place_shift, norm_gain, norm_shift, out_bias, mlp_gain, mlp_shift, down_bias)
    packed, vec, up_b, targets = pack(
        spot, mask_count, mask_index.T, place_proj, joint_weight, out_weight, up_weight, down_weight, up_bias, vectors, dp
    )
    packed = lax.all_gather(packed, "fsdp", axis=0)
    packed_other = swapped(packed, 1, dp)
    half = (3 * joint_weight.shape[0] + place_proj.shape[0]) // 2
    late = packed[:, half:]
    pieces = [swapped(late, 2 * offset, dp) for offset in range(1, dp // 2)]
    entry, joint, mixture, shares, weights, joint_w, proj, cen, place_w = front(
        core, tokens, centers, targets, vec, place_weight, place_bias[None, :], packed, packed_other
    )
    pieces, mixture = tied(pieces, mixture)
    pieces_other = [swapped(piece, 1, dp) for piece in pieces]
    order = list(range(dp))
    output, mid_grad, mix_grad, kept, sent, up_bg, vec_g = middle_part(
        spot, entry, mixture, shares, cotangent, vec, up_b, packed, packed_other, pieces, pieces_other, order
    )
    chips = chip_bits(dp)
    near, far = [offset % fsdp for offset in (1, 2)]
    sums = [kept, swapped(sent, 1, dp)]
    mix_grad, sums[-1] = tied(mix_grad, sums[-1])
    sums = scattered(sums, chips[0], dp)
    given = [entry, joint, mixture, weights, mix_grad, mid_grad, cen, targets, vec, place_w, proj, joint_w]
    steps = tokens.shape[0] // ROWS
    early_steps = steps // 2
    before = list(back_part(given, 0, early_steps, order))
    for bits in chips[1:]:
        sums = scattered(sums, bits, dp)
    sums[-1], before[0] = tied(sums[-1], before[0])
    middle_row = sums[0].shape[0] // 2
    upper = total([term[:middle_row] for term in sums])
    lower = total([term[middle_row:] for term in sums])
    upper_got, lower_got = crossed(upper, near, fsdp), crossed(lower, far, fsdp)
    given[4] = after(given[4], lower)
    tokens_grad, kept, sent = back_part(given, early_steps, steps - early_steps, order, before, [core, up_bg, vec_g])
    sent, upper_got, lower_got = lax.optimization_barrier((sent, upper_got, lower_got))
    upper, lower = total([upper, upper_got]), total([lower, lower_got])
    upper_got, lower_got = crossed(upper, far, fsdp), crossed(lower, near, fsdp)
    last = [kept, swapped(sent, 1, dp)]
    last = scattered(last, chips[0], dp)
    upper_got = after(upper_got, last[-1])
    sums = {0: jnp.concatenate([total([upper, upper_got]), total([lower, lower_got])], axis=0)}
    for bits in chips[1:]:
        last = scattered(last, bits, dp)
    value = total(last)
    near_got = after(crossed(value, near, fsdp), sums[0])
    for bits in reversed(chips):
        sums = joined(sums, bits, dp)
    value = total([value, near_got])
    far_got = crossed(value, far, fsdp)
    soonest = list(sums)[1]
    far_got, sums[soonest] = tied(far_got, sums[soonest])
    last = {0: total([value, far_got])}
    for bits in reversed(chips):
        last = joined(last, bits, dp)
    held = jnp.concatenate(list(sums.values()), axis=0)
    up_grad, down_grad, out_grad = widen(spot, list(sums), [held, swapped(held, 1, dp)])
    newest = list(last)[-1]
    last[newest] = after(last[newest], out_grad)
    held = jnp.concatenate(list(last.values()), axis=0)
    joint_grad, proj_grad, place_weight_grad, place_bias_grad, up_bias_grad, *small = close(
        spot, list(last), [held, swapped(held, 1, dp)]
    )
    return (
        output,
        tokens_grad,
        small[0],
        place_weight_grad,
        place_bias_grad,
        proj_grad,
        small[1],
        small[2],
        small[3],
        joint_grad,
        out_grad,
        small[6],
        small[4],
        small[5],
        up_grad,
        up_bias_grad,
        down_grad,
        small[7],
    )


def solution(mesh):
    rows = P(("dp", "fsdp"), None)
    in_specs = (
        rows,
        P(None, ("dp", "fsdp")),
        P(("dp", "fsdp")),
        rows,
        P(),
        P(),
        P(),
        P("fsdp", None),
        P(),
        P(),
        P(),
        P("fsdp", None),
        P("fsdp", None),
        P(),
        P(),
        P(),
        P("fsdp", None),
        P(),
        P("fsdp", None),
        P(),
        rows,
    )
    out_specs = (rows, rows) + (P(),) * 16
    return jax.shard_map(
        functools.partial(per_device, dict(mesh.shape)), mesh=mesh, in_specs=in_specs, out_specs=out_specs, check_vma=False
    )
```

```python
import functools

import jax
import jax.numpy as jnp
from jax import lax
from jax.experimental import pallas as pl
from jax.experimental.pallas import tpu as pltpu
from jax.sharding import PartitionSpec as P

D = 384
HEADS = 6
FF = 1536
POSH = 128
SEQ = 66
TILE = 8
ROWS = TILE * SEQ
STEP = 64
WIN = 80
KEYS = 128
PAIRS = HEADS // 2
GROUP = 8
BACK_GROUP = 24
SUBS = 2
LOG2E = 1.4426950408889634
ROOT_HALF = 0.7071067811865476
PDF = 0.3989422804014327
bf16 = jnp.bfloat16
f32 = jnp.float32

NN = (((1,), (0,)), ((), ()))
NT = (((1,), (1,)), ((), ()))
TN = (((0,), (0,)), ((), ()))


def dot(left, right, dims=NN):
    return lax.dot_general(left, right, dims, preferred_element_type=f32)


def cdf(u):
    return 0.5 + 0.5 * lax.erf(u * ROOT_HALF)


def smooth_slope(u, mass):
    return mass + u * (PDF * jnp.exp2(u * u * (-0.5 * LOG2E)))


def row_mean(values):
    return jnp.sum(values, axis=-1, keepdims=True) * (1.0 / values.shape[-1])


def normalised(values):
    centred = values - row_mean(values)
    scale = lax.rsqrt(row_mean(centred * centred) + 1e-05)
    return centred * scale, scale


def hidden_column(targets):
    windows = []
    for cloud in range(TILE):
        rows = lax.broadcasted_iota(jnp.int32, (WIN, targets.shape[1]), 0) + cloud * STEP
        windows.append(jnp.where(rows == targets[cloud : cloud + 1], 1.0, 0.0))
    blocks = [windows[0][:STEP]]
    for cloud in range(1, TILE):
        blocks += [windows[cloud][:16] + windows[cloud - 1][STEP:], windows[cloud][16:STEP]]
    blocks.append(windows[-1][STEP:])
    return jnp.max(jnp.concatenate(blocks, axis=0), axis=1, keepdims=True)


def lane_mask(rows, odd, kind=bf16):
    lanes = lax.broadcasted_iota(jnp.int32, (rows, 128), 1)
    return (lanes >= 64) if odd else (lanes < 64)


def stacked_heads(tile):
    zero = jnp.zeros_like(tile)
    even = lane_mask(tile.shape[0], False)
    return jnp.concatenate([jnp.where(even, tile, zero), jnp.where(even, zero, tile)], axis=0)


def merged_heads(pair):
    half = pair.shape[0] // 2
    even = lane_mask(half, False)
    return jnp.where(even, pair[:half], pair[half:])


def row_range(rows, low, high, width=128):
    ids = lax.broadcasted_iota(jnp.int32, (rows, width), 0)
    return (ids >= low) & (ids < high)


def spread_heads(flipped):
    none = jnp.zeros((64, flipped.shape[1]), flipped.dtype)
    left = jnp.concatenate([flipped[:64], none], axis=0)
    right = jnp.concatenate([none, flipped[64:]], axis=0)
    return jnp.concatenate([left, right], axis=1)


def head_ones(value):
    rows = lax.broadcasted_iota(jnp.int32, (2 * KEYS, 128), 0) < KEYS
    lanes = lax.broadcasted_iota(jnp.int32, (2 * KEYS, 128), 1) < 64
    return jnp.where(rows == lanes, value, 0.0).astype(bf16)


def lane_ones(value):
    rows = lax.broadcasted_iota(jnp.int32, (128, 2 * KEYS), 0) < 64
    lanes = lax.broadcasted_iota(jnp.int32, (128, 2 * KEYS), 1) < KEYS
    return jnp.where(rows == lanes, value, 0.0).astype(bf16)


def pack_kernel(spot, counts, index, proj, joint, out, up, down, up_bias, *refs):
    vectors, (packed, vec, up_b, targets, early, late, turned) = refs[:8], refs[8:]
    for at, vector in enumerate(vectors):
        vec[at : at + 1, :] = vector[...].reshape(1, D)
    up_b[...] = up_bias[...].reshape(1, FF)
    most, clouds = index.shape
    slots = lax.broadcasted_iota(jnp.int32, (1, 128), 1)
    turned[...] = jnp.zeros(turned.shape, f32)
    turned[:most, :clouds] = index[...].astype(f32)
    chosen = turned[...].T.astype(jnp.int32)
    for cloud in range(clouds):
        first = 1 + SEQ * (cloud % TILE)
        targets[cloud : cloud + 1, :] = jnp.where(slots < counts[cloud], chosen[cloud : cloud + 1, :] + first, -1)
    rows = joint.shape[0]
    for part in range(3):
        early[part * rows : part * rows + rows, :] = joint[:, part * D : part * D + D]
    early[3 * rows :, :] = proj[...]
    late[:rows, :] = out[...]
    for part in range(4):
        late[(part + 1) * rows : (part + 2) * rows, :] = up[:, part * D : part * D + D]
    late[5 * rows : 5 * rows + down.shape[0], :] = down[...]
    half = early.shape[0] // 2
    piece = packed.shape[0] - half
    chips = late.shape[0] // piece // 2
    packed[:half, :] = early[pl.ds(pl.multiple_of((spot[0] % 2) * half, 16), half), :]
    own = (spot[0] % 2) * chips + spot[0] // 2
    packed[half:, :] = late[pl.ds(pl.multiple_of(own * piece, 16), piece), :]


def pack(spot, counts, index, proj, joint, out, up, down, up_bias, vectors, parts):
    rows, low, deep = joint.shape[0], proj.shape[0], down.shape[0]
    size = 3 * rows + low
    late = padded(5 * rows + deep, parts)
    vmem = pl.BlockSpec(memory_space=pltpu.VMEM)
    return pl.pallas_call(
        pack_kernel,
        in_specs=[pl.BlockSpec(memory_space=pltpu.SMEM)] * 2 + [vmem] * 15,
        out_specs=[vmem] * 4,
        out_shape=[
            shape_of((size // 2 + late // parts, D), bf16), shape_of((8, D), f32), shape_of((1, FF), f32),
            shape_of((counts.shape[0], 128), jnp.int32),
        ],
        scratch_shapes=[pltpu.VMEM((size, D), bf16), pltpu.VMEM((late, D), bf16), pltpu.VMEM((128, 128), f32)],
        compiler_params=settings(),
        name="pack",
    )(spot, counts, index, proj, joint, out, up, down, up_bias, *vectors)


def unpack_early(core, mine, other, joint_w, proj):
    groups = mine.shape[0]
    rows, low = D // groups, POSH // groups
    half = (3 * rows + low) // 2

    def place(side, source):
        for group in range(groups):
            at = 0
            while at < half:
                row = side * half + at
                if row < 3 * rows:
                    part, inner = divmod(row, rows)
                    size = min(half - at, rows - inner)
                    first = group * rows + inner
                    joint_w[first : first + size, part * D : part * D + D] = source[group, at : at + size]
                else:
                    size = half - at
                    first = group * low + row - 3 * rows
                    proj[first : first + size, :] = source[group, at : at + size]
                at += size

    @pl.when(core == 0)
    def _():
        place(0, mine)
        place(1, other)

    @pl.when(core == 1)
    def _():
        place(0, other)
        place(1, mine)


def unpack_late(spot, mine, other, near, near_other, lates, out_w, up_w, down_w):
    _, chips, groups, piece, _ = lates.shape
    rows, deep = D // groups, FF // groups
    half = mine.shape[1] - piece
    core, chip = spot % 2, spot // 2
    for side, own, rest in ((core, mine, near), (1 - core, other, near_other)):
        lates[side, chip] = own[:, half:, :]
        for offset, source in enumerate(rest):
            lates[side, chip ^ (offset + 1)] = source[...]
    for at_chip in range(2 * chips):
        for group in range(groups):
            at = 0
            while at < piece:
                row = at_chip * piece + at
                source = lates.at[at_chip // chips, at_chip % chips, group]
                if row < rows:
                    size = min(piece - at, rows - row)
                    first = group * rows + row
                    out_w[first : first + size, :] = source[at : at + size, :]
                elif row < 5 * rows:
                    block, inner = divmod(row - rows, rows)
                    size = min(piece - at, rows - inner)
                    first = group * rows + inner
                    up_w[first : first + size, block * D : block * D + D] = source[at : at + size, :]
                elif row < 5 * rows + deep:
                    inner = row - 5 * rows
                    size = min(piece - at, deep - inner)
                    first = group * deep + inner
                    down_w[first : first + size, :] = source[at : at + size, :]
                else:
                    size = piece - at
                at += size


def picked(rows, first, source):
    ids = lax.broadcasted_iota(jnp.int32, (16, rows), 0) - lax.broadcasted_iota(jnp.int32, (16, rows), 1)
    return dot(jnp.where(ids == first, 1.0, 0.0).astype(bf16), source)


def split16(values):
    high = values.astype(bf16)
    return high, (values - high.astype(f32)).astype(bf16)


def place_inputs(centers, place_weight, place_bias, cen, place_w):
    for tile in range(cen.shape[0]):
        high, rest = split16(centers[:, tile * ROWS : tile * ROWS + ROWS])
        ids = lax.broadcasted_iota(jnp.int32, (16, ROWS), 0)
        ones = jnp.where((ids == 9) | (ids == 10), 1.0, 0.0)
        cen[tile] = (picked(3, 0, high) + picked(3, 3, rest) + picked(3, 6, high) + ones).astype(bf16)
    high, rest = split16(place_weight[...])
    bias_high, bias_rest = split16(place_bias[...])
    value = picked(3, 0, high) + picked(3, 3, high) + picked(3, 6, rest) + picked(1, 9, bias_high) + picked(1, 10, bias_rest)
    place_w[...] = value.astype(bf16)


def front_kernel(core, tokens, centers, targets, vec, place_weight, place_bias, mine, other,
                 entry, joint, mixture, shares, weights, joint_w, proj, cen, place_w, qkv):
    step = pl.program_id(0)

    @pl.when(step == 0)
    def _():
        for sub in range(SUBS):
            qkv[sub, ROWS:, :] = jnp.zeros((qkv.shape[1] - ROWS, 3 * D), bf16)
        unpack_early(core[0], mine, other, joint_w, proj)
        place_inputs(centers, place_weight, place_bias, cen, place_w)

    lanes = lax.broadcasted_iota(jnp.int32, (1, 2 * KEYS), 1) % KEYS
    sums_of = head_ones(1.0)
    none = jnp.zeros((16, 2 * KEYS), bf16)
    scale_row = jnp.where(lax.broadcasted_iota(jnp.int32, (1, 3 * D), 1) < D, 0.125 * LOG2E, 1.0)

    def normal_rows(sub):
        span = slice(sub * ROWS, sub * ROWS + ROWS)
        pre = dot(cen[step * SUBS + sub], place_w[...], TN)
        low = (pre * cdf(pre)).astype(bf16)
        placed = dot(low, proj[...]) + vec[1:2, :]
        hidden = hidden_column(targets[sub * TILE : sub * TILE + TILE, :])
        rows = jnp.where(hidden > 0.5, vec[0:1, :], tokens[span, :].astype(f32)) + placed
        entry[span, :] = rows.astype(bf16)
        unit, _ = normalised(rows)
        return (unit * vec[2:3, :] + vec[3:4, :]).astype(bf16)

    def project(sub, normed, first):
        cols = slice(first, min(first + 256, 3 * D))
        value = (dot(normed, joint_w[:, cols]) * scale_row[:, cols]).astype(bf16)
        qkv[sub, :ROWS, cols] = value
        joint[sub * ROWS : sub * ROWS + ROWS, cols] = value

    def score(sub, pair, cloud):
        base = cloud * STEP
        query = qkv[sub, base : base + WIN, pair * 128 : pair * 128 + 128]
        key = qkv[sub, base : base + KEYS, D + pair * 128 : D + pair * 128 + 128]
        return dot(query, spread_heads(key.T))

    def exponentials(cloud, scores):
        live = (lanes >= 2 * cloud) & (lanes < 2 * cloud + SEQ - 1)
        scores = jnp.where(live, scores, -1e30)
        parts = []
        for half in (scores[:, :KEYS], scores[:, KEYS:]):
            parts.append(jnp.exp2(half - jnp.max(half, axis=-1, keepdims=True)).astype(bf16))
        return jnp.concatenate(parts, axis=1)

    def mixed(sub, pair, cloud, e):
        base = cloud * STEP
        value = qkv[sub, base : base + KEYS, 2 * D + pair * 128 : 2 * D + pair * 128 + 128]
        return dot(e, jnp.concatenate([stacked_heads(value), sums_of], axis=1))

    tails = {}

    def store(sub, pair, cloud, e, both):
        base = sub * ROWS + cloud * STEP
        cols = slice(pair * 128, pair * 128 + 128)
        share = 1.0 / both[:, 128:]
        mix = both[:, :128] * share
        spot = slice(pair * 256, pair * 256 + 256)
        at = sub * TILE + cloud
        weights[at, :16, spot] = jnp.where(row_range(16, 2 * cloud, 16, 256), e[:16], none)
        weights[at, 16:64, spot] = e[16:64]
        weights[at, 64:80, spot] = jnp.where(row_range(16, 0, 2 * cloud + 2, 256), e[64:80], none)
        head_mix, head_share = mix[:16], share[:16]
        if cloud:
            head = row_range(16, 0, 2 * cloud)
            tail_mix, tail_share = tails[sub, pair]
            head_mix = jnp.where(head, tail_mix, head_mix)
            head_share = jnp.where(head, tail_share, head_share)
        mixture[base : base + 16, cols] = head_mix.astype(bf16)
        shares[base : base + 16, cols] = head_share.astype(bf16)
        mixture[base + 16 : base + 64, cols] = mix[16:64].astype(bf16)
        shares[base + 16 : base + 64, cols] = share[16:64].astype(bf16)
        tails[sub, pair] = (mix[64:], share[64:])
        if cloud == TILE - 1:
            mixture[base + 64 : base + 80, cols] = mix[64:].astype(bf16)
            shares[base + 64 : base + 80, cols] = share[64:].astype(bf16)

    jobs = [(pair, cloud) for pair in range(PAIRS) for cloud in range(TILE)]
    groups = [jobs[at : at + GROUP] for at in range(0, len(jobs), GROUP)]
    normed = [normal_rows(sub) for sub in range(SUBS)]
    chunks = range(0, 3 * D, 256)
    for first in chunks:
        project(0, normed[0], first)
    waiting = None
    for sub in range(SUBS):
        fill = [functools.partial(project, sub + 1, normed[sub + 1], first) for first in chunks] if sub + 1 < SUBS else []
        share_of = -(-len(fill) // len(groups))
        for group in groups:
            exps = [exponentials(cloud, score(sub, pair, cloud)) for pair, cloud in group]
            for task in fill[:share_of]:
                task()
            fill = fill[share_of:]
            if waiting:
                close_group(mixed, store, *waiting)
            waiting = (sub, group, exps)
    close_group(mixed, store, *waiting)


def close_group(mixed, store, sub, group, exps):
    boths = [mixed(sub, pair, cloud, e) for (pair, cloud), e in zip(group, exps)]
    for (pair, cloud), e, both in zip(group, exps, boths):
        store(sub, pair, cloud, e, both)


def whole(shape):
    return pl.BlockSpec(shape, lambda i: (0,) * len(shape))


def rows_of(width, rows=ROWS):
    return pl.BlockSpec((rows, width), lambda i: (i, 0))


def slab(shape):
    return pl.BlockSpec((1, *shape), lambda i: (i,) + (0,) * len(shape))


def shape_of(dims, kind):
    return jax.ShapeDtypeStruct(dims, kind)


def cost(microseconds):
    return pl.CostEstimate(flops=int(microseconds * 9e8), bytes_accessed=int(microseconds * 2e6), transcendentals=0)


def settings(megabytes=60):
    return pltpu.CompilerParams(vmem_limit_bytes=megabytes * 2**20)


def front(core, tokens, centers, targets, vec, place_weight, place_bias, mine, other):
    count = tokens.shape[0]
    steps = count // ROWS
    rows = SUBS * ROWS
    return pl.pallas_call(
        front_kernel,
        grid=(steps // SUBS,),
        in_specs=[
            pl.BlockSpec(memory_space=pltpu.SMEM), rows_of(D, rows), whole(centers.shape),
            pl.BlockSpec((SUBS * TILE, 128), lambda i: (i, 0)), whole((8, D)),
            whole((3, POSH)), whole((1, POSH)), whole(mine.shape), whole(other.shape),
        ],
        out_specs=[
            rows_of(D, rows), rows_of(3 * D, rows), rows_of(D, rows), rows_of(D, rows),
            pl.BlockSpec((SUBS * TILE, WIN, HEADS * KEYS), lambda i: (i, 0, 0)), whole((D, 3 * D)), whole((POSH, D)),
            whole((steps, 16, ROWS)), whole((16, POSH)),
        ],
        out_shape=[
            shape_of((count, D), bf16), shape_of((count, 3 * D), bf16),
            shape_of((count, D), bf16), shape_of((count, D), bf16),
            shape_of((steps * TILE, WIN, HEADS * KEYS), bf16), shape_of((D, 3 * D), bf16), shape_of((POSH, D), bf16),
            shape_of((steps, 16, ROWS), bf16), shape_of((16, POSH), bf16),
        ],
        scratch_shapes=[pltpu.VMEM((SUBS, ROWS + 48, 3 * D), bf16)],
        compiler_params=settings(),
        cost_estimate=cost(28),
        name="front",
    )(core, tokens, centers, targets, vec, place_weight, place_bias, mine, other)


def write_sums(sums, order, first, values):
    size = sums.shape[0] // len(order)
    at = 0
    while at < values.shape[0]:
        row = first + at
        segment, inner = divmod(row, size)
        step = min(size - inner, values.shape[0] - at)
        spot = order[segment] * size + inner
        sums[spot : spot + step, :] = values[at : at + step].astype(bf16)
        at += step


def share_halves(core, sums, kept, sent):
    half = sent.shape[0]
    kept[...] = sums[pl.ds(pl.multiple_of(core * half, 16), half), :]
    sent[...] = sums[pl.ds(pl.multiple_of((1 - core) * half, 16), half), :]


def padded(rows, size):
    return -(-rows // (16 * size)) * 16 * size


def middle_kernel(chunk, order, spot, entry, mixture, shares, cot, vec, up_b, mine, other, *refs):
    chips = len(order) // 2
    near, near_other, refs = refs[: chips - 1], refs[chips - 1 : 2 * chips - 2], refs[2 * chips - 2 :]
    (output, mid_grad, mix_grad, kept, sent, up_bg, vec_g,
     down_acc, up_acc, out_acc, out_w, up_w, down_w, gated, sums, lates) = refs
    step = pl.program_id(0)

    @pl.when(step == 0)
    def _():
        unpack_late(spot[0], mine, other, near, near_other, lates, out_w, up_w, down_w)
        for ref in (down_acc, up_acc, out_acc, up_bg, vec_g):
            ref[...] = jnp.zeros(ref.shape, ref.dtype)

    parts = FF // chunk
    spans = [slice(part * chunk, part * chunk + chunk) for part in range(parts)]
    mix = mixture[...]
    cotangent = cot[...]
    mid = entry[...].astype(f32) + (dot(mix, out_w[...]) + vec[4:5, :])
    gates = [dot(cotangent, down_w[spans[0], :], NT)]
    unit, scale = normalised(mid)
    normed = (unit * vec[5:6, :] + vec[6:7, :]).astype(bf16)
    lows = []

    def down_part(part):
        down_acc[:, spans[part]] += dot(cotangent, gated[:, spans[part]], TN)

    def up_part(part):
        up_acc[:, spans[part]] += dot(normed, lows[part], TN)

    for part in range(parts):
        cols = spans[part]
        raised = dot(normed, up_w[:, cols]) + up_b[:, cols]
        if part + 1 < parts:
            gates.append(dot(cotangent, down_w[spans[part + 1], :], NT))
        mass = cdf(raised)
        gated[:, cols] = (raised * mass).astype(bf16)
        grad = gates[part] * smooth_slope(raised, mass)
        up_bg[:, cols] += jnp.sum(grad, axis=0, keepdims=True)
        lows.append(grad.astype(bf16))
        if part:
            down_part(part - 1)
            if part > 1:
                up_part(part - 2)
    back = dot(jnp.concatenate(lows, axis=1), up_w[...], NT)
    up_part(parts - 2)
    down_part(parts - 1)
    up_part(parts - 1)
    output[...] = (mid + (dot(gated[...], down_w[...]) + vec[7:8, :])).astype(bf16)
    upstream = cotangent.astype(f32)
    tilted = back * vec[5:6, :]
    grad = upstream + scale * (tilted - row_mean(tilted) - unit * row_mean(tilted * unit))
    low = grad.astype(bf16)
    mid_grad[...] = low
    mix_grad[...] = (dot(low, out_w[...], NT) * shares[...].astype(f32)).astype(bf16)
    out_acc[...] += dot(mix, low, TN)
    vec_g[0:1, :] += jnp.sum(back * unit, axis=0, keepdims=True)
    vec_g[1:2, :] += jnp.sum(back, axis=0, keepdims=True)
    vec_g[2:3, :] += jnp.sum(grad, axis=0, keepdims=True)
    vec_g[3:4, :] += jnp.sum(upstream, axis=0, keepdims=True)

    @pl.when(step == pl.num_programs(0) - 1)
    def _():
        for part in range(4):
            write_sums(sums, order, part * D, up_acc[:, part * D : part * D + D])
        write_sums(sums, order, 4 * D, down_acc[...].T)
        write_sums(sums, order, 8 * D, out_acc[...])
        if sums.shape[0] > 9 * D:
            write_sums(sums, order, 9 * D, jnp.zeros((sums.shape[0] - 9 * D, D), f32))
        share_halves(spot[0] % 2, sums, kept, sent)


def middle_part(spot, entry, mixture, shares, cot, vec, up_b, mine, other, near, near_other, order, rows=704, chunk=768):
    count = entry.shape[0]
    size = padded(9 * D, len(order))
    return pl.pallas_call(
        functools.partial(middle_kernel, chunk, order),
        grid=(count // rows,),
        in_specs=[
            pl.BlockSpec(memory_space=pltpu.SMEM), rows_of(D, rows), rows_of(D, rows), rows_of(D, rows), rows_of(D, rows),
            whole((8, D)), whole((1, FF)), whole(mine.shape), whole(other.shape),
        ]
        + [whole(piece.shape) for piece in [*near, *near_other]],
        out_specs=[
            rows_of(D, rows), rows_of(D, rows), rows_of(D, rows),
            whole((size // 2, D)), whole((size // 2, D)), whole((1, FF)), whole((8, D)),
        ],
        out_shape=[
            shape_of((count, D), bf16), shape_of((count, D), bf16), shape_of((count, D), bf16),
            shape_of((size // 2, D), bf16), shape_of((size // 2, D), bf16), shape_of((1, FF), f32), shape_of((8, D), f32),
        ],
        scratch_shapes=[
            pltpu.VMEM((D, FF), f32), pltpu.VMEM((D, FF), f32), pltpu.VMEM((D, D), f32),
            pltpu.VMEM((D, D), bf16), pltpu.VMEM((D, FF), bf16), pltpu.VMEM((FF, D), bf16),
            pltpu.VMEM((rows, FF), bf16), pltpu.VMEM((size, D), bf16),
            pltpu.VMEM((2, len(order) // 2, *near[0].shape), bf16),
        ],
        compiler_params=settings(),
        cost_estimate=cost(55),
        name="middle",
    )(spot, entry, mixture, shares, cot, vec, up_b, mine, other, *near, *near_other)


def back_kernel(is_first, is_last, order, *refs):
    entry, joint, mixture, weights, mix_grad, mid_grad, cen, targets, vec, place_w, proj, joint_w = refs[:12]
    refs = refs[12:]
    if not is_first:
        before, refs = refs[1:5], refs[5:]
    if is_last:
        core, up_bg, mid_vec_g, tokens_g, kept, sent, joint_g, proj_g, place_g, vec_g, qkv, dqkv, sums = refs
    else:
        tokens_g, joint_g, proj_g, place_g, vec_g, qkv, dqkv = refs
    step = pl.program_id(0)

    @pl.when(step == 0)
    def _():
        for at, ref in enumerate((joint_g, proj_g, place_g, vec_g)):
            ref[...] = jnp.zeros(ref.shape, ref.dtype) if is_first else before[at][...]
        qkv[ROWS:, :] = jnp.zeros((qkv.shape[0] - ROWS, 3 * D), bf16)

    qkv[:ROWS, :] = joint[...]
    pre = dot(cen[0], place_w[...], TN)
    unit, scale = normalised(entry[...].astype(f32))
    normed = (unit * vec[2:3, :] + vec[3:4, :]).astype(bf16)
    minus = lane_ones(-1.0)
    jobs = [(pair, cloud) for pair in range(PAIRS) for cloud in range(TILE)]
    tails = {}
    for at in range(0, len(jobs), BACK_GROUP):
        group = jobs[at : at + BACK_GROUP]
        gaps = []
        for pair, cloud in group:
            base = cloud * STEP
            window = slice(base, base + WIN)
            cols = slice(pair * 128, pair * 128 + 128)
            value = qkv[base : base + KEYS, 2 * D + pair * 128 : 2 * D + pair * 128 + 128]
            dmw = mix_grad[window, cols]
            left = jnp.concatenate([dmw, dmw * mixture[window, cols]], axis=1)
            gaps.append(dot(left, jnp.concatenate([spread_heads(value.T), minus], axis=0)))
        es, dss = [], []
        for (pair, cloud), gap in zip(group, gaps):
            e = weights[cloud, :, pair * 256 : pair * 256 + 256]
            es.append(e)
            dss.append((e.astype(f32) * gap).astype(bf16))
        results = []
        for (pair, cloud), e, ds in zip(group, es, dss):
            base = cloud * STEP
            query = stacked_heads(qkv[base : base + WIN, pair * 128 : pair * 128 + 128])
            key = stacked_heads(qkv[base : base + KEYS, D + pair * 128 : D + pair * 128 + 128])
            sdm = stacked_heads(mix_grad[base : base + WIN, pair * 128 : pair * 128 + 128])
            e = jnp.concatenate([e[:, :KEYS], e[:, KEYS:]], axis=0)
            tall = jnp.concatenate([ds[:, :KEYS], ds[:, KEYS:]], axis=0)
            results.append((dot(ds, key), dot(tall[:, :WIN], query, TN), dot(e[:, :WIN], sdm, TN)))
        for (pair, cloud), (dq, dk, dv) in zip(group, results):
            base = cloud * STEP
            parts = (dq * 0.125, dk * (1.0 / LOG2E), dv)
            for which, part in enumerate(parts):
                cols = slice(which * D + pair * 128, which * D + pair * 128 + 128)
                head = part[:16]
                if cloud:
                    head = jnp.where(row_range(16, 0, 2 * cloud), tails[pair, which], head)
                dqkv[base : base + 16, cols] = head.astype(bf16)
                dqkv[base + 16 : base + 64, cols] = part[16:64].astype(bf16)
                tails[pair, which] = part[64:80]
                if cloud == TILE - 1:
                    dqkv[ROWS - 16 :, cols] = part[64:80].astype(bf16)


    back = dot(dqkv[...], joint_w[...], NT)
    joint_g[...] += dot(normed, dqkv[...], TN)
    tilted = back * vec[2:3, :]
    grad = mid_grad[...].astype(f32) + scale * (tilted - row_mean(tilted) - unit * row_mean(tilted * unit))
    low = grad.astype(bf16)
    mass = cdf(pre)
    place_low = (pre * mass).astype(bf16)
    pre_grad = dot(low, proj[...], NT) * smooth_slope(pre, mass)
    proj_g[...] += dot(place_low, low, TN)
    hidden = hidden_column(targets[...])
    marked = jnp.where(hidden > 0.5, grad, 0.0)
    tokens_g[...] = (grad - marked).astype(bf16)
    high_part = pre_grad.astype(bf16)
    low_part = (pre_grad - high_part.astype(f32)).astype(bf16)
    place_g[...] += dot(cen[0], jnp.concatenate([high_part, low_part], axis=1))
    vec_g[0:1, :] += jnp.sum(marked, axis=0, keepdims=True)
    vec_g[1:2, :] += jnp.sum(grad, axis=0, keepdims=True)
    vec_g[2:3, :] += jnp.sum(back * unit, axis=0, keepdims=True)
    vec_g[3:4, :] += jnp.sum(back, axis=0, keepdims=True)
    if not is_last:
        return

    @pl.when(step == pl.num_programs(0) - 1)
    def _():
        for part in range(3):
            write_sums(sums, order, part * D, joint_g[:, part * D : part * D + D])
        write_sums(sums, order, 3 * D, proj_g[...])
        place = place_g[:, :POSH] + place_g[:, POSH:]
        place_weight = place[0:3] + place_g[3:6, :POSH]
        small = jnp.concatenate(
            [
                vec_g[0:4, :],
                mid_vec_g[0:4, :],
                jnp.concatenate([place_weight[0:1], place_weight[1:2], place_weight[2:3]], axis=1),
                jnp.concatenate([place[9:10], jnp.zeros((1, D - POSH), f32)], axis=1),
                jnp.concatenate([up_bg[:, part * D : part * D + D] for part in range(4)], axis=0),
                jnp.zeros((sums.shape[0] - 3 * D - POSH - 14, D), f32),
            ],
            axis=0,
        )
        write_sums(sums, order, 3 * D + POSH, small)
        share_halves(core[0], sums, kept, sent)


def back_part(given, first, steps, order, before=None, extra=None):
    count = given[0].shape[0]

    def shifted(width):
        return pl.BlockSpec((ROWS, width), lambda i: (i + first, 0))

    def shifted_slab(shape):
        return pl.BlockSpec((1, *shape), lambda i: (i + first, 0, 0))

    accs = [(D, 3 * D), (POSH, D), (16, 256), (8, D)]
    in_specs = [
        shifted(D), shifted(3 * D), shifted(D),
        pl.BlockSpec((TILE, WIN, HEADS * KEYS), lambda i: (i + first, 0, 0)),
        shifted(D), shifted(D), shifted_slab((16, ROWS)),
        pl.BlockSpec((TILE, 128), lambda i: (i + first, 0)),
        whole((8, D)), whole((16, POSH)), whole((POSH, D)), whole((D, 3 * D)),
    ]
    given = list(given)
    if before is not None:
        given += before
        in_specs += [pl.BlockSpec(memory_space=pl.ANY)] + [whole(acc) for acc in accs]
    out_specs, out_shape = [shifted(D)], [shape_of((count, D), bf16)]
    scratch = [pltpu.VMEM((ROWS + 48, 3 * D), bf16), pltpu.VMEM((ROWS, 3 * D), bf16)]
    if extra is not None:
        given += extra
        in_specs += [pl.BlockSpec(memory_space=pltpu.SMEM), whole((1, FF)), whole((8, D))]
        size = padded(3 * D + POSH + 16, len(order))
        out_specs += [whole((size // 2, D))] * 2
        out_shape += [shape_of((size // 2, D), bf16)] * 2
        scratch = [pltpu.VMEM(acc, f32) for acc in accs] + scratch + [pltpu.VMEM((size, D), bf16)]
    else:
        out_specs += [whole(acc) for acc in accs]
        out_shape += [shape_of(acc, f32) for acc in accs]
    return pl.pallas_call(
        functools.partial(back_kernel, before is None, extra is not None, order),
        grid=(steps,),
        in_specs=in_specs,
        out_specs=out_specs,
        out_shape=out_shape,
        scratch_shapes=scratch,
        input_output_aliases={} if before is None else {12: 0},
        compiler_params=settings(),
        cost_estimate=cost(5 * steps),
        name="back",
    )(*given)


def gather_pieces(spot, offsets, pieces, sums):
    segment = pieces[0].shape[0] // len(offsets)
    chips = len(offsets)
    for core, piece in enumerate(pieces):
        for at, offset in enumerate(offsets):
            holder = spot ^ offset ^ core
            row = pl.multiple_of(((holder % 2) * chips + holder // 2) * segment, 16)
            sums[pl.ds(row, segment), :] = piece[at * segment : at * segment + segment, :]


def widen_kernel(offsets, spot, *refs):
    pieces, (up_g, down_g, out_g, sums) = refs[:2], refs[2:]
    step = pl.program_id(0)

    @pl.when(step == 0)
    def _():
        gather_pieces(spot[0], offsets, pieces, sums)
        out_g[...] = sums[8 * D : 9 * D, :].astype(f32)

    up_g[...] = sums[pl.ds(pl.multiple_of(step * D, 16), D), :].astype(f32)
    down_g[...] = sums[pl.ds(pl.multiple_of((step + 4) * D, 16), D), :].astype(f32)


def close_kernel(offsets, spot, *refs):
    pieces, (joint_g, proj_g, place_g, *small), last = refs[:2], refs[2:-1], refs[-1]
    step = pl.program_id(0)

    @pl.when(step == 0)
    def _():
        gather_pieces(spot[0], offsets, pieces, last)
        proj_g[...] = last[3 * D : 3 * D + POSH, :].astype(f32)
        rows = last[3 * D + POSH : 3 * D + POSH + 16, :].astype(f32)
        for part in range(3):
            place_g[part : part + 1, :] = rows[8:9, part * POSH : part * POSH + POSH]
        small[0][...] = rows[9:10, :POSH].reshape(POSH)
        small[1][...] = jnp.concatenate([rows[10 + part : 11 + part] for part in range(4)], axis=1).reshape(FF)
        for at in range(8):
            small[2 + at][...] = rows[at : at + 1].reshape(D)

    joint_g[...] = last[pl.ds(pl.multiple_of(step * D, 16), D), :].astype(f32)


def one(shape):
    return pl.BlockSpec(shape, lambda i: (0,) * len(shape))


def unpacked(kernel, name, steps, shapes, specs, spot, offsets, values):
    return pl.pallas_call(
        functools.partial(kernel, offsets),
        grid=(steps,),
        in_specs=[pl.BlockSpec(memory_space=pltpu.SMEM)] + [one(value.shape) for value in values],
        out_specs=specs,
        out_shape=[shape_of(shape, f32) for shape in shapes],
        scratch_shapes=[pltpu.VMEM((values[0].shape[0] * 2, D), bf16)],
        compiler_params=settings(24),
        cost_estimate=cost(4),
        name=name,
    )(spot, *values)


def widen(spot, offsets, values):
    specs = [pl.BlockSpec((D, D), lambda i: (0, i)), pl.BlockSpec((D, D), lambda i: (i, 0)), one((D, D))]
    return unpacked(widen_kernel, "widen", 4, [(D, FF), (FF, D), (D, D)], specs, spot, offsets, values)


def close(spot, offsets, values):
    shapes = [(POSH, D), (3, POSH), (POSH,), (FF,)] + [(D,)] * 8
    specs = [pl.BlockSpec((D, D), lambda i: (0, i))] + [one(shape) for shape in shapes]
    return unpacked(close_kernel, "close", 3, [(D, 3 * D)] + shapes, specs, spot, offsets, values)


def bits_of(size):
    return [1 << bit for bit in range(size.bit_length() - 1)]


def chip_bits(size):
    bits = bits_of(size)[:0:-1]
    return [bits[at : at + 2] for at in range(0, len(bits), 2)]


def offsets_of(bits):
    found = [0]
    for bit in reversed(bits):
        found += [offset + bit for offset in found]
    return found


def swapped(values, offset, size):
    return lax.ppermute(values, "dp", [(i, i ^ offset) for i in range(size)])


def total(terms):
    return sum(term.astype(f32) for term in terms).astype(bf16)


def scattered(terms, bits, size):
    offsets = offsets_of(bits)
    mine = (lax.axis_index("dp") // bits[-1]) % len(offsets)
    parts = [term.reshape(len(offsets), -1, D) for term in terms]

    def part(offset):
        return [lax.dynamic_index_in_dim(term, mine ^ (offset // bits[-1]), 0, keepdims=False) for term in parts]

    return part(0) + [swapped(total(part(offset)), offset, size) for offset in offsets[1:]]


def joined(pieces, bits, size):
    found = dict(pieces)
    for offset in offsets_of(bits)[1:]:
        for held, piece in pieces.items():
            found[held ^ offset] = swapped(piece, offset, size)
    return found


def crossed(values, offset, size):
    return lax.ppermute(values, "fsdp", [(i, i ^ offset) for i in range(size)])


def tied(first, second):
    return lax.optimization_barrier((first, second))


def after(value, other):
    return lax.optimization_barrier((value, other))[0]


def per_device(
    sizes,
    tokens,
    centers,
    mask_count,
    mask_index,
    mask_embed,
    place_weight,
    place_bias,
    place_proj,
    place_shift,
    norm_gain,
    norm_shift,
    joint_weight,
    out_weight,
    out_bias,
    mlp_gain,
    mlp_shift,
    up_weight,
    up_bias,
    down_weight,
    down_bias,
    cotangent,
):
    dp, fsdp = sizes["dp"], sizes["fsdp"]
    spot = lax.axis_index("dp").astype(jnp.int32)[None]
    core = spot % 2
    vectors = (mask_embed, place_shift, norm_gain, norm_shift, out_bias, mlp_gain, mlp_shift, down_bias)
    packed, vec, up_b, targets = pack(
        spot, mask_count, mask_index.T, place_proj, joint_weight, out_weight, up_weight, down_weight, up_bias, vectors, dp
    )
    packed = lax.all_gather(packed, "fsdp", axis=0)
    packed_other = swapped(packed, 1, dp)
    half = (3 * joint_weight.shape[0] + place_proj.shape[0]) // 2
    late = packed[:, half:]
    pieces = [swapped(late, 2 * offset, dp) for offset in range(1, dp // 2)]
    entry, joint, mixture, shares, weights, joint_w, proj, cen, place_w = front(
        core, tokens, centers, targets, vec, place_weight, place_bias[None, :], packed, packed_other
    )
    pieces, mixture = tied(pieces, mixture)
    pieces_other = [swapped(piece, 1, dp) for piece in pieces]
    order = list(range(dp))
    output, mid_grad, mix_grad, kept, sent, up_bg, vec_g = middle_part(
        spot, entry, mixture, shares, cotangent, vec, up_b, packed, packed_other, pieces, pieces_other, order
    )
    chips = chip_bits(dp)
    near, far = [offset % fsdp for offset in (1, 2)]
    sums = [kept, swapped(sent, 1, dp)]
    mix_grad, sums[-1] = tied(mix_grad, sums[-1])
    sums = scattered(sums, chips[0], dp)
    given = [entry, joint, mixture, weights, mix_grad, mid_grad, cen, targets, vec, place_w, proj, joint_w]
    steps = tokens.shape[0] // ROWS
    early_steps = steps // 2
    before = list(back_part(given, 0, early_steps, order))
    for bits in chips[1:]:
        sums = scattered(sums, bits, dp)
    sums[-1], before[0] = tied(sums[-1], before[0])
    middle_row = sums[0].shape[0] // 2
    upper = total([term[:middle_row] for term in sums])
    lower = total([term[middle_row:] for term in sums])
    upper_got, lower_got = crossed(upper, near, fsdp), crossed(lower, far, fsdp)
    given[4] = after(given[4], lower)
    tokens_grad, kept, sent = back_part(given, early_steps, steps - early_steps, order, before, [core, up_bg, vec_g])
    sent, upper_got, lower_got = lax.optimization_barrier((sent, upper_got, lower_got))
    upper, lower = total([upper, upper_got]), total([lower, lower_got])
    upper_got, lower_got = crossed(upper, far, fsdp), crossed(lower, near, fsdp)
    last = [kept, swapped(sent, 1, dp)]
    last = scattered(last, chips[0], dp)
    upper_got = after(upper_got, last[-1])
    sums = {0: jnp.concatenate([total([upper, upper_got]), total([lower, lower_got])], axis=0)}
    for bits in chips[1:]:
        last = scattered(last, bits, dp)
    value = total(last)
    near_got = after(crossed(value, near, fsdp), sums[0])
    for bits in reversed(chips):
        sums = joined(sums, bits, dp)
    value = total([value, near_got])
    far_got = crossed(value, far, fsdp)
    soonest = list(sums)[1]
    far_got, sums[soonest] = tied(far_got, sums[soonest])
    last = {0: total([value, far_got])}
    for bits in reversed(chips):
        last = joined(last, bits, dp)
    held = jnp.concatenate(list(sums.values()), axis=0)
    up_grad, down_grad, out_grad = widen(spot, list(sums), [held, swapped(held, 1, dp)])
    newest = list(last)[-1]
    last[newest] = after(last[newest], out_grad)
    held = jnp.concatenate(list(last.values()), axis=0)
    joint_grad, proj_grad, place_weight_grad, place_bias_grad, up_bias_grad, *small = close(
        spot, list(last), [held, swapped(held, 1, dp)]
    )
    return (
        output,
        tokens_grad,
        small[0],
        place_weight_grad,
        place_bias_grad,
        proj_grad,
        small[1],
        small[2],
        small[3],
        joint_grad,
        out_grad,
        small[6],
        small[4],
        small[5],
        up_grad,
        up_bias_grad,
        down_grad,
        small[7],
    )


def solution(mesh):
    rows = P(("dp", "fsdp"), None)
    in_specs = (
        rows,
        P(None, ("dp", "fsdp")),
        P(("dp", "fsdp")),
        rows,
        P(),
        P(),
        P(),
        P("fsdp", None),
        P(),
        P(),
        P(),
        P("fsdp", None),
        P("fsdp", None),
        P(),
        P(),
        P(),
        P("fsdp", None),
        P(),
        P("fsdp", None),
        P(),
        rows,
    )
    out_specs = (rows, rows) + (P(),) * 16
    return jax.shard_map(
        functools.partial(per_device, dict(mesh.shape)), mesh=mesh, in_specs=in_specs, out_specs=out_specs, check_vma=False
    )
```

```python
import functools

import jax
import jax.numpy as jnp
from jax import lax
from jax.experimental import pallas as pl
from jax.experimental.pallas import tpu as pltpu
from jax.sharding import PartitionSpec as P

D = 384
HEADS = 6
FF = 1536
POSH = 128
SEQ = 66
TILE = 8
ROWS = TILE * SEQ
STEP = 64
WIN = 80
KEYS = 128
PAIRS = HEADS // 2
GROUP = 8
BACK_GROUP = 24
SUBS = 2
LOG2E = 1.4426950408889634
ROOT_HALF = 0.7071067811865476
PDF = 0.3989422804014327
bf16 = jnp.bfloat16
f32 = jnp.float32

NN = (((1,), (0,)), ((), ()))
NT = (((1,), (1,)), ((), ()))
TN = (((0,), (0,)), ((), ()))


def dot(left, right, dims=NN):
    return lax.dot_general(left, right, dims, preferred_element_type=f32)


def cdf(u):
    return 0.5 + 0.5 * lax.erf(u * ROOT_HALF)


def smooth_slope(u, mass):
    return mass + u * (PDF * jnp.exp2(u * u * (-0.5 * LOG2E)))


def row_mean(values):
    return jnp.sum(values, axis=-1, keepdims=True) * (1.0 / values.shape[-1])


def normalised(values):
    centred = values - row_mean(values)
    scale = lax.rsqrt(row_mean(centred * centred) + 1e-05)
    return centred * scale, scale


def hidden_column(targets):
    windows = []
    for cloud in range(TILE):
        rows = lax.broadcasted_iota(jnp.int32, (WIN, targets.shape[1]), 0) + cloud * STEP
        windows.append(jnp.where(rows == targets[cloud : cloud + 1], 1.0, 0.0))
    blocks = [windows[0][:STEP]]
    for cloud in range(1, TILE):
        blocks += [windows[cloud][:16] + windows[cloud - 1][STEP:], windows[cloud][16:STEP]]
    blocks.append(windows[-1][STEP:])
    return jnp.max(jnp.concatenate(blocks, axis=0), axis=1, keepdims=True)


def lane_mask(rows, odd, kind=bf16):
    lanes = lax.broadcasted_iota(jnp.int32, (rows, 128), 1)
    return (lanes >= 64) if odd else (lanes < 64)


def stacked_heads(tile):
    zero = jnp.zeros_like(tile)
    even = lane_mask(tile.shape[0], False)
    return jnp.concatenate([jnp.where(even, tile, zero), jnp.where(even, zero, tile)], axis=0)


def merged_heads(pair):
    half = pair.shape[0] // 2
    even = lane_mask(half, False)
    return jnp.where(even, pair[:half], pair[half:])


def row_range(rows, low, high, width=128):
    ids = lax.broadcasted_iota(jnp.int32, (rows, width), 0)
    return (ids >= low) & (ids < high)


def spread_heads(flipped):
    none = jnp.zeros((64, flipped.shape[1]), flipped.dtype)
    left = jnp.concatenate([flipped[:64], none], axis=0)
    right = jnp.concatenate([none, flipped[64:]], axis=0)
    return jnp.concatenate([left, right], axis=1)


def head_ones(value):
    rows = lax.broadcasted_iota(jnp.int32, (2 * KEYS, 128), 0) < KEYS
    lanes = lax.broadcasted_iota(jnp.int32, (2 * KEYS, 128), 1) < 64
    return jnp.where(rows == lanes, value, 0.0).astype(bf16)


def block_ones():
    rows = lax.broadcasted_iota(jnp.int32, (2 * KEYS, 2 * KEYS), 0) < KEYS
    lanes = lax.broadcasted_iota(jnp.int32, (2 * KEYS, 2 * KEYS), 1) < KEYS
    return jnp.where(rows == lanes, 1.0, 0.0).astype(bf16)


def pack_kernel(spot, counts, index, proj, joint, out, up, down, up_bias, *refs):
    vectors, (packed, vec, up_b, targets, early, late, turned) = refs[:8], refs[8:]
    for at, vector in enumerate(vectors):
        vec[at : at + 1, :] = vector[...].reshape(1, D)
    up_b[...] = up_bias[...].reshape(1, FF)
    most, clouds = index.shape
    slots = lax.broadcasted_iota(jnp.int32, (1, 128), 1)
    turned[...] = jnp.zeros(turned.shape, f32)
    turned[:most, :clouds] = index[...].astype(f32)
    chosen = turned[...].T.astype(jnp.int32)
    for cloud in range(clouds):
        first = 1 + SEQ * (cloud % TILE)
        targets[cloud : cloud + 1, :] = jnp.where(slots < counts[cloud], chosen[cloud : cloud + 1, :] + first, -1)
    rows = joint.shape[0]
    for part in range(3):
        early[part * rows : part * rows + rows, :] = joint[:, part * D : part * D + D]
    early[3 * rows :, :] = proj[...]
    late[:rows, :] = out[...]
    for part in range(4):
        late[(part + 1) * rows : (part + 2) * rows, :] = up[:, part * D : part * D + D]
    late[5 * rows : 5 * rows + down.shape[0], :] = down[...]
    half = early.shape[0] // 2
    piece = packed.shape[0] - half
    chips = late.shape[0] // piece // 2
    packed[:half, :] = early[pl.ds(pl.multiple_of((spot[0] % 2) * half, 16), half), :]
    own = (spot[0] % 2) * chips + spot[0] // 2
    packed[half:, :] = late[pl.ds(pl.multiple_of(own * piece, 16), piece), :]


def pack(spot, counts, index, proj, joint, out, up, down, up_bias, vectors, parts):
    rows, low, deep = joint.shape[0], proj.shape[0], down.shape[0]
    size = 3 * rows + low
    late = padded(5 * rows + deep, parts)
    vmem = pl.BlockSpec(memory_space=pltpu.VMEM)
    return pl.pallas_call(
        pack_kernel,
        in_specs=[pl.BlockSpec(memory_space=pltpu.SMEM)] * 2 + [vmem] * 15,
        out_specs=[vmem] * 4,
        out_shape=[
            shape_of((size // 2 + late // parts, D), bf16), shape_of((8, D), f32), shape_of((1, FF), f32),
            shape_of((counts.shape[0], 128), jnp.int32),
        ],
        scratch_shapes=[pltpu.VMEM((size, D), bf16), pltpu.VMEM((late, D), bf16), pltpu.VMEM((128, 128), f32)],
        compiler_params=settings(),
        name="pack",
    )(spot, counts, index, proj, joint, out, up, down, up_bias, *vectors)


def unpack_early(core, mine, other, joint_w, proj):
    groups = mine.shape[0]
    rows, low = D // groups, POSH // groups
    half = (3 * rows + low) // 2

    def place(side, source):
        for group in range(groups):
            at = 0
            while at < half:
                row = side * half + at
                if row < 3 * rows:
                    part, inner = divmod(row, rows)
                    size = min(half - at, rows - inner)
                    first = group * rows + inner
                    joint_w[first : first + size, part * D : part * D + D] = source[group, at : at + size]
                else:
                    size = half - at
                    first = group * low + row - 3 * rows
                    proj[first : first + size, :] = source[group, at : at + size]
                at += size

    @pl.when(core == 0)
    def _():
        place(0, mine)
        place(1, other)

    @pl.when(core == 1)
    def _():
        place(0, other)
        place(1, mine)


def unpack_late(spot, mine, other, near, near_other, lates, out_w, up_w, down_w):
    _, chips, groups, piece, _ = lates.shape
    rows, deep = D // groups, FF // groups
    half = mine.shape[1] - piece
    core, chip = spot % 2, spot // 2
    for side, own, rest in ((core, mine, near), (1 - core, other, near_other)):
        lates[side, chip] = own[:, half:, :]
        for offset, source in enumerate(rest):
            lates[side, chip ^ (offset + 1)] = source[...]
    for at_chip in range(2 * chips):
        for group in range(groups):
            at = 0
            while at < piece:
                row = at_chip * piece + at
                source = lates.at[at_chip // chips, at_chip % chips, group]
                if row < rows:
                    size = min(piece - at, rows - row)
                    first = group * rows + row
                    out_w[first : first + size, :] = source[at : at + size, :]
                elif row < 5 * rows:
                    block, inner = divmod(row - rows, rows)
                    size = min(piece - at, rows - inner)
                    first = group * rows + inner
                    up_w[first : first + size, block * D : block * D + D] = source[at : at + size, :]
                elif row < 5 * rows + deep:
                    inner = row - 5 * rows
                    size = min(piece - at, deep - inner)
                    first = group * deep + inner
                    down_w[first : first + size, :] = source[at : at + size, :]
                else:
                    size = piece - at
                at += size


def picked(rows, first, source):
    ids = lax.broadcasted_iota(jnp.int32, (16, rows), 0) - lax.broadcasted_iota(jnp.int32, (16, rows), 1)
    return dot(jnp.where(ids == first, 1.0, 0.0).astype(bf16), source)


def split16(values):
    high = values.astype(bf16)
    return high, (values - high.astype(f32)).astype(bf16)


def place_inputs(centers, place_weight, place_bias, cen, place_w):
    for tile in range(cen.shape[0]):
        high, rest = split16(centers[:, tile * ROWS : tile * ROWS + ROWS])
        ids = lax.broadcasted_iota(jnp.int32, (16, ROWS), 0)
        ones = jnp.where((ids == 9) | (ids == 10), 1.0, 0.0)
        cen[tile] = (picked(3, 0, high) + picked(3, 3, rest) + picked(3, 6, high) + ones).astype(bf16)
    high, rest = split16(place_weight[...])
    bias_high, bias_rest = split16(place_bias[...])
    value = picked(3, 0, high) + picked(3, 3, high) + picked(3, 6, rest) + picked(1, 9, bias_high) + picked(1, 10, bias_rest)
    place_w[...] = value.astype(bf16)


def front_kernel(core, tokens, centers, targets, vec, place_weight, place_bias, mine, other,
                 entry, joint, mixture, shares, weights, joint_w, proj, cen, place_w, qkv):
    step = pl.program_id(0)

    @pl.when(step == 0)
    def _():
        for sub in range(SUBS):
            qkv[sub, ROWS:, :] = jnp.zeros((qkv.shape[1] - ROWS, 3 * D), bf16)
        unpack_early(core[0], mine, other, joint_w, proj)
        place_inputs(centers, place_weight, place_bias, cen, place_w)

    lanes = lax.broadcasted_iota(jnp.int32, (1, 2 * KEYS), 1) % KEYS
    sums_of = head_ones(1.0)
    none = jnp.zeros((16, 2 * KEYS), bf16)
    scale_row = jnp.where(lax.broadcasted_iota(jnp.int32, (1, 3 * D), 1) < D, 0.125 * LOG2E, 1.0)

    def normal_rows(sub):
        span = slice(sub * ROWS, sub * ROWS + ROWS)
        pre = dot(cen[step * SUBS + sub], place_w[...], TN)
        low = (pre * cdf(pre)).astype(bf16)
        placed = dot(low, proj[...]) + vec[1:2, :]
        hidden = hidden_column(targets[sub * TILE : sub * TILE + TILE, :])
        rows = jnp.where(hidden > 0.5, vec[0:1, :], tokens[span, :].astype(f32)) + placed
        entry[span, :] = rows
        unit, _ = normalised(rows)
        return (unit * vec[2:3, :] + vec[3:4, :]).astype(bf16)

    def project(sub, normed, first):
        cols = slice(first, min(first + 256, 3 * D))
        value = (dot(normed, joint_w[:, cols]) * scale_row[:, cols]).astype(bf16)
        qkv[sub, :ROWS, cols] = value
        joint[sub * ROWS : sub * ROWS + ROWS, cols] = value

    def score(sub, pair, cloud):
        base = cloud * STEP
        query = qkv[sub, base : base + WIN, pair * 128 : pair * 128 + 128]
        key = qkv[sub, base : base + KEYS, D + pair * 128 : D + pair * 128 + 128]
        return dot(query, spread_heads(key.T))

    def exponentials(cloud, scores):
        live = (lanes >= 2 * cloud) & (lanes < 2 * cloud + SEQ - 1)
        scores = jnp.where(live, scores, -1e30)
        parts = []
        for half in (scores[:, :KEYS], scores[:, KEYS:]):
            parts.append(jnp.exp2(half - jnp.max(half, axis=-1, keepdims=True)).astype(bf16))
        return jnp.concatenate(parts, axis=1)

    def mixed(sub, pair, cloud, e):
        base = cloud * STEP
        value = qkv[sub, base : base + KEYS, 2 * D + pair * 128 : 2 * D + pair * 128 + 128]
        return dot(e, jnp.concatenate([stacked_heads(value), sums_of], axis=1))

    tails = {}

    def store(sub, pair, cloud, e, both):
        base = sub * ROWS + cloud * STEP
        cols = slice(pair * 128, pair * 128 + 128)
        share = 1.0 / both[:, 128:]
        mix = both[:, :128] * share
        spot = slice(pair * 256, pair * 256 + 256)
        at = sub * TILE + cloud
        weights[at, :16, spot] = jnp.where(row_range(16, 2 * cloud, 16, 256), e[:16], none)
        weights[at, 16:64, spot] = e[16:64]
        weights[at, 64:80, spot] = jnp.where(row_range(16, 0, 2 * cloud + 2, 256), e[64:80], none)
        head_mix, head_share = mix[:16], share[:16]
        if cloud:
            head = row_range(16, 0, 2 * cloud)
            tail_mix, tail_share = tails[sub, pair]
            head_mix = jnp.where(head, tail_mix, head_mix)
            head_share = jnp.where(head, tail_share, head_share)
        mixture[base : base + 16, cols] = head_mix.astype(bf16)
        shares[base : base + 16, cols] = head_share.astype(bf16)
        mixture[base + 16 : base + 64, cols] = mix[16:64].astype(bf16)
        shares[base + 16 : base + 64, cols] = share[16:64].astype(bf16)
        tails[sub, pair] = (mix[64:], share[64:])
        if cloud == TILE - 1:
            mixture[base + 64 : base + 80, cols] = mix[64:].astype(bf16)
            shares[base + 64 : base + 80, cols] = share[64:].astype(bf16)

    jobs = [(pair, cloud) for pair in range(PAIRS) for cloud in range(TILE)]
    groups = [jobs[at : at + GROUP] for at in range(0, len(jobs), GROUP)]
    normed = [normal_rows(sub) for sub in range(SUBS)]
    chunks = range(0, 3 * D, 256)
    for first in chunks:
        project(0, normed[0], first)
    waiting = None
    for sub in range(SUBS):
        fill = [functools.partial(project, sub + 1, normed[sub + 1], first) for first in chunks] if sub + 1 < SUBS else []
        share_of = -(-len(fill) // len(groups))
        for group in groups:
            exps = [exponentials(cloud, score(sub, pair, cloud)) for pair, cloud in group]
            for task in fill[:share_of]:
                task()
            fill = fill[share_of:]
            if waiting:
                close_group(mixed, store, *waiting)
            waiting = (sub, group, exps)
    close_group(mixed, store, *waiting)


def close_group(mixed, store, sub, group, exps):
    boths = [mixed(sub, pair, cloud, e) for (pair, cloud), e in zip(group, exps)]
    for (pair, cloud), e, both in zip(group, exps, boths):
        store(sub, pair, cloud, e, both)


def whole(shape):
    return pl.BlockSpec(shape, lambda i: (0,) * len(shape))


def rows_of(width, rows=ROWS):
    return pl.BlockSpec((rows, width), lambda i: (i, 0))


def slab(shape):
    return pl.BlockSpec((1, *shape), lambda i: (i,) + (0,) * len(shape))


def shape_of(dims, kind):
    return jax.ShapeDtypeStruct(dims, kind)


def cost(microseconds):
    return pl.CostEstimate(flops=int(microseconds * 9e8), bytes_accessed=int(microseconds * 2e6), transcendentals=0)


def settings(megabytes=60):
    return pltpu.CompilerParams(vmem_limit_bytes=megabytes * 2**20)


def front(core, tokens, centers, targets, vec, place_weight, place_bias, mine, other):
    count = tokens.shape[0]
    steps = count // ROWS
    rows = SUBS * ROWS
    return pl.pallas_call(
        front_kernel,
        grid=(steps // SUBS,),
        in_specs=[
            pl.BlockSpec(memory_space=pltpu.SMEM), rows_of(D, rows), whole(centers.shape),
            pl.BlockSpec((SUBS * TILE, 128), lambda i: (i, 0)), whole((8, D)),
            whole((3, POSH)), whole((1, POSH)), whole(mine.shape), whole(other.shape),
        ],
        out_specs=[
            rows_of(D, rows), rows_of(3 * D, rows), rows_of(D, rows), rows_of(D, rows),
            pl.BlockSpec((SUBS * TILE, WIN, HEADS * KEYS), lambda i: (i, 0, 0)), whole((D, 3 * D)), whole((POSH, D)),
            whole((steps, 16, ROWS)), whole((16, POSH)),
        ],
        out_shape=[
            shape_of((count, D), f32), shape_of((count, 3 * D), bf16),
            shape_of((count, D), bf16), shape_of((count, D), bf16),
            shape_of((steps * TILE, WIN, HEADS * KEYS), bf16), shape_of((D, 3 * D), bf16), shape_of((POSH, D), bf16),
            shape_of((steps, 16, ROWS), bf16), shape_of((16, POSH), bf16),
        ],
        scratch_shapes=[pltpu.VMEM((SUBS, ROWS + 48, 3 * D), bf16)],
        compiler_params=settings(),
        cost_estimate=cost(28),
        name="front",
    )(core, tokens, centers, targets, vec, place_weight, place_bias, mine, other)


def write_sums(sums, order, first, values):
    size = sums.shape[0] // len(order)
    at = 0
    while at < values.shape[0]:
        row = first + at
        segment, inner = divmod(row, size)
        step = min(size - inner, values.shape[0] - at)
        spot = order[segment] * size + inner
        sums[spot : spot + step, :] = values[at : at + step].astype(bf16)
        at += step


def share_halves(core, sums, kept, sent):
    half = sent.shape[0]
    kept[...] = sums[pl.ds(pl.multiple_of(core * half, 16), half), :]
    sent[...] = sums[pl.ds(pl.multiple_of((1 - core) * half, 16), half), :]


def padded(rows, size):
    return -(-rows // (16 * size)) * 16 * size


def middle_kernel(chunk, order, spot, entry, mixture, shares, cot, vec, up_b, mine, other, *refs):
    chips = len(order) // 2
    near, near_other, refs = refs[: chips - 1], refs[chips - 1 : 2 * chips - 2], refs[2 * chips - 2 :]
    (output, mid_grad, mix_grad, kept, sent, up_bg, vec_g,
     down_acc, up_acc, out_acc, out_w, up_w, down_w, gated, sums, lates) = refs
    step = pl.program_id(0)

    @pl.when(step == 0)
    def _():
        unpack_late(spot[0], mine, other, near, near_other, lates, out_w, up_w, down_w)
        for ref in (down_acc, up_acc, out_acc, up_bg, vec_g):
            ref[...] = jnp.zeros(ref.shape, ref.dtype)

    parts = FF // chunk
    spans = [slice(part * chunk, part * chunk + chunk) for part in range(parts)]
    mix = mixture[...]
    cotangent = cot[...]
    mid = entry[...] + (dot(mix, out_w[...]) + vec[4:5, :])
    gates = [dot(cotangent, down_w[spans[0], :], NT)]
    unit, scale = normalised(mid)
    normed = (unit * vec[5:6, :] + vec[6:7, :]).astype(bf16)
    lows = []

    def down_part(part):
        down_acc[:, spans[part]] += dot(cotangent, gated[:, spans[part]], TN)

    def up_part(part):
        up_acc[:, spans[part]] += dot(normed, lows[part], TN)

    for part in range(parts):
        cols = spans[part]
        raised = dot(normed, up_w[:, cols]) + up_b[:, cols]
        if part + 1 < parts:
            gates.append(dot(cotangent, down_w[spans[part + 1], :], NT))
        mass = cdf(raised)
        gated[:, cols] = (raised * mass).astype(bf16)
        grad = gates[part] * smooth_slope(raised, mass)
        up_bg[:, cols] += jnp.sum(grad, axis=0, keepdims=True)
        lows.append(grad.astype(bf16))
        if part:
            down_part(part - 1)
            if part > 1:
                up_part(part - 2)
    back = dot(jnp.concatenate(lows, axis=1), up_w[...], NT)
    up_part(parts - 2)
    down_part(parts - 1)
    up_part(parts - 1)
    output[...] = (mid + (dot(gated[...], down_w[...]) + vec[7:8, :])).astype(bf16)
    upstream = cotangent.astype(f32)
    tilted = back * vec[5:6, :]
    grad = upstream + scale * (tilted - row_mean(tilted) - unit * row_mean(tilted * unit))
    low = grad.astype(bf16)
    mid_grad[...] = low
    mix_grad[...] = (dot(low, out_w[...], NT) * shares[...].astype(f32)).astype(bf16)
    out_acc[...] += dot(mix, low, TN)
    vec_g[0:1, :] += jnp.sum(back * unit, axis=0, keepdims=True)
    vec_g[1:2, :] += jnp.sum(back, axis=0, keepdims=True)
    vec_g[2:3, :] += jnp.sum(grad, axis=0, keepdims=True)
    vec_g[3:4, :] += jnp.sum(upstream, axis=0, keepdims=True)

    @pl.when(step == pl.num_programs(0) - 1)
    def _():
        for part in range(4):
            write_sums(sums, order, part * D, up_acc[:, part * D : part * D + D])
        write_sums(sums, order, 4 * D, down_acc[...].T)
        write_sums(sums, order, 8 * D, out_acc[...])
        if sums.shape[0] > 9 * D:
            write_sums(sums, order, 9 * D, jnp.zeros((sums.shape[0] - 9 * D, D), f32))
        share_halves(spot[0] % 2, sums, kept, sent)


def middle_part(spot, entry, mixture, shares, cot, vec, up_b, mine, other, near, near_other, order, rows=704, chunk=768):
    count = entry.shape[0]
    size = padded(9 * D, len(order))
    return pl.pallas_call(
        functools.partial(middle_kernel, chunk, order),
        grid=(count // rows,),
        in_specs=[
            pl.BlockSpec(memory_space=pltpu.SMEM), rows_of(D, rows), rows_of(D, rows), rows_of(D, rows), rows_of(D, rows),
            whole((8, D)), whole((1, FF)), whole(mine.shape), whole(other.shape),
        ]
        + [whole(piece.shape) for piece in [*near, *near_other]],
        out_specs=[
            rows_of(D, rows), rows_of(D, rows), rows_of(D, rows),
            whole((size // 2, D)), whole((size // 2, D)), whole((1, FF)), whole((8, D)),
        ],
        out_shape=[
            shape_of((count, D), bf16), shape_of((count, D), bf16), shape_of((count, D), bf16),
            shape_of((size // 2, D), bf16), shape_of((size // 2, D), bf16), shape_of((1, FF), f32), shape_of((8, D), f32),
        ],
        scratch_shapes=[
            pltpu.VMEM((D, FF), f32), pltpu.VMEM((D, FF), f32), pltpu.VMEM((D, D), f32),
            pltpu.VMEM((D, D), bf16), pltpu.VMEM((D, FF), bf16), pltpu.VMEM((FF, D), bf16),
            pltpu.VMEM((rows, FF), bf16), pltpu.VMEM((size, D), bf16),
            pltpu.VMEM((2, len(order) // 2, *near[0].shape), bf16),
        ],
        compiler_params=settings(),
        cost_estimate=cost(55),
        name="middle",
    )(spot, entry, mixture, shares, cot, vec, up_b, mine, other, *near, *near_other)


def back_kernel(is_first, is_last, order, *refs):
    entry, joint, mixture, weights, mix_grad, mid_grad, cen, targets, vec, place_w, proj, joint_w = refs[:12]
    refs = refs[12:]
    if not is_first:
        before, refs = refs[1:5], refs[5:]
    if is_last:
        core, up_bg, mid_vec_g, tokens_g, kept, sent, joint_g, proj_g, place_g, vec_g, qkv, dqkv, sums = refs
    else:
        tokens_g, joint_g, proj_g, place_g, vec_g, qkv, dqkv = refs
    step = pl.program_id(0)

    @pl.when(step == 0)
    def _():
        for at, ref in enumerate((joint_g, proj_g, place_g, vec_g)):
            ref[...] = jnp.zeros(ref.shape, ref.dtype) if is_first else before[at][...]
        qkv[ROWS:, :] = jnp.zeros((qkv.shape[0] - ROWS, 3 * D), bf16)

    qkv[:ROWS, :] = joint[...]
    pre = dot(cen[0], place_w[...], TN)
    unit, scale = normalised(entry[...])
    normed = (unit * vec[2:3, :] + vec[3:4, :]).astype(bf16)
    ones = block_ones()
    jobs = [(pair, cloud) for pair in range(PAIRS) for cloud in range(TILE)]
    tails = {}
    for at in range(0, len(jobs), BACK_GROUP):
        group = jobs[at : at + BACK_GROUP]
        gaps = []
        for pair, cloud in group:
            base = cloud * STEP
            window = slice(base, base + WIN)
            cols = slice(pair * 128, pair * 128 + 128)
            value = qkv[base : base + KEYS, 2 * D + pair * 128 : 2 * D + pair * 128 + 128]
            gaps.append(dot(mix_grad[window, cols], spread_heads(value.T)))
        es, products, sums_of = [], [], []
        for (pair, cloud), gap in zip(group, gaps):
            e = weights[cloud, :, pair * 256 : pair * 256 + 256]
            product = e.astype(f32) * gap
            high, rest = split16(product)
            es.append(e)
            products.append(product)
            sums_of.append(dot(jnp.concatenate([high, rest, e], axis=0), ones))
        dss = []
        for e, product, found in zip(es, products, sums_of):
            share = (found[:WIN] + found[WIN : 2 * WIN]) / jnp.maximum(found[2 * WIN :], 1e-30)
            dss.append((product - e.astype(f32) * share).astype(bf16))
        results = []
        for (pair, cloud), e, ds in zip(group, es, dss):
            base = cloud * STEP
            query = stacked_heads(qkv[base : base + WIN, pair * 128 : pair * 128 + 128])
            key = stacked_heads(qkv[base : base + KEYS, D + pair * 128 : D + pair * 128 + 128])
            sdm = stacked_heads(mix_grad[base : base + WIN, pair * 128 : pair * 128 + 128])
            e = jnp.concatenate([e[:, :KEYS], e[:, KEYS:]], axis=0)
            tall = jnp.concatenate([ds[:, :KEYS], ds[:, KEYS:]], axis=0)
            results.append((dot(ds, key), dot(tall[:, :WIN], query, TN), dot(e[:, :WIN], sdm, TN)))
        for (pair, cloud), (dq, dk, dv) in zip(group, results):
            base = cloud * STEP
            parts = (dq * 0.125, dk * (1.0 / LOG2E), dv)
            for which, part in enumerate(parts):
                cols = slice(which * D + pair * 128, which * D + pair * 128 + 128)
                head = part[:16]
                if cloud:
                    head = jnp.where(row_range(16, 0, 2 * cloud), tails[pair, which], head)
                dqkv[base : base + 16, cols] = head.astype(bf16)
                dqkv[base + 16 : base + 64, cols] = part[16:64].astype(bf16)
                tails[pair, which] = part[64:80]
                if cloud == TILE - 1:
                    dqkv[ROWS - 16 :, cols] = part[64:80].astype(bf16)


    back = dot(dqkv[...], joint_w[...], NT)
    joint_g[...] += dot(normed, dqkv[...], TN)
    tilted = back * vec[2:3, :]
    grad = mid_grad[...].astype(f32) + scale * (tilted - row_mean(tilted) - unit * row_mean(tilted * unit))
    low = grad.astype(bf16)
    mass = cdf(pre)
    place_low = (pre * mass).astype(bf16)
    pre_grad = dot(low, proj[...], NT) * smooth_slope(pre, mass)
    proj_g[...] += dot(place_low, low, TN)
    hidden = hidden_column(targets[...])
    marked = jnp.where(hidden > 0.5, grad, 0.0)
    tokens_g[...] = (grad - marked).astype(bf16)
    high_part = pre_grad.astype(bf16)
    low_part = (pre_grad - high_part.astype(f32)).astype(bf16)
    place_g[...] += dot(cen[0], jnp.concatenate([high_part, low_part], axis=1))
    vec_g[0:1, :] += jnp.sum(marked, axis=0, keepdims=True)
    vec_g[1:2, :] += jnp.sum(grad, axis=0, keepdims=True)
    vec_g[2:3, :] += jnp.sum(back * unit, axis=0, keepdims=True)
    vec_g[3:4, :] += jnp.sum(back, axis=0, keepdims=True)
    if not is_last:
        return

    @pl.when(step == pl.num_programs(0) - 1)
    def _():
        for part in range(3):
            write_sums(sums, order, part * D, joint_g[:, part * D : part * D + D])
        write_sums(sums, order, 3 * D, proj_g[...])
        place = place_g[:, :POSH] + place_g[:, POSH:]
        place_weight = place[0:3] + place_g[3:6, :POSH]
        small = jnp.concatenate(
            [
                vec_g[0:4, :],
                mid_vec_g[0:4, :],
                jnp.concatenate([place_weight[0:1], place_weight[1:2], place_weight[2:3]], axis=1),
                jnp.concatenate([place[9:10], jnp.zeros((1, D - POSH), f32)], axis=1),
                jnp.concatenate([up_bg[:, part * D : part * D + D] for part in range(4)], axis=0),
                jnp.zeros((sums.shape[0] - 3 * D - POSH - 14, D), f32),
            ],
            axis=0,
        )
        write_sums(sums, order, 3 * D + POSH, small)
        share_halves(core[0], sums, kept, sent)


def back_part(given, first, steps, order, before=None, extra=None):
    count = given[0].shape[0]

    def shifted(width):
        return pl.BlockSpec((ROWS, width), lambda i: (i + first, 0))

    def shifted_slab(shape):
        return pl.BlockSpec((1, *shape), lambda i: (i + first, 0, 0))

    accs = [(D, 3 * D), (POSH, D), (16, 256), (8, D)]
    in_specs = [
        shifted(D), shifted(3 * D), shifted(D),
        pl.BlockSpec((TILE, WIN, HEADS * KEYS), lambda i: (i + first, 0, 0)),
        shifted(D), shifted(D), shifted_slab((16, ROWS)),
        pl.BlockSpec((TILE, 128), lambda i: (i + first, 0)),
        whole((8, D)), whole((16, POSH)), whole((POSH, D)), whole((D, 3 * D)),
    ]
    given = list(given)
    if before is not None:
        given += before
        in_specs += [pl.BlockSpec(memory_space=pl.ANY)] + [whole(acc) for acc in accs]
    out_specs, out_shape = [shifted(D)], [shape_of((count, D), bf16)]
    scratch = [pltpu.VMEM((ROWS + 48, 3 * D), bf16), pltpu.VMEM((ROWS, 3 * D), bf16)]
    if extra is not None:
        given += extra
        in_specs += [pl.BlockSpec(memory_space=pltpu.SMEM), whole((1, FF)), whole((8, D))]
        size = padded(3 * D + POSH + 16, len(order))
        out_specs += [whole((size // 2, D))] * 2
        out_shape += [shape_of((size // 2, D), bf16)] * 2
        scratch = [pltpu.VMEM(acc, f32) for acc in accs] + scratch + [pltpu.VMEM((size, D), bf16)]
    else:
        out_specs += [whole(acc) for acc in accs]
        out_shape += [shape_of(acc, f32) for acc in accs]
    return pl.pallas_call(
        functools.partial(back_kernel, before is None, extra is not None, order),
        grid=(steps,),
        in_specs=in_specs,
        out_specs=out_specs,
        out_shape=out_shape,
        scratch_shapes=scratch,
        input_output_aliases={} if before is None else {12: 0},
        compiler_params=settings(),
        cost_estimate=cost(5 * steps),
        name="back",
    )(*given)


def gather_pieces(spot, offsets, pieces, sums):
    segment = pieces[0].shape[0] // len(offsets)
    chips = len(offsets)
    for core, piece in enumerate(pieces):
        for at, offset in enumerate(offsets):
            holder = spot ^ offset ^ core
            row = pl.multiple_of(((holder % 2) * chips + holder // 2) * segment, 16)
            sums[pl.ds(row, segment), :] = piece[at * segment : at * segment + segment, :]


def widen_kernel(offsets, spot, *refs):
    pieces, (up_g, down_g, out_g, sums) = refs[:2], refs[2:]
    step = pl.program_id(0)

    @pl.when(step == 0)
    def _():
        gather_pieces(spot[0], offsets, pieces, sums)
        out_g[...] = sums[8 * D : 9 * D, :].astype(f32)

    up_g[...] = sums[pl.ds(pl.multiple_of(step * D, 16), D), :].astype(f32)
    down_g[...] = sums[pl.ds(pl.multiple_of((step + 4) * D, 16), D), :].astype(f32)


def close_kernel(offsets, spot, *refs):
    pieces, (joint_g, proj_g, place_g, *small), last = refs[:2], refs[2:-1], refs[-1]
    step = pl.program_id(0)

    @pl.when(step == 0)
    def _():
        gather_pieces(spot[0], offsets, pieces, last)
        proj_g[...] = last[3 * D : 3 * D + POSH, :].astype(f32)
        rows = last[3 * D + POSH : 3 * D + POSH + 16, :].astype(f32)
        for part in range(3):
            place_g[part : part + 1, :] = rows[8:9, part * POSH : part * POSH + POSH]
        small[0][...] = rows[9:10, :POSH].reshape(POSH)
        small[1][...] = jnp.concatenate([rows[10 + part : 11 + part] for part in range(4)], axis=1).reshape(FF)
        for at in range(8):
            small[2 + at][...] = rows[at : at + 1].reshape(D)

    joint_g[...] = last[pl.ds(pl.multiple_of(step * D, 16), D), :].astype(f32)


def one(shape):
    return pl.BlockSpec(shape, lambda i: (0,) * len(shape))


def unpacked(kernel, name, steps, shapes, specs, spot, offsets, values):
    return pl.pallas_call(
        functools.partial(kernel, offsets),
        grid=(steps,),
        in_specs=[pl.BlockSpec(memory_space=pltpu.SMEM)] + [one(value.shape) for value in values],
        out_specs=specs,
        out_shape=[shape_of(shape, f32) for shape in shapes],
        scratch_shapes=[pltpu.VMEM((values[0].shape[0] * 2, D), bf16)],
        compiler_params=settings(24),
        cost_estimate=cost(4),
        name=name,
    )(spot, *values)


def widen(spot, offsets, values):
    specs = [pl.BlockSpec((D, D), lambda i: (0, i)), pl.BlockSpec((D, D), lambda i: (i, 0)), one((D, D))]
    return unpacked(widen_kernel, "widen", 4, [(D, FF), (FF, D), (D, D)], specs, spot, offsets, values)


def close(spot, offsets, values):
    shapes = [(POSH, D), (3, POSH), (POSH,), (FF,)] + [(D,)] * 8
    specs = [pl.BlockSpec((D, D), lambda i: (0, i))] + [one(shape) for shape in shapes]
    return unpacked(close_kernel, "close", 3, [(D, 3 * D)] + shapes, specs, spot, offsets, values)


def bits_of(size):
    return [1 << bit for bit in range(size.bit_length() - 1)]


def chip_bits(size):
    bits = bits_of(size)[:0:-1]
    return [bits[at : at + 2] for at in range(0, len(bits), 2)]


def offsets_of(bits):
    found = [0]
    for bit in reversed(bits):
        found += [offset + bit for offset in found]
    return found


def swapped(values, offset, size):
    return lax.ppermute(values, "dp", [(i, i ^ offset) for i in range(size)])


def total(terms):
    return sum(term.astype(f32) for term in terms).astype(bf16)


def scattered(terms, bits, size):
    offsets = offsets_of(bits)
    mine = (lax.axis_index("dp") // bits[-1]) % len(offsets)
    parts = [term.reshape(len(offsets), -1, D) for term in terms]

    def part(offset):
        return [lax.dynamic_index_in_dim(term, mine ^ (offset // bits[-1]), 0, keepdims=False) for term in parts]

    return part(0) + [swapped(total(part(offset)), offset, size) for offset in offsets[1:]]


def joined(pieces, bits, size):
    found = dict(pieces)
    for offset in offsets_of(bits)[1:]:
        for held, piece in pieces.items():
            found[held ^ offset] = swapped(piece, offset, size)
    return found


def crossed(values, offset, size):
    return lax.ppermute(values, "fsdp", [(i, i ^ offset) for i in range(size)])


def tied(first, second):
    return lax.optimization_barrier((first, second))


def after(value, other):
    return lax.optimization_barrier((value, other))[0]


def per_device(
    sizes,
    tokens,
    centers,
    mask_count,
    mask_index,
    mask_embed,
    place_weight,
    place_bias,
    place_proj,
    place_shift,
    norm_gain,
    norm_shift,
    joint_weight,
    out_weight,
    out_bias,
    mlp_gain,
    mlp_shift,
    up_weight,
    up_bias,
    down_weight,
    down_bias,
    cotangent,
):
    dp, fsdp = sizes["dp"], sizes["fsdp"]
    spot = lax.axis_index("dp").astype(jnp.int32)[None]
    core = spot % 2
    vectors = (mask_embed, place_shift, norm_gain, norm_shift, out_bias, mlp_gain, mlp_shift, down_bias)
    packed, vec, up_b, targets = pack(
        spot, mask_count, mask_index.T, place_proj, joint_weight, out_weight, up_weight, down_weight, up_bias, vectors, dp
    )
    packed = lax.all_gather(packed, "fsdp", axis=0)
    packed_other = swapped(packed, 1, dp)
    half = (3 * joint_weight.shape[0] + place_proj.shape[0]) // 2
    late = packed[:, half:]
    pieces = [swapped(late, 2 * offset, dp) for offset in range(1, dp // 2)]
    entry, joint, mixture, shares, weights, joint_w, proj, cen, place_w = front(
        core, tokens, centers, targets, vec, place_weight, place_bias[None, :], packed, packed_other
    )
    pieces, mixture = tied(pieces, mixture)
    pieces_other = [swapped(piece, 1, dp) for piece in pieces]
    order = list(range(dp))
    output, mid_grad, mix_grad, kept, sent, up_bg, vec_g = middle_part(
        spot, entry, mixture, shares, cotangent, vec, up_b, packed, packed_other, pieces, pieces_other, order
    )
    chips = chip_bits(dp)
    near, far = [offset % fsdp for offset in (1, 2)]
    sums = [kept, swapped(sent, 1, dp)]
    mix_grad, sums[-1] = tied(mix_grad, sums[-1])
    sums = scattered(sums, chips[0], dp)
    given = [entry, joint, mixture, weights, mix_grad, mid_grad, cen, targets, vec, place_w, proj, joint_w]
    steps = tokens.shape[0] // ROWS
    early_steps = steps // 2
    before = list(back_part(given, 0, early_steps, order))
    for bits in chips[1:]:
        sums = scattered(sums, bits, dp)
    sums[-1], before[0] = tied(sums[-1], before[0])
    middle_row = sums[0].shape[0] // 2
    upper = total([term[:middle_row] for term in sums])
    lower = total([term[middle_row:] for term in sums])
    upper_got, lower_got = crossed(upper, near, fsdp), crossed(lower, far, fsdp)
    given[4] = after(given[4], lower)
    tokens_grad, kept, sent = back_part(given, early_steps, steps - early_steps, order, before, [core, up_bg, vec_g])
    sent, upper_got, lower_got = lax.optimization_barrier((sent, upper_got, lower_got))
    upper, lower = total([upper, upper_got]), total([lower, lower_got])
    upper_got, lower_got = crossed(upper, far, fsdp), crossed(lower, near, fsdp)
    last = [kept, swapped(sent, 1, dp)]
    last = scattered(last, chips[0], dp)
    upper_got = after(upper_got, last[-1])
    sums = {0: jnp.concatenate([total([upper, upper_got]), total([lower, lower_got])], axis=0)}
    for bits in chips[1:]:
        last = scattered(last, bits, dp)
    value = total(last)
    near_got = after(crossed(value, near, fsdp), sums[0])
    for bits in reversed(chips):
        sums = joined(sums, bits, dp)
    value = total([value, near_got])
    far_got = crossed(value, far, fsdp)
    soonest = list(sums)[1]
    far_got, sums[soonest] = tied(far_got, sums[soonest])
    last = {0: total([value, far_got])}
    for bits in reversed(chips):
        last = joined(last, bits, dp)
    held = jnp.concatenate(list(sums.values()), axis=0)
    up_grad, down_grad, out_grad = widen(spot, list(sums), [held, swapped(held, 1, dp)])
    newest = list(last)[-1]
    last[newest] = after(last[newest], out_grad)
    held = jnp.concatenate(list(last.values()), axis=0)
    joint_grad, proj_grad, place_weight_grad, place_bias_grad, up_bias_grad, *small = close(
        spot, list(last), [held, swapped(held, 1, dp)]
    )
    return (
        output,
        tokens_grad,
        small[0],
        place_weight_grad,
        place_bias_grad,
        proj_grad,
        small[1],
        small[2],
        small[3],
        joint_grad,
        out_grad,
        small[6],
        small[4],
        small[5],
        up_grad,
        up_bias_grad,
        down_grad,
        small[7],
    )


def solution(mesh):
    rows = P(("dp", "fsdp"), None)
    in_specs = (
        rows,
        P(None, ("dp", "fsdp")),
        P(("dp", "fsdp")),
        rows,
        P(),
        P(),
        P(),
        P("fsdp", None),
        P(),
        P(),
        P(),
        P("fsdp", None),
        P("fsdp", None),
        P(),
        P(),
        P(),
        P("fsdp", None),
        P(),
        P("fsdp", None),
        P(),
        rows,
    )
    out_specs = (rows, rows) + (P(),) * 16
    return jax.shard_map(
        functools.partial(per_device, dict(mesh.shape)), mesh=mesh, in_specs=in_specs, out_specs=out_specs, check_vma=False
    )
```
